32 devices in a mesh: seq: 8 (over z, x), slide: 4 (over y, core).
Axes of the slice: x: 2, y: 2, z: 4, core: 2. Of those that a mesh axis runs over, the one named last changes fastest.
Arguments:
- tokens: bfloat16 [4, 4096, 768], P('slide', 'seq'), may hold values from -6 to 6
- qkv_weight: bfloat16 [768, 2304], replicated, may hold values from -0.21875 to 0.21875
- out_weight: bfloat16 [768, 768], replicated, may hold values from -3 to 3
- up_weight: bfloat16 [768, 3072], replicated, may hold values from -0.21875 to 0.21875
- down_weight: bfloat16 [3072, 768], replicated, may hold values from -0.109375 to 0.109375
- norm1_gain: float32 [768], replicated, may hold values from 0.5 to 1.5
- norm1_bias: float32 [768], replicated, may hold values from -2 to 2
- norm2_gain: float32 [768], replicated, may hold values from 0.5 to 1.5
- norm2_bias: float32 [768], replicated, may hold values from -2 to 2
- visible: int32 [4], P('slide'), may hold values from 2048 to 4096, as said below
- cotangent: bfloat16 [4, 4096, 768], P('slide', 'seq'), may hold values from -6 to 6
Outputs:
- mixed: bfloat16 [4, 4096, 768], P('slide', 'seq')
- tokens_grad: bfloat16 [4, 4096, 768], P('slide', 'seq')
- qkv_grad: float32 [768, 2304], P('seq')
- out_grad: float32 [768, 768], P('seq')
- up_grad: float32 [768, 3072], P('seq')
- down_grad: float32 [3072, 768], P('seq')
- norm1_gain_grad: float32 [768], replicated
- norm1_bias_grad: float32 [768], replicated
- norm2_gain_grad: float32 [768], replicated
- norm2_bias_grad: float32 [768], replicated
The draws below stay inside these ranges and needn't reach their ends.
Inputs may be any that keep to these rules, and one draw needn't show every extreme that they name: Entry b counts the leading rows of slide b that hold visible tiles; every row after them is padding. Some slide is full (4096 rows) and another holds exactly 2048.
All inputs are finite; a program needn't handle non-finite values.
Results may differ from the reference program's by a relative error of at most 0.013.
Values may be sent and summed in bfloat16 or wider, within the bound.
A program may use at most 256 MiB of HBM per device.

```python
import jax
import jax.numpy as jnp
from jax import lax

D = 768
HEADS = 16
HEAD_WIDTH = 48
FF = 3072
SEG = 512
QB = 512
DILATION_STEP = 16
SLIDES = 4
SEQ_LEN = 4096


def draw_visible(key, part):
    key = jax.random.fold_in(key, 7)
    order_key, count_key = jax.random.split(key)
    slide_order = jax.random.permutation(order_key, SLIDES)
    counts = jax.random.randint(count_key, (SLIDES,), SEQ_LEN // 2, SEQ_LEN + 1)
    counts = jnp.where(slide_order == 0, SEQ_LEN, counts)
    counts = jnp.where(slide_order == 1, SEQ_LEN // 2, counts)
    return counts.astype(jnp.int32)


def levels(own_key, shape, shards, low, largest):
    loudness = 1.0
    for axis_at, parts in shards:
        draws = jax.random.uniform(jax.random.fold_in(jax.random.fold_in(own_key, 6), axis_at), (parts,), jnp.float32, low / len(shards), largest / len(shards))
        loudness = loudness * jnp.repeat(jnp.exp(draws), shape[axis_at] // parts).reshape((-1,) + (1,) * (len(shape) - 1 - axis_at))
    return loudness


def normal_values(key, shape, scale, limit, cuts=(), held_as=jnp.bfloat16):
    entries = scale * jax.random.normal(key, shape, jnp.float32)
    if cuts:
        entries = entries * levels(key, shape, cuts, -0.22, 0.18)
    return jnp.clip(entries, -limit, limit).astype(held_as)


def setup_inputs(seed: int = 0) -> dict:
    arg_keys = jax.random.split(jax.random.key(seed), 12)
    return {
        "tokens": normal_values(arg_keys[0], (SLIDES, SEQ_LEN, D), 1.0, 6.0, ((0, 4), (1, 8))),
        "qkv_weight": normal_values(arg_keys[1], (D, 3 * D), D ** -0.5, 0.21875),
        "out_weight": normal_values(arg_keys[2], (D, D), (D // 256 + 1) ** -0.5, 3.0),
        "up_weight": normal_values(arg_keys[3], (D, FF), D ** -0.5, 0.21875),
        "down_weight": normal_values(arg_keys[4], (FF, D), FF ** -0.5, 0.109375),
        "norm1_gain": jnp.clip(1.0 + 0.1 * jax.random.normal(arg_keys[5], (D,), jnp.float32), 0.5, 1.5),
        "norm1_bias": normal_values(arg_keys[6], (D,), 0.3, 2.0, (), jnp.float32),
        "norm2_gain": jnp.clip(1.0 + 0.1 * jax.random.normal(arg_keys[7], (D,), jnp.float32), 0.5, 1.5),
        "norm2_bias": normal_values(arg_keys[8], (D,), 0.3, 2.0, (), jnp.float32),
        "visible": draw_visible(jax.random.fold_in(arg_keys[11], 71), 0),
        "cotangent": normal_values(arg_keys[10], (SLIDES, SEQ_LEN, D), 1.0, 6.0, ((0, 4), (1, 8))),
    }


epsilon = 1e-05

@jax.custom_vjp
def low(v):
    return lax.optimization_barrier(v.astype(jnp.bfloat16)).astype(jnp.float32)

@jax.custom_vjp
def low_back(v):
    return v

def low_keep(v):
    return (low(v), None)

def low_pass(kept, grad):
    return (grad,)

def back_keep(v):
    return (v, None)

def back_low(kept, grad):
    return (low(grad),)
low.defvjp(low_keep, low_pass)
low_back.defvjp(back_keep, back_low)

def product(left, right):
    return jnp.dot(left, right, precision=lax.Precision.HIGHEST)

def layer_norm(values, norm_gain, norm_shift):
    average = lax.optimization_barrier(jnp.mean(values, axis=-1, keepdims=True))
    centered = values - average
    variance = lax.optimization_barrier(jnp.mean(centered * centered, axis=-1, keepdims=True))
    return centered * lax.rsqrt(variance + epsilon) * norm_gain + norm_shift

def exact_gelu(values):
    return jax.nn.gelu(values, approximate=False)

def attend_block(query_block, seg_keys, seg_values, seg_valid, distant_keys, distant_values, distant_valid):
    highest = lax.Precision.HIGHEST
    nearby_scores = low_back(jnp.einsum('iyo,uyo->yiu', query_block, seg_keys, precision=highest))
    nearby_scores = jnp.where(seg_valid[None, None, :], nearby_scores, -1000000000.0)
    sampled_rows = query_block[::DILATION_STEP]
    far_scores = low_back(jnp.einsum('iyo,uyo->yiu', sampled_rows, distant_keys, precision=highest))
    far_scores = jnp.where(distant_valid[None, None, :], far_scores, -1000000000.0)
    head_number = nearby_scores.shape[0]
    row_number = nearby_scores.shape[1]
    chosen_count = row_number // DILATION_STEP
    maximum_table = lax.optimization_barrier(jnp.max(nearby_scores, axis=-1)).reshape(head_number, chosen_count, DILATION_STEP)
    combined_top = jnp.maximum(maximum_table[:, :, 0], lax.optimization_barrier(jnp.max(far_scores, axis=-1)))
    row_maximum = maximum_table.at[:, :, 0].set(combined_top).reshape(head_number, row_number)
    nearby_exponent = jnp.exp(nearby_scores - row_maximum[:, :, None])
    far_exp = jnp.exp(far_scores - combined_top[:, :, None])
    exponent_sums = lax.optimization_barrier(jnp.sum(nearby_exponent, axis=-1)).reshape(head_number, chosen_count, DILATION_STEP)
    combined_total = exponent_sums[:, :, 0] + lax.optimization_barrier(jnp.sum(far_exp, axis=-1))
    row_sum_total = exponent_sums.at[:, :, 0].set(combined_total).reshape(head_number, row_number)
    local_weights = low(nearby_exponent / row_sum_total[:, :, None])
    far_weights = low(far_exp / combined_total[:, :, None])
    attended_rows = jnp.einsum('hqk,khd->qhd', local_weights, seg_values, precision=highest)
    distant_attended = jnp.einsum('hqk,khd->qhd', far_weights, distant_values, precision=highest)
    attended_rows = attended_rows.reshape(chosen_count, DILATION_STEP, head_number, HEAD_WIDTH).at[:, 0].add(distant_attended)
    return attended_rows.reshape(row_number, head_number * HEAD_WIDTH)

def slide_forward(params, tokens_row, row_limit):
    qkv_weight, out_weight, up_weight, down_weight, gain_one, shift_one, gain_two, shift_two = params
    positions = jnp.arange(SEQ_LEN, dtype=jnp.int32)
    row_validity = positions < row_limit
    normed = low(layer_norm(tokens_row, gain_one, shift_one))
    projected = product(normed, qkv_weight)
    query_rows = low(low_back(projected[:, :D]) * HEAD_WIDTH ** (-0.5)).reshape(SEQ_LEN, HEADS, HEAD_WIDTH)
    key_matrix = low(low_back(projected[:, D:2 * D])).reshape(SEQ_LEN, HEADS, HEAD_WIDTH)
    value_matrix = low(low_back(projected[:, 2 * D:])).reshape(SEQ_LEN, HEADS, HEAD_WIDTH)
    distant_keys = key_matrix[::DILATION_STEP]
    distant_values = value_matrix[::DILATION_STEP]
    distant_valid = row_validity[::DILATION_STEP]
    per_segment = SEG // QB
    query_blocks = query_rows.reshape(SEQ_LEN // QB, QB, HEADS, HEAD_WIDTH)
    key_blocks = jnp.repeat(key_matrix.reshape(SEQ_LEN // SEG, SEG, HEADS, HEAD_WIDTH), per_segment, axis=0)
    value_blocks = jnp.repeat(value_matrix.reshape(SEQ_LEN // SEG, SEG, HEADS, HEAD_WIDTH), per_segment, axis=0)
    valid_blocks = jnp.repeat(row_validity.reshape(SEQ_LEN // SEG, SEG), per_segment, axis=0)
    block_fn = jax.checkpoint(attend_block)

    def one_block(packed):
        return block_fn(packed[0], packed[1], packed[2], packed[3], distant_keys, distant_values, distant_valid)
    attended_rows = lax.map(one_block, (query_blocks, key_blocks, value_blocks, valid_blocks)).reshape(SEQ_LEN, D)
    attn_low = low(low_back(attended_rows))
    after_attn = tokens_row + low_back(product(attn_low, out_weight))
    normed_two = low(layer_norm(after_attn, gain_two, shift_two))
    hidden = low(exact_gelu(low_back(product(normed_two, up_weight))))
    result = after_attn + low_back(product(hidden, down_weight))
    return jnp.where(row_validity[:, None], result, 0.0)

def reference(tokens, qkv_weight, out_weight, up_weight, down_weight, norm1_gain, norm1_bias, norm2_gain, norm2_bias, visible, cotangent):
    params = tuple((w.astype(jnp.float32) for w in (qkv_weight, out_weight, up_weight, down_weight, norm1_gain, norm1_bias, norm2_gain, norm2_bias)))
    inputs = tokens.astype(jnp.float32)
    slide_fn = jax.checkpoint(slide_forward)

    def forward(weights, rows_in):

        def per_slide(slide_carry, packed):
            return (slide_carry, slide_fn(weights, packed[0], packed[1]))
        _, stacked = lax.scan(per_slide, jnp.zeros((), jnp.float32), (rows_in, visible))
        return stacked
    mixed_out, pullback = jax.vjp(forward, params, inputs)
    weight_grads, input_grads = pullback(cotangent.astype(jnp.float32))
    return (mixed_out.astype(jnp.bfloat16), input_grads.astype(jnp.bfloat16), weight_grads[0], weight_grads[1], weight_grads[2], weight_grads[3], weight_grads[4], weight_grads[5], weight_grads[6], weight_grads[7])
```

```python
import functools

import jax
import jax.numpy as jnp
from jax import lax
from jax.experimental import pallas as pl
from jax.experimental.pallas import tpu as pltpu
from jax.sharding import PartitionSpec as P

HEADS = 16
HEAD_WIDTH = 48
SEG = 512
QB = 512
DILATION_STEP = 16


epsilon = 1e-05


def layer_norm(values, norm_gain, norm_shift):
    average = jnp.mean(values, axis=-1, keepdims=True)
    centered = values - average
    variance = jnp.mean(centered * centered, axis=-1, keepdims=True)
    return centered * lax.rsqrt(variance + epsilon) * norm_gain + norm_shift


def exact_gelu(values):
    return jax.nn.gelu(values, approximate=False)


def block_scores(query_block, seg_keys, seg_valid, distant_keys, distant_valid):
    nearby_scores = jnp.einsum(
        "iyo,uyo->yiu", query_block, seg_keys, preferred_element_type=jnp.float32
    )
    nearby_scores = jnp.where(seg_valid[None, None, :], nearby_scores, -1000000000.0)
    far_scores = jnp.einsum(
        "iyo,uyo->yiu",
        query_block[::DILATION_STEP],
        distant_keys,
        preferred_element_type=jnp.float32,
    )
    far_scores = jnp.where(distant_valid[None, None, :], far_scores, -1000000000.0)
    return (nearby_scores, far_scores)


def block_forward(
    query_block, seg_keys, seg_values, seg_valid, distant_keys, distant_values, distant_valid
):
    nearby_scores, far_scores = block_scores(
        query_block, seg_keys, seg_valid, distant_keys, distant_valid
    )
    head_number = nearby_scores.shape[0]
    row_number = nearby_scores.shape[1]
    chosen_count = row_number // DILATION_STEP
    maximum_table = jnp.max(nearby_scores, axis=-1).reshape(
        head_number, chosen_count, DILATION_STEP
    )
    combined_top = jnp.maximum(maximum_table[:, :, 0], jnp.max(far_scores, axis=-1))
    row_maximum = maximum_table.at[:, :, 0].set(combined_top).reshape(head_number, row_number)
    nearby_exponent = jnp.exp(nearby_scores - row_maximum[:, :, None])
    far_exp = jnp.exp(far_scores - combined_top[:, :, None])
    exponent_sums = jnp.sum(nearby_exponent, axis=-1).reshape(
        head_number, chosen_count, DILATION_STEP
    )
    combined_total = exponent_sums[:, :, 0] + jnp.sum(far_exp, axis=-1)
    row_sum_total = exponent_sums.at[:, :, 0].set(combined_total).reshape(head_number, row_number)
    local_weights = (nearby_exponent / row_sum_total[:, :, None]).astype(jnp.bfloat16)
    far_weights = (far_exp / combined_total[:, :, None]).astype(jnp.bfloat16)
    attended_rows = jnp.einsum(
        "hqk,khd->qhd", local_weights, seg_values, preferred_element_type=jnp.float32
    )
    distant_attended = jnp.einsum(
        "hqk,khd->qhd", far_weights, distant_values, preferred_element_type=jnp.float32
    )
    attended_rows = (
        attended_rows.reshape(chosen_count, DILATION_STEP, head_number, HEAD_WIDTH)
        .at[:, 0]
        .add(distant_attended)
    )
    return (attended_rows.reshape(row_number, head_number, HEAD_WIDTH), row_maximum, row_sum_total)


def block_backward(
    query_block,
    seg_keys,
    seg_values,
    seg_valid,
    distant_keys,
    distant_values,
    distant_valid,
    gradient_block,
    row_maximum,
    row_sum_total,
):
    nearby_scores, far_scores = block_scores(
        query_block, seg_keys, seg_valid, distant_keys, distant_valid
    )
    head_number = row_maximum.shape[0]
    row_number = row_maximum.shape[1]
    chosen_count = row_number // DILATION_STEP
    combined_top = row_maximum.reshape(head_number, chosen_count, DILATION_STEP)[:, :, 0]
    combined_total = row_sum_total.reshape(head_number, chosen_count, DILATION_STEP)[:, :, 0]
    nearby_probability = (
        jnp.exp(nearby_scores - row_maximum[:, :, None]) / row_sum_total[:, :, None]
    )
    far_prob = jnp.exp(far_scores - combined_top[:, :, None]) / combined_total[:, :, None]
    local_weights = nearby_probability.astype(jnp.bfloat16)
    gradient_sampled = gradient_block[::DILATION_STEP]
    value_grad = jnp.einsum(
        "mns,nmg->smg", local_weights, gradient_block, preferred_element_type=jnp.float32
    )
    nearby_dots = jnp.einsum(
        "iyo,uyo->yiu", gradient_block, seg_values, preferred_element_type=jnp.float32
    )
    far_dots = jnp.einsum(
        "iyo,uyo->yiu", gradient_sampled, distant_values, preferred_element_type=jnp.float32
    )
    delta_table = jnp.sum(nearby_probability * nearby_dots, axis=-1).reshape(
        head_number, chosen_count, DILATION_STEP
    )
    joint_delta = delta_table[:, :, 0] + jnp.sum(far_prob * far_dots, axis=-1)
    row_delta = delta_table.at[:, :, 0].set(joint_delta).reshape(head_number, row_number)
    local_slope = (nearby_probability * (nearby_dots - row_delta[:, :, None])).astype(jnp.bfloat16)
    distant_slope = (far_prob * (far_dots - joint_delta[:, :, None])).astype(jnp.bfloat16)
    query_gradient = jnp.einsum(
        "hqk,khd->qhd", local_slope, seg_keys, preferred_element_type=jnp.float32
    )
    distant_query = jnp.einsum(
        "hqk,khd->qhd", distant_slope, distant_keys, preferred_element_type=jnp.float32
    )
    query_gradient = (
        query_gradient.reshape(chosen_count, DILATION_STEP, head_number, HEAD_WIDTH)
        .at[:, 0]
        .add(distant_query)
    )
    key_grad = jnp.einsum(
        "mns,nmg->smg", local_slope, query_block, preferred_element_type=jnp.float32
    )
    far_weights = far_prob.astype(jnp.bfloat16)
    far_value_grad = jnp.einsum(
        "mns,nmg->smg", far_weights, gradient_sampled, preferred_element_type=jnp.float32
    )
    far_key_grad = jnp.einsum(
        "mns,nmg->smg",
        distant_slope,
        query_block[::DILATION_STEP],
        preferred_element_type=jnp.float32,
    )
    return (
        query_gradient.reshape(row_number, head_number, HEAD_WIDTH),
        key_grad,
        value_grad,
        far_key_grad,
        far_value_grad,
    )


MESH = pl.DeviceIdType.MESH
SPLIT = 32
PIECES = 3


def remote(src, dst, send_sem, recv_sem, device):
    return pltpu.make_async_remote_copy(
        src_ref=src,
        dst_ref=dst,
        send_sem=send_sem,
        recv_sem=recv_sem,
        device_id=device,
        device_id_type=MESH,
    )


class Place:
    orders = (("y", "x", "a", "b"), ("x", "a", "b", "y"))

    def __init__(self):
        seq, slide = lax.axis_index("seq"), lax.axis_index("slide")
        self.b, self.a, self.x = seq // 4, (seq // 2) % 2, seq % 2
        self.y, self.c = slide // 2, slide % 2
        self.seq, self.slide = seq, slide
        self.partner = {
            "c": (seq, slide + 1 - 2 * self.c),
            "y": (seq, slide + 2 - 4 * self.y),
            "x": (seq + 1 - 2 * self.x, slide),
            "a": (seq + 2 - 4 * self.a, slide),
            "b": (seq + 4 - 8 * self.b, slide),
        }

    def blocks(self, core, phase, flip):
        order = self.orders[core]
        mine = {"b": self.b, "a": self.a, "x": self.x, "y": self.y}
        choices = []
        for name in ("b", "a", "x", "y"):
            at = order.index(name) + 1
            if at < phase:
                choices.append([mine[name]])
            elif at == phase:
                choices.append([1 - mine[name] if flip else mine[name]])
            else:
                choices.append([0, 1])
        return [
            ((b * 2 + a) * 2 + x) * 4 + core * 2 + y
            for b in choices[0]
            for a in choices[1]
            for x in choices[2]
            for y in choices[3]
        ]


class Reducer:
    def __init__(self, place, held, core_got, got, final, send_sem, recv_sem):
        self.place, self.held, self.core_got, self.got, self.final = place, held, core_got, got, final
        self.send_sem, self.recv_sem = send_sem, recv_sem
        self.slot = {1: (0, 8), 2: (8, 4), 3: (12, 2), 4: (14, 1)}

    def landing(self, phase):
        if phase == 0:
            return self.core_got
        if phase == 5:
            return self.final.at[pl.ds(0, 1)]
        if phase == 6:
            return self.final.at[pl.ds(0, 2)]
        first, count = self.slot[phase]
        return self.got.at[pl.ds(first, count)]

    def start(self, phase):
        place = self.place
        send, recv = self.send_sem.at[phase], self.recv_sem.at[phase]
        if phase == 0:
            for owner in range(8):
                away = owner * 4 + (1 - place.c) * 2
                remote(
                    self.held.at[pl.ds(away, 2)],
                    self.core_got.at[pl.ds(owner * 2, 2)],
                    send,
                    recv,
                    place.partner["c"],
                ).start()
        elif phase <= 4:
            first, _ = self.slot[phase]
            for core in range(2):

                @pl.when(place.c == core)
                def _(core=core):
                    partner = place.partner[place.orders[core][phase - 1]]
                    for n, block in enumerate(place.blocks(core, phase, True)):
                        remote(
                            self.held.at[block], self.got.at[first + n], send, recv, partner
                        ).start()
        elif phase == 5:
            own = self.final.at[pl.ds(place.c * 2 + place.y, 1)]
            remote(own, own, send, recv, place.partner["y"]).start()
        else:
            own = self.final.at[pl.ds(place.c * 2, 2)]
            remote(own, own, send, recv, place.partner["c"]).start()

    def finish(self, phase):
        place = self.place
        whole = self.landing(phase)
        wait = remote(whole, whole, self.send_sem.at[phase], self.recv_sem.at[phase], place.partner["c"])
        wait.wait_recv()
        wait.wait_send()
        if phase == 0:

            @pl.loop(0, 8)
            def _(owner):
                for y in range(2):
                    keep = owner * 4 + place.c * 2 + y
                    self.add(keep, self.core_got, owner * 2 + y)
        elif phase <= 4:
            first, _ = self.slot[phase]
            for core in range(2):

                @pl.when(place.c == core)
                def _(core=core):
                    for n, block in enumerate(place.blocks(core, phase, False)):
                        self.add(block, self.got, first + n)
            if phase == 4:
                block = place.seq * 4 + place.c * 2 + place.y
                self.final[place.c * 2 + place.y] = self.held[block]

    def add(self, block, source, at):
        total = self.held[block].astype(jnp.float32) + source[at].astype(jnp.float32)
        self.held[block] = total.astype(jnp.bfloat16)


class NormSum:
    def __init__(self, place, total, got, send_sem, recv_sem):
        self.place, self.total, self.got = place, total, got
        self.send_sem, self.recv_sem = send_sem, recv_sem

    def start(self, step):
        place = self.place
        send, recv = self.send_sem.at[step], self.recv_sem.at[step]
        for core in range(2):

            @pl.when(place.c == core)
            def _(core=core):
                partner = place.partner[(("c",) + place.orders[core])[step]]
                remote(self.total.at[step], self.got.at[step], send, recv, partner).start()

    def finish(self, step):
        wait = remote(
            self.got.at[step],
            self.got.at[step],
            self.send_sem.at[step],
            self.recv_sem.at[step],
            self.place.partner["c"],
        )
        wait.wait_recv()
        wait.wait_send()
        self.total[step + 1] = self.total[step] + self.got[step]


def meet(place, names):
    barrier = pltpu.get_barrier_semaphore()
    for name in names:
        pl.semaphore_signal(barrier, inc=1, device_id=place.partner[name], device_id_type=MESH)
    pl.semaphore_wait(barrier, len(names))


def reduce_kernel(
    parts_ref, norm_ref, out_ref, norm_out_ref, held, core_got, got, final, totals, norm_got,
    load_sem, send_sem, recv_sem, norm_send, norm_recv,
):
    place = Place()
    loads = [
        pltpu.make_async_copy(parts_ref.at[p], held.at[p], load_sem.at[p]) for p in range(PIECES)
    ]
    for load in loads:
        load.start()
    totals[0] = norm_ref[...]
    meet(place, ("c", "y", "x", "a", "b"))
    pieces = [
        Reducer(
            place, held.at[p], core_got.at[p], got.at[p], final.at[p], send_sem.at[p], recv_sem.at[p]
        )
        for p in range(PIECES)
    ]
    norm = NormSum(place, totals, norm_got, norm_send, norm_recv)
    last = 6
    for turn in range(last + PIECES + 1):
        for p, piece in enumerate(pieces):
            phase = turn - p
            if phase == 0:
                loads[p].wait()
            if 1 <= phase <= last + 1:
                piece.finish(phase - 1)
            if 0 <= phase <= last:
                piece.start(phase)
            if phase == last + 1:
                out_ref[p] = final[p].astype(jnp.float32)
        if turn >= 1 and turn <= 5:
            norm.finish(turn - 1)
        if turn < 5:
            norm.start(turn)
    norm_out_ref[...] = totals[5]


def reduce_weights(parts, norm_parts):
    pieces, blocks, rows, width = parts.shape
    return pl.pallas_call(
        reduce_kernel,
        out_shape=(
            jax.ShapeDtypeStruct((pieces, 4, rows, width), jnp.float32),
            jax.ShapeDtypeStruct(norm_parts.shape, jnp.float32),
        ),
        in_specs=[
            pl.BlockSpec(memory_space=pl.ANY),
            pl.BlockSpec(memory_space=pltpu.VMEM),
        ],
        out_specs=(
            pl.BlockSpec(memory_space=pltpu.VMEM),
            pl.BlockSpec(memory_space=pltpu.VMEM),
        ),
        scratch_shapes=[
            pltpu.VMEM((pieces, blocks, rows, width), jnp.bfloat16),
            pltpu.VMEM((pieces, 16, rows, width), jnp.bfloat16),
            pltpu.VMEM((pieces, 15, rows, width), jnp.bfloat16),
            pltpu.VMEM((pieces, 4, rows, width), jnp.bfloat16),
            pltpu.VMEM((6,) + norm_parts.shape, jnp.float32),
            pltpu.VMEM((5,) + norm_parts.shape, jnp.float32),
            pltpu.SemaphoreType.DMA((pieces,)),
            pltpu.SemaphoreType.DMA((pieces, 7)),
            pltpu.SemaphoreType.DMA((pieces, 7)),
            pltpu.SemaphoreType.DMA((5,)),
            pltpu.SemaphoreType.DMA((5,)),
        ],
        compiler_params=pltpu.CompilerParams(
            collective_id=0, has_side_effects=True, vmem_limit_bytes=56 << 20
        ),
        name="reduce_weights",
    )(parts, norm_parts)


def meet_row(seq, slide, count):
    barrier = pltpu.get_barrier_semaphore()
    for step in range(1, count):
        other = (lax.rem(seq + step, count), slide)
        pl.semaphore_signal(barrier, inc=1, device_id=other, device_id_type=MESH)
    pl.semaphore_wait(barrier, count - 1)


def gather_kernel(count, own_ref, all_ref, gathered, send_sem, recv_sem):
    seq, slide = lax.axis_index("seq"), lax.axis_index("slide")
    meet_row(seq, slide, count)
    for step in range(1, count):
        other = lax.rem(seq + step, count)
        remote(
            own_ref, gathered.at[seq], send_sem.at[step], recv_sem.at[step], (other, slide)
        ).start()
    gathered[seq] = own_ref[...]
    for step in range(1, count):
        source = lax.rem(seq + count - step, count)
        wait = remote(
            own_ref, gathered.at[source], send_sem.at[step], recv_sem.at[step], (source, slide)
        )
        wait.wait_recv()
        wait.wait_send()
    all_ref[...] = gathered[...]


def gather_rows(rows, count):
    shape = (count,) + rows.shape
    return pl.pallas_call(
        functools.partial(gather_kernel, count),
        out_shape=jax.ShapeDtypeStruct(shape, rows.dtype),
        in_specs=[pl.BlockSpec(memory_space=pltpu.VMEM)],
        out_specs=pl.BlockSpec(memory_space=pltpu.VMEM),
        scratch_shapes=[
            pltpu.VMEM(shape, rows.dtype),
            pltpu.SemaphoreType.DMA((count,)),
            pltpu.SemaphoreType.DMA((count,)),
        ],
        compiler_params=pltpu.CompilerParams(collective_id=1, has_side_effects=True),
        name="gather_rows",
    )(rows)


def scatter_kernel(count, parts_ref, sum_ref, got, send_sem, recv_sem):
    seq, slide = lax.axis_index("seq"), lax.axis_index("slide")
    meet_row(seq, slide, count)
    for step in range(1, count):
        other = lax.rem(seq + step, count)
        remote(
            parts_ref.at[other], got.at[step], send_sem.at[step], recv_sem.at[step], (other, slide)
        ).start()
    total = parts_ref[seq].astype(jnp.float32)
    for step in range(1, count):
        source = lax.rem(seq + count - step, count)
        wait = remote(
            parts_ref.at[seq], got.at[step], send_sem.at[step], recv_sem.at[step], (source, slide)
        )
        wait.wait_recv()
        wait.wait_send()
        total = total + got[step].astype(jnp.float32)
    sum_ref[...] = total


def scatter_rows(parts):
    count = parts.shape[0]
    return pl.pallas_call(
        functools.partial(scatter_kernel, count),
        out_shape=jax.ShapeDtypeStruct(parts.shape[1:], jnp.float32),
        in_specs=[pl.BlockSpec(memory_space=pltpu.VMEM)],
        out_specs=pl.BlockSpec(memory_space=pltpu.VMEM),
        scratch_shapes=[
            pltpu.VMEM(parts.shape, parts.dtype),
            pltpu.SemaphoreType.DMA((count,)),
            pltpu.SemaphoreType.DMA((count,)),
        ],
        compiler_params=pltpu.CompilerParams(collective_id=2, has_side_effects=True),
        name="scatter_rows",
    )(parts)


def per_device(
    direct,
    tokens,
    qkv_weight,
    out_weight,
    up_weight,
    down_weight,
    norm1_gain,
    norm1_bias,
    norm2_gain,
    norm2_bias,
    visible,
    cotangent,
):
    row_number = tokens.shape[1]
    embedding_width = tokens.shape[2]
    query_scale = HEAD_WIDTH ** (-0.5)
    first_row = lax.axis_index("seq") * row_number
    positions = first_row + jnp.arange(row_number, dtype=jnp.int32)
    row_validity = positions < visible[0]
    inputs = tokens[0].astype(jnp.float32)
    norm_one, pull_one = jax.vjp(layer_norm, inputs, norm1_gain, norm1_bias)
    normed = norm_one.astype(jnp.bfloat16)
    projected = jnp.dot(normed, qkv_weight, preferred_element_type=jnp.float32)
    query_rows = (
        (projected[:, :embedding_width] * query_scale)
        .astype(jnp.bfloat16)
        .reshape(row_number, HEADS, HEAD_WIDTH)
    )
    flat_keys = projected[:, embedding_width : 2 * embedding_width].astype(jnp.bfloat16)
    flat_values = projected[:, 2 * embedding_width :].astype(jnp.bfloat16)
    key_matrix = flat_keys.reshape(row_number, HEADS, HEAD_WIDTH)
    value_matrix = flat_values.reshape(row_number, HEADS, HEAD_WIDTH)
    if direct:
        gathered = gather_rows(
            projected[::DILATION_STEP, embedding_width:].astype(jnp.bfloat16), lax.axis_size("seq")
        ).reshape(-1, 2 * embedding_width)
        gathered_keys, gathered_values = (
            gathered[:, :embedding_width],
            gathered[:, embedding_width:],
        )
    else:
        gathered_keys, gathered_values = (
            lax.all_gather(flat_keys[::DILATION_STEP], "seq", axis=0, tiled=True),
            lax.all_gather(flat_values[::DILATION_STEP], "seq", axis=0, tiled=True),
        )
    distant_count = gathered_keys.shape[0]
    distant_valid = jnp.arange(distant_count, dtype=jnp.int32) * DILATION_STEP < visible[0]
    distant_keys = gathered_keys.reshape(distant_count, HEADS, HEAD_WIDTH)
    distant_values = gathered_values.reshape(distant_count, HEADS, HEAD_WIDTH)
    per_segment = SEG // QB
    attended_rows, row_maximum, row_sum_total = block_forward(
        query_rows,
        key_matrix,
        value_matrix,
        row_validity,
        distant_keys,
        distant_values,
        distant_valid,
    )
    attn_low = attended_rows.reshape(row_number, embedding_width).astype(jnp.bfloat16)
    after_attn = inputs + jnp.dot(attn_low, out_weight, preferred_element_type=jnp.float32)
    norm_two, pull_two = jax.vjp(layer_norm, after_attn, norm2_gain, norm2_bias)
    normed_two = norm_two.astype(jnp.bfloat16)
    up_cols = jnp.dot(normed_two, up_weight, preferred_element_type=jnp.float32)
    activated, pull_gelu = jax.vjp(exact_gelu, up_cols)
    hidden = activated.astype(jnp.bfloat16)
    result = after_attn + jnp.dot(hidden, down_weight, preferred_element_type=jnp.float32)
    mixed_out = jnp.where(row_validity[:, None], result, 0.0).astype(jnp.bfloat16)[None]
    grad_out = jnp.where(row_validity[:, None], cotangent[0], jnp.zeros_like(cotangent[0]))
    down_grad = jnp.einsum("tf,td->fd", hidden, grad_out, preferred_element_type=jnp.float32)
    hidden_grad = jnp.einsum("td,fd->tf", grad_out, down_weight, preferred_element_type=jnp.float32)
    (up_slope,) = pull_gelu(hidden_grad)
    up_low = up_slope.astype(jnp.bfloat16)
    up_grad = jnp.einsum("td,tf->df", normed_two, up_low, preferred_element_type=jnp.float32)
    norm_two_in = jnp.einsum("tf,df->td", up_low, up_weight, preferred_element_type=jnp.float32)
    after_part, gain_two_grad, shift_two_grad = pull_two(norm_two_in)
    resid_grad = grad_out.astype(jnp.float32) + after_part
    resid_low = resid_grad.astype(jnp.bfloat16)
    out_grad = jnp.einsum("td,te->de", attn_low, resid_low, preferred_element_type=jnp.float32)
    attn_grad = jnp.einsum("te,de->td", resid_low, out_weight, preferred_element_type=jnp.float32)
    attn_grad = attn_grad.astype(jnp.bfloat16).reshape(row_number, HEADS, HEAD_WIDTH)
    query_gradient, key_grad, value_grad, far_key_grad, far_value_grad = block_backward(
        query_rows,
        key_matrix,
        value_matrix,
        row_validity,
        distant_keys,
        distant_values,
        distant_valid,
        attn_grad,
        row_maximum,
        row_sum_total,
    )
    key_list = [key_grad]
    value_list = [value_grad]
    if direct:
        far_parts = jnp.concatenate(
            [
                far_key_grad.reshape(distant_count, embedding_width),
                far_value_grad.reshape(distant_count, embedding_width),
            ],
            axis=1,
        ).astype(jnp.bfloat16)
        owned = scatter_rows(far_parts.reshape(lax.axis_size("seq"), -1, 2 * embedding_width))
        owned_keys, owned_values = owned[:, :embedding_width], owned[:, embedding_width:]
    else:
        owned_keys, owned_values = (
            lax.psum_scatter(
                far_key_grad.reshape(distant_count, embedding_width),
                "seq",
                scatter_dimension=0,
                tiled=True,
            ),
            lax.psum_scatter(
                far_value_grad.reshape(distant_count, embedding_width),
                "seq",
                scatter_dimension=0,
                tiled=True,
            ),
        )
    chosen_count = row_number // DILATION_STEP
    segment_count = row_number // SEG
    nearby_keys = jnp.sum(
        jnp.stack(key_list).reshape(segment_count, per_segment, SEG, embedding_width), axis=1
    )
    nearby_values = jnp.sum(
        jnp.stack(value_list).reshape(segment_count, per_segment, SEG, embedding_width), axis=1
    )
    key_total = (
        nearby_keys.reshape(chosen_count, DILATION_STEP, embedding_width)
        .at[:, 0]
        .add(owned_keys)
        .reshape(row_number, embedding_width)
    )
    value_total = (
        nearby_values.reshape(chosen_count, DILATION_STEP, embedding_width)
        .at[:, 0]
        .add(owned_values)
        .reshape(row_number, embedding_width)
    )
    query_total = query_gradient.reshape(row_number, embedding_width)
    mixed_grad = jnp.concatenate(
        [
            (query_total * query_scale).astype(jnp.bfloat16),
            key_total.astype(jnp.bfloat16),
            value_total.astype(jnp.bfloat16),
        ],
        axis=1,
    )
    qkv_grad = jnp.einsum("td,tf->df", normed, mixed_grad, preferred_element_type=jnp.float32)
    norm_one_in = jnp.einsum(
        "tf,df->td", mixed_grad, qkv_weight, preferred_element_type=jnp.float32
    )
    input_part, gain_one_grad, shift_one_grad = pull_one(norm_one_in)
    tokens_grad = (resid_grad + input_part).astype(jnp.bfloat16)[None]
    weight_grads = (qkv_grad, out_grad, up_grad, down_grad)
    if direct:
        owners = lax.axis_size("seq")

        def by_owner(grad):
            rows = grad.shape[0] // owners
            wide = grad.astype(jnp.bfloat16).reshape(owners, rows, -1, embedding_width)
            return wide.transpose(0, 2, 1, 3).reshape(owners, -1, embedding_width)

        parts = jnp.stack(
            [
                by_owner(down_grad),
                by_owner(up_grad),
                jnp.concatenate([by_owner(qkv_grad), by_owner(out_grad)], axis=1),
            ]
        ).reshape(PIECES, SPLIT, -1, embedding_width)
        norm_parts = jnp.stack([gain_one_grad, shift_one_grad, gain_two_grad, shift_two_grad])
        sums, norm_grads = reduce_weights(parts, jnp.pad(norm_parts, ((0, 4), (0, 0))))
        sums = sums.reshape(PIECES, -1, embedding_width)

        def wide_again(block, rows):
            return block.reshape(-1, rows, embedding_width).transpose(1, 0, 2).reshape(rows, -1)

        rows = embedding_width // owners
        final_grads = (
            wide_again(sums[2, : 3 * rows], rows),
            sums[2, 3 * rows :],
            wide_again(sums[1], rows),
            sums[0],
        )
    else:
        row_parts = (
            lax.psum_scatter(weight_grads[0], "seq", scatter_dimension=0, tiled=True),
            lax.psum_scatter(weight_grads[1], "seq", scatter_dimension=0, tiled=True),
            lax.psum_scatter(weight_grads[2], "seq", scatter_dimension=0, tiled=True),
            lax.psum_scatter(weight_grads[3], "seq", scatter_dimension=0, tiled=True),
        )
        final_grads = (
            lax.psum(row_parts[0].astype(jnp.bfloat16), "slide").astype(jnp.float32),
            lax.psum(row_parts[1].astype(jnp.bfloat16), "slide").astype(jnp.float32),
            lax.psum(row_parts[2].astype(jnp.bfloat16), "slide").astype(jnp.float32),
            lax.psum(row_parts[3].astype(jnp.bfloat16), "slide").astype(jnp.float32),
        )
        norm_grads = lax.psum(
            (gain_one_grad, shift_one_grad, gain_two_grad, shift_two_grad), ("seq", "slide")
        )
    return (
        mixed_out,
        tokens_grad,
        final_grads[0],
        final_grads[1],
        final_grads[2],
        final_grads[3],
        norm_grads[0],
        norm_grads[1],
        norm_grads[2],
        norm_grads[3],
    )


def solution(mesh):
    placed = (
        P("slide", "seq", None),
        P(),
        P(),
        P(),
        P(),
        P(),
        P(),
        P(),
        P(),
        P("slide"),
        P("slide", "seq", None),
    )
    direct = mesh.shape["seq"] == 8 and mesh.shape["slide"] == 4
    return jax.shard_map(
        functools.partial(per_device, direct),
        mesh=mesh,
        in_specs=placed,
        out_specs=(
            P("slide", "seq", None),
            P("slide", "seq", None),
            P("seq", None),
            P("seq", None),
            P("seq", None),
            P("seq", None),
            P(),
            P(),
            P(),
            P(),
        ),
        check_vma=False,
    )
```

```python
import functools

import jax
import jax.numpy as jnp
from jax import lax
from jax.experimental import pallas as pl
from jax.experimental.pallas import tpu as pltpu
from jax.sharding import PartitionSpec as P

HEADS = 16
HEAD_WIDTH = 48
SEG = 512
QB = 512
DILATION_STEP = 16


epsilon = 1e-05


def layer_norm(values, norm_gain, norm_shift):
    average = jnp.mean(values, axis=-1, keepdims=True)
    centered = values - average
    variance = jnp.mean(centered * centered, axis=-1, keepdims=True)
    return centered * lax.rsqrt(variance + epsilon) * norm_gain + norm_shift


def exact_gelu(values):
    return jax.nn.gelu(values, approximate=False)


def block_scores(query_block, seg_keys, seg_valid, distant_keys, distant_valid):
    nearby_scores = jnp.einsum(
        "iyo,uyo->yiu", query_block, seg_keys, preferred_element_type=jnp.float32
    )
    nearby_scores = jnp.where(seg_valid[None, None, :], nearby_scores, -1000000000.0)
    far_scores = jnp.einsum(
        "iyo,uyo->yiu",
        query_block[::DILATION_STEP],
        distant_keys,
        preferred_element_type=jnp.float32,
    )
    far_scores = jnp.where(distant_valid[None, None, :], far_scores, -1000000000.0)
    return (nearby_scores, far_scores)


def block_forward(
    query_block, seg_keys, seg_values, seg_valid, distant_keys, distant_values, distant_valid
):
    nearby_scores, far_scores = block_scores(
        query_block, seg_keys, seg_valid, distant_keys, distant_valid
    )
    head_number = nearby_scores.shape[0]
    row_number = nearby_scores.shape[1]
    chosen_count = row_number // DILATION_STEP
    maximum_table = jnp.max(nearby_scores, axis=-1).reshape(
        head_number, chosen_count, DILATION_STEP
    )
    combined_top = jnp.maximum(maximum_table[:, :, 0], jnp.max(far_scores, axis=-1))
    row_maximum = maximum_table.at[:, :, 0].set(combined_top).reshape(head_number, row_number)
    nearby_exponent = jnp.exp(nearby_scores - row_maximum[:, :, None])
    far_exp = jnp.exp(far_scores - combined_top[:, :, None])
    exponent_sums = jnp.sum(nearby_exponent, axis=-1).reshape(
        head_number, chosen_count, DILATION_STEP
    )
    combined_total = exponent_sums[:, :, 0] + jnp.sum(far_exp, axis=-1)
    row_sum_total = exponent_sums.at[:, :, 0].set(combined_total).reshape(head_number, row_number)
    local_weights = (nearby_exponent / row_sum_total[:, :, None]).astype(jnp.bfloat16)
    far_weights = (far_exp / combined_total[:, :, None]).astype(jnp.bfloat16)
    attended_rows = jnp.einsum(
        "hqk,khd->qhd", local_weights, seg_values, preferred_element_type=jnp.float32
    )
    distant_attended = jnp.einsum(
        "hqk,khd->qhd", far_weights, distant_values, preferred_element_type=jnp.float32
    )
    attended_rows = (
        attended_rows.reshape(chosen_count, DILATION_STEP, head_number, HEAD_WIDTH)
        .at[:, 0]
        .add(distant_attended)
    )
    return (attended_rows.reshape(row_number, head_number, HEAD_WIDTH), row_maximum, row_sum_total)


def block_backward(
    query_block,
    seg_keys,
    seg_values,
    seg_valid,
    distant_keys,
    distant_values,
    distant_valid,
    gradient_block,
    row_maximum,
    row_sum_total,
):
    nearby_scores, far_scores = block_scores(
        query_block, seg_keys, seg_valid, distant_keys, distant_valid
    )
    head_number = row_maximum.shape[0]
    row_number = row_maximum.shape[1]
    chosen_count = row_number // DILATION_STEP
    combined_top = row_maximum.reshape(head_number, chosen_count, DILATION_STEP)[:, :, 0]
    combined_total = row_sum_total.reshape(head_number, chosen_count, DILATION_STEP)[:, :, 0]
    nearby_probability = (
        jnp.exp(nearby_scores - row_maximum[:, :, None]) / row_sum_total[:, :, None]
    )
    far_prob = jnp.exp(far_scores - combined_top[:, :, None]) / combined_total[:, :, None]
    local_weights = nearby_probability.astype(jnp.bfloat16)
    gradient_sampled = gradient_block[::DILATION_STEP]
    value_grad = jnp.einsum(
        "mns,nmg->smg", local_weights, gradient_block, preferred_element_type=jnp.float32
    )
    nearby_dots = jnp.einsum(
        "iyo,uyo->yiu", gradient_block, seg_values, preferred_element_type=jnp.float32
    )
    far_dots = jnp.einsum(
        "iyo,uyo->yiu", gradient_sampled, distant_values, preferred_element_type=jnp.float32
    )
    delta_table = jnp.sum(nearby_probability * nearby_dots, axis=-1).reshape(
        head_number, chosen_count, DILATION_STEP
    )
    joint_delta = delta_table[:, :, 0] + jnp.sum(far_prob * far_dots, axis=-1)
    row_delta = delta_table.at[:, :, 0].set(joint_delta).reshape(head_number, row_number)
    local_slope = (nearby_probability * (nearby_dots - row_delta[:, :, None])).astype(jnp.bfloat16)
    distant_slope = (far_prob * (far_dots - joint_delta[:, :, None])).astype(jnp.bfloat16)
    query_gradient = jnp.einsum(
        "hqk,khd->qhd", local_slope, seg_keys, preferred_element_type=jnp.float32
    )
    distant_query = jnp.einsum(
        "hqk,khd->qhd", distant_slope, distant_keys, preferred_element_type=jnp.float32
    )
    query_gradient = (
        query_gradient.reshape(chosen_count, DILATION_STEP, head_number, HEAD_WIDTH)
        .at[:, 0]
        .add(distant_query)
    )
    key_grad = jnp.einsum(
        "mns,nmg->smg", local_slope, query_block, preferred_element_type=jnp.float32
    )
    far_weights = far_prob.astype(jnp.bfloat16)
    far_value_grad = jnp.einsum(
        "mns,nmg->smg", far_weights, gradient_sampled, preferred_element_type=jnp.float32
    )
    far_key_grad = jnp.einsum(
        "mns,nmg->smg",
        distant_slope,
        query_block[::DILATION_STEP],
        preferred_element_type=jnp.float32,
    )
    return (
        query_gradient.reshape(row_number, head_number, HEAD_WIDTH),
        key_grad,
        value_grad,
        far_key_grad,
        far_value_grad,
    )


def plain_device(
    tokens,
    qkv_weight,
    out_weight,
    up_weight,
    down_weight,
    norm1_gain,
    norm1_bias,
    norm2_gain,
    norm2_bias,
    visible,
    cotangent,
):
    row_number = tokens.shape[1]
    embedding_width = tokens.shape[2]
    query_scale = HEAD_WIDTH ** (-0.5)
    first_row = lax.axis_index("seq") * row_number
    positions = first_row + jnp.arange(row_number, dtype=jnp.int32)
    row_validity = positions < visible[0]
    inputs = tokens[0].astype(jnp.float32)
    norm_one, pull_one = jax.vjp(layer_norm, inputs, norm1_gain, norm1_bias)
    normed = norm_one.astype(jnp.bfloat16)
    projected = jnp.dot(normed, qkv_weight, preferred_element_type=jnp.float32)
    query_rows = (
        (projected[:, :embedding_width] * query_scale)
        .astype(jnp.bfloat16)
        .reshape(row_number, HEADS, HEAD_WIDTH)
    )
    flat_keys = projected[:, embedding_width : 2 * embedding_width].astype(jnp.bfloat16)
    flat_values = projected[:, 2 * embedding_width :].astype(jnp.bfloat16)
    key_matrix = flat_keys.reshape(row_number, HEADS, HEAD_WIDTH)
    value_matrix = flat_values.reshape(row_number, HEADS, HEAD_WIDTH)
    gathered_keys, gathered_values = (
        lax.all_gather(flat_keys[::DILATION_STEP], "seq", axis=0, tiled=True),
        lax.all_gather(flat_values[::DILATION_STEP], "seq", axis=0, tiled=True),
    )
    distant_count = gathered_keys.shape[0]
    distant_valid = jnp.arange(distant_count, dtype=jnp.int32) * DILATION_STEP < visible[0]
    distant_keys = gathered_keys.reshape(distant_count, HEADS, HEAD_WIDTH)
    distant_values = gathered_values.reshape(distant_count, HEADS, HEAD_WIDTH)
    per_segment = SEG // QB
    attended_rows, row_maximum, row_sum_total = block_forward(
        query_rows,
        key_matrix,
        value_matrix,
        row_validity,
        distant_keys,
        distant_values,
        distant_valid,
    )
    attn_low = attended_rows.reshape(row_number, embedding_width).astype(jnp.bfloat16)
    after_attn = inputs + jnp.dot(attn_low, out_weight, preferred_element_type=jnp.float32)
    norm_two, pull_two = jax.vjp(layer_norm, after_attn, norm2_gain, norm2_bias)
    normed_two = norm_two.astype(jnp.bfloat16)
    up_cols = jnp.dot(normed_two, up_weight, preferred_element_type=jnp.float32)
    activated, pull_gelu = jax.vjp(exact_gelu, up_cols)
    hidden = activated.astype(jnp.bfloat16)
    result = after_attn + jnp.dot(hidden, down_weight, preferred_element_type=jnp.float32)
    mixed_out = jnp.where(row_validity[:, None], result, 0.0).astype(jnp.bfloat16)[None]
    grad_out = jnp.where(row_validity[:, None], cotangent[0], jnp.zeros_like(cotangent[0]))
    down_grad = jnp.einsum("tf,td->fd", hidden, grad_out, preferred_element_type=jnp.float32)
    hidden_grad = jnp.einsum("td,fd->tf", grad_out, down_weight, preferred_element_type=jnp.float32)
    (up_slope,) = pull_gelu(hidden_grad)
    up_low = up_slope.astype(jnp.bfloat16)
    up_grad = jnp.einsum("td,tf->df", normed_two, up_low, preferred_element_type=jnp.float32)
    norm_two_in = jnp.einsum("tf,df->td", up_low, up_weight, preferred_element_type=jnp.float32)
    after_part, gain_two_grad, shift_two_grad = pull_two(norm_two_in)
    resid_grad = grad_out.astype(jnp.float32) + after_part
    resid_low = resid_grad.astype(jnp.bfloat16)
    out_grad = jnp.einsum("td,te->de", attn_low, resid_low, preferred_element_type=jnp.float32)
    attn_grad = jnp.einsum("te,de->td", resid_low, out_weight, preferred_element_type=jnp.float32)
    attn_grad = attn_grad.astype(jnp.bfloat16).reshape(row_number, HEADS, HEAD_WIDTH)
    query_gradient, key_grad, value_grad, far_key_grad, far_value_grad = block_backward(
        query_rows,
        key_matrix,
        value_matrix,
        row_validity,
        distant_keys,
        distant_values,
        distant_valid,
        attn_grad,
        row_maximum,
        row_sum_total,
    )
    key_list = [key_grad]
    value_list = [value_grad]
    owned_keys, owned_values = (
        lax.psum_scatter(
            far_key_grad.reshape(distant_count, embedding_width),
            "seq",
            scatter_dimension=0,
            tiled=True,
        ),
        lax.psum_scatter(
            far_value_grad.reshape(distant_count, embedding_width),
            "seq",
            scatter_dimension=0,
            tiled=True,
        ),
    )
    chosen_count = row_number // DILATION_STEP
    segment_count = row_number // SEG
    nearby_keys = jnp.sum(
        jnp.stack(key_list).reshape(segment_count, per_segment, SEG, embedding_width), axis=1
    )
    nearby_values = jnp.sum(
        jnp.stack(value_list).reshape(segment_count, per_segment, SEG, embedding_width), axis=1
    )
    key_total = (
        nearby_keys.reshape(chosen_count, DILATION_STEP, embedding_width)
        .at[:, 0]
        .add(owned_keys)
        .reshape(row_number, embedding_width)
    )
    value_total = (
        nearby_values.reshape(chosen_count, DILATION_STEP, embedding_width)
        .at[:, 0]
        .add(owned_values)
        .reshape(row_number, embedding_width)
    )
    query_total = query_gradient.reshape(row_number, embedding_width)
    mixed_grad = jnp.concatenate(
        [
            (query_total * query_scale).astype(jnp.bfloat16),
            key_total.astype(jnp.bfloat16),
            value_total.astype(jnp.bfloat16),
        ],
        axis=1,
    )
    qkv_grad = jnp.einsum("td,tf->df", normed, mixed_grad, preferred_element_type=jnp.float32)
    norm_one_in = jnp.einsum(
        "tf,df->td", mixed_grad, qkv_weight, preferred_element_type=jnp.float32
    )
    input_part, gain_one_grad, shift_one_grad = pull_one(norm_one_in)
    tokens_grad = (resid_grad + input_part).astype(jnp.bfloat16)[None]
    weight_grads = (qkv_grad, out_grad, up_grad, down_grad)
    row_parts = (
        lax.psum_scatter(weight_grads[0], "seq", scatter_dimension=0, tiled=True),
        lax.psum_scatter(weight_grads[1], "seq", scatter_dimension=0, tiled=True),
        lax.psum_scatter(weight_grads[2], "seq", scatter_dimension=0, tiled=True),
        lax.psum_scatter(weight_grads[3], "seq", scatter_dimension=0, tiled=True),
    )
    final_grads = (
        lax.psum(row_parts[0].astype(jnp.bfloat16), "slide").astype(jnp.float32),
        lax.psum(row_parts[1].astype(jnp.bfloat16), "slide").astype(jnp.float32),
        lax.psum(row_parts[2].astype(jnp.bfloat16), "slide").astype(jnp.float32),
        lax.psum(row_parts[3].astype(jnp.bfloat16), "slide").astype(jnp.float32),
    )
    norm_grads = lax.psum(
        (gain_one_grad, shift_one_grad, gain_two_grad, shift_two_grad), ("seq", "slide")
    )
    return (
        mixed_out,
        tokens_grad,
        final_grads[0],
        final_grads[1],
        final_grads[2],
        final_grads[3],
        norm_grads[0],
        norm_grads[1],
        norm_grads[2],
        norm_grads[3],
    )


MESH = pl.DeviceIdType.MESH
LOW = jnp.bfloat16
FULL = jnp.float32
AUG = 64
LANES = 128
NEVER = -1000000000.0
ANY = pl.BlockSpec(memory_space=pl.ANY)
VMEM = pl.BlockSpec(memory_space=pltpu.VMEM)
SMEM = pl.BlockSpec(memory_space=pltpu.SMEM)


def nn(left, right):
    return jnp.dot(left, right, preferred_element_type=FULL)


def nt(left, right):
    return lax.dot_general(left, right, (((1,), (1,)), ((), ())), preferred_element_type=FULL)


def tn(left, right):
    return lax.dot_general(left, right, (((0,), (0,)), ((), ())), preferred_element_type=FULL)


def remote(src, dst, send_sem, recv_sem, device):
    return pltpu.make_async_remote_copy(
        src_ref=src,
        dst_ref=dst,
        send_sem=send_sem,
        recv_sem=recv_sem,
        device_id=device,
        device_id_type=MESH,
    )


def greet(devices):
    barrier = pltpu.get_barrier_semaphore()
    for device in devices:
        pl.semaphore_signal(barrier, inc=1, device_id=device, device_id_type=MESH)
    pl.semaphore_wait(barrier, len(devices))


def row_peers(count):
    seq, slide = lax.axis_index("seq"), lax.axis_index("slide")
    return [(lax.rem(seq + step, count), slide) for step in range(1, count)]


def spread(ref, values):
    for group in range(ref.shape[0]):
        ref[group] = values[:, group * LANES : (group + 1) * LANES]


def strided_rows(ref, step, count):
    groups = [
        ref[group, pl.ds(step, count, stride=DILATION_STEP), :] for group in range(ref.shape[0])
    ]
    return jnp.concatenate(groups, axis=1)


def strided_store(ref, step, count, values):
    for group in range(ref.shape[0]):
        ref[group, pl.ds(step, count, stride=DILATION_STEP), :] = values[
            :, group * LANES : (group + 1) * LANES
        ]


def row_mean(values):
    return jnp.mean(values, axis=-1, keepdims=True)


def fold_rows(values):
    return jnp.sum(values.reshape(-1, 8, values.shape[-1]), axis=0)


def mask_rows(ref, bias):
    first = lax.broadcasted_iota(jnp.int32, (AUG - HEAD_WIDTH, ref.shape[2]), 0) == 0
    ref[:, HEAD_WIDTH:, :] = jnp.broadcast_to(
        jnp.where(first, bias, 0.0).astype(LOW), (HEADS, AUG - HEAD_WIDTH, ref.shape[2])
    )


def forward_kernel(
    count, tokens, cotangent, qkv_weight, out_weight, up_weight, down_weight,
    gain_one, shift_one, gain_two, shift_two, visible,
    mixed_out, far_key_out, far_value_out, query_out, key_out, value_out, weights_out,
    far_weights_out, scale_out, far_scale_out, delta_out, slope_out, normed_out, norm_out,
    spread_out, resid_out, down_out, up_out, out_out, gains_out,
    wide, held_n1, held_r1, h1, h1_t, wqkv, wo, wup, wdown,
    query, key, value, own_far, all_far, far_key, far_value,
    top, total, attended, weights, far_weights, scale, far_scale, attn_t,
    after, norm_two, spread_two, dyb, resid, delta, slope,
    down_grad, up_grad, out_grad,
    load_sem, store_sem, send_sem, recv_sem,
):
    seq, slide = lax.axis_index("seq"), lax.axis_index("slide")
    rows, width = tokens.shape
    chosen = rows // DILATION_STEP
    tiles = wup.shape[0]
    loads = [pltpu.make_async_copy(qkv_weight, wqkv, load_sem.at[0])]
    loads.append(pltpu.make_async_copy(out_weight, wo, load_sem.at[1]))
    for tile in range(tiles):
        at = pl.ds(tile * width, width)
        loads.append(
            pltpu.make_async_copy(up_weight.at[:, at], wup.at[tile], load_sem.at[2 + 2 * tile])
        )
        loads.append(
            pltpu.make_async_copy(down_weight.at[at], wdown.at[tile], load_sem.at[3 + 2 * tile])
        )
    for load in loads:
        load.start()
    stores = []

    def store(source, target):
        copy = pltpu.make_async_copy(source, target, store_sem.at[len(stores)])
        copy.start()
        stores.append(copy)

    greet(row_peers(count))
    first_row = seq * rows
    limit = visible[0]

    def valid_rows(step):
        places = lax.broadcasted_iota(jnp.int32, (chosen, 1), 0) * DILATION_STEP + step
        return first_row + places < limit

    spread(wide, tokens[...].astype(FULL))

    @pl.loop(0, DILATION_STEP)
    def _(step):
        at = pl.ds(pl.multiple_of(step * chosen, chosen), chosen)
        values = strided_rows(wide, step, chosen)
        centered = values - row_mean(values)
        inverse = lax.rsqrt(row_mean(centered * centered) + epsilon)
        normal = centered * inverse
        after[at] = values
        held_n1[at] = normal
        held_r1[at] = jnp.broadcast_to(inverse, (chosen, LANES))
        h1[at] = (normal * gain_one[...] + shift_one[...]).astype(LOW)

    store(held_n1, norm_out)
    store(held_r1, spread_out)
    loads[0].wait()

    def project(part):
        return nn(h1[...], wqkv[:, part * width : (part + 1) * width])

    for part, ref in ((1, key), (2, value)):
        projected = project(part).astype(LOW)
        own_far[:, (part - 1) * width : part * width] = projected[:chosen]
        ref[:, :HEAD_WIDTH, :] = projected.T.reshape(HEADS, HEAD_WIDTH, rows)
    peers = row_peers(count)
    sends = [
        remote(own_far, all_far.at[seq], send_sem.at[n], recv_sem.at[n], peer)
        for n, peer in enumerate(peers)
    ]
    for send in sends:
        send.start()
    all_far[seq] = own_far[...]
    projected = (project(0) * HEAD_WIDTH ** (-0.5)).astype(LOW)
    query[:, :HEAD_WIDTH, :] = projected.T.reshape(HEADS, HEAD_WIDTH, rows)
    places = lax.broadcasted_iota(jnp.int32, (1, rows), 1)
    places = first_row + (places % chosen) * DILATION_STEP + places // chosen
    mask_rows(key, jnp.where(places < limit, 0.0, NEVER))
    mask_rows(query, jnp.ones((1, rows), FULL))
    h1_t[...] = h1[...].T
    store(h1_t, normed_out)
    store(query, query_out)
    store(key, key_out)
    store(value, value_out)

    @pl.loop(0, HEADS // 4)
    def _(group):
        for member in range(4):
            head = group * 4 + member
            scores = tn(key[head], query[head])
            highest = jnp.max(scores, axis=0, keepdims=True)
            exponent = jnp.exp(scores - highest)
            top[head] = highest
            total[head] = jnp.sum(exponent, axis=0, keepdims=True)
            low = exponent.astype(LOW)
            weights[head] = low
            attended[head] = nn(value[head], low)

    store(weights, weights_out)

    spread(wide, cotangent[...].astype(FULL))

    @pl.loop(0, DILATION_STEP)
    def _(step):
        at = pl.ds(pl.multiple_of(step * chosen, chosen), chosen)
        dyb[at] = jnp.where(valid_rows(step), strided_rows(wide, step, chosen), 0.0).astype(LOW)

    for n in range(count - 1):
        source = lax.rem(seq + count - 1 - n, count)
        wait = remote(own_far, all_far.at[source], send_sem.at[n], recv_sem.at[n], peers[0])
        wait.wait_recv()
        wait.wait_send()
    distant = count * chosen
    for part, ref in ((0, far_key), (1, far_value)):
        flat = all_far[:, :, part * width : (part + 1) * width].reshape(distant, width)
        ref[:, :HEAD_WIDTH, :] = flat.T.reshape(HEADS, HEAD_WIDTH, distant)
    places = lax.broadcasted_iota(jnp.int32, (1, distant), 1) * DILATION_STEP
    mask_rows(far_key, jnp.where(places < limit, 0.0, NEVER))
    store(far_key, far_key_out)
    store(far_value, far_value_out)
    lane_mask = jnp.where(lax.broadcasted_iota(jnp.int32, (1, LANES), 1) < chosen, 0.0, NEVER)

    @pl.loop(0, HEADS // 4)
    def _(group):
        for member in range(4):
            head = group * 4 + member
            scores = tn(far_key[head], query[head][:, :LANES]) + lane_mask
            highest = jnp.max(scores, axis=0, keepdims=True)
            exponent = jnp.exp(scores - highest)
            low = exponent.astype(LOW)
            far_weights[head] = low
            near = top[head][:, :LANES]
            joint = jnp.maximum(near, highest)
            near_part, far_part = jnp.exp(near - joint), jnp.exp(highest - joint)
            joint_total = total[head][:, :LANES] * near_part + far_part * jnp.sum(
                exponent, axis=0, keepdims=True
            )
            near_part, far_part = near_part / joint_total, far_part / joint_total
            far_scale[head] = far_part
            local = jnp.concatenate([near_part, 1.0 / total[head][:, LANES:]], axis=1)
            scale[head] = local
            result = attended[head] * local
            with_far = result[:, :LANES] + nn(far_value[head], low)[:HEAD_WIDTH] * far_part
            result = jnp.concatenate([with_far, result[:, LANES:]], axis=1)
            attended[head] = result
            attn_t[head] = result.astype(LOW)

    store(far_weights, far_weights_out)
    store(scale, scale_out)
    store(far_scale, far_scale_out)
    loads[1].wait()
    flat_attn = attn_t[...].reshape(width, rows)
    after[...] += nn(flat_attn.T, wo[...])
    h2 = h1

    @pl.loop(0, DILATION_STEP)
    def _(step):
        at = pl.ds(pl.multiple_of(step * chosen, chosen), chosen)
        values = after[at]
        centered = values - row_mean(values)
        inverse = lax.rsqrt(row_mean(centered * centered) + epsilon)
        normal = centered * inverse
        norm_two[at] = normal
        spread_two[at] = jnp.broadcast_to(inverse, (chosen, LANES))
        h2[at] = (normal * gain_two[...] + shift_two[...]).astype(LOW)

    resid[...] = jnp.zeros_like(resid)
    h2_t = h2[...].T
    for load in loads[2:]:
        load.wait()

    blocks = 4 * count // tiles
    sent = {}
    for tile in range(tiles):
        slot = tile % 2
        up_tile, down_tile = wup[tile], wdown[tile]
        hidden = nn(h2[...], up_tile)
        hidden_slope = nt(dyb[...], down_tile)
        share = 0.5 * (1.0 + lax.erf(hidden * 0.7071067811865476))
        active = (hidden * share).astype(LOW)
        density = hidden * jnp.exp(-0.5 * hidden * hidden) * 0.3989422804014327
        low_slope = (hidden_slope * (share + density)).astype(LOW)
        after[...] += nn(active, down_tile)
        resid[...] += nt(low_slope, up_tile)
        for n in sent.pop(tile - 2, ()):
            stores[n].wait()
            stores[n] = None
        grads = nn(h2_t, low_slope).astype(LOW)
        up_grad[slot] = grads.reshape(count, -1, width)
        store(up_grad.at[slot], up_out.at[:, tile])
        grads = tn(active, dyb[...]).astype(LOW)
        down_grad[slot] = grads.reshape(blocks, -1, width)
        store(down_grad.at[slot], down_out.at[pl.ds(tile * blocks, blocks)])
        sent[tile] = (len(stores) - 2, len(stores) - 1)

    gains_out[...] = jnp.zeros_like(gains_out)

    @pl.loop(0, DILATION_STEP)
    def _(step):
        at = pl.ds(pl.multiple_of(step * chosen, chosen), chosen)
        strided_store(wide, step, chosen, jnp.where(valid_rows(step), after[at], 0.0))
        given, normal = resid[at], norm_two[at]
        gains_out[0] += fold_rows(given * normal)
        gains_out[1] += fold_rows(given)
        scaled = given * gain_two[...]
        part = scaled - row_mean(scaled) - normal * row_mean(scaled * normal)
        value_here = dyb[at].astype(FULL) + spread_two[at][:, :1] * part
        resid[at] = value_here
        h1[at] = value_here.astype(LOW)

    store(resid, resid_out)
    low_resid = h1
    for group in range(width // LANES):
        mixed_out[:, group * LANES : (group + 1) * LANES] = wide[group].astype(LOW)
    grads = nn(flat_attn, low_resid[...]).astype(LOW)
    out_grad[...] = grads.reshape(count, -1, width)
    store(out_grad, out_out)
    slope[...] = nt(wo[...], low_resid[...]).astype(LOW).reshape(HEADS, HEAD_WIDTH, rows)
    store(slope, slope_out)

    @pl.loop(0, HEADS)
    def _(head):
        delta[head] = jnp.sum(slope[head].astype(FULL) * attended[head], axis=0, keepdims=True)

    store(delta, delta_out)
    for copy in stores:
        if copy is not None:
            copy.wait()


def forward_pass(
    count, tokens, cotangent, qkv_weight, out_weight, up_weight, down_weight, norms, visible
):
    rows, width = tokens.shape
    chosen = rows // DILATION_STEP
    distant = count * chosen
    hidden = up_weight.shape[1]
    tiles = hidden // width
    owned = width // count
    low, full = functools.partial(jax.ShapeDtypeStruct, dtype=LOW), functools.partial(
        jax.ShapeDtypeStruct, dtype=FULL
    )
    outs = {
        "mixed": low((rows, width)),
        "far_key": low((HEADS, AUG, distant)),
        "far_value": low((HEADS, HEAD_WIDTH, distant)),
        "query": low((HEADS, AUG, rows)),
        "key": low((HEADS, AUG, rows)),
        "value": low((HEADS, HEAD_WIDTH, rows)),
        "weights": low((HEADS, rows, rows)),
        "far_weights": low((HEADS, distant, LANES)),
        "scale": full((HEADS, 1, rows)),
        "far_scale": full((HEADS, 1, LANES)),
        "delta": full((HEADS, 1, rows)),
        "slope": low((HEADS, HEAD_WIDTH, rows)),
        "normed": low((width, rows)),
        "norm_one": full((rows, width)),
        "spread_one": full((rows, LANES)),
        "resid": full((rows, width)),
        "down": low((count * 4, owned, width)),
        "up": low((count, 4, owned, width)),
        "out": low((count, owned, width)),
        "gains": full((2, 8, width)),
    }
    held = {name: pltpu.VMEM(out.shape, out.dtype) for name, out in outs.items()}
    vm = pltpu.VMEM
    scratch = [
        vm((width // LANES, rows, LANES), FULL),
        held["norm_one"],
        held["spread_one"],
        vm((rows, width), LOW),
        held["normed"],
        vm(qkv_weight.shape, LOW),
        vm(out_weight.shape, LOW),
        vm((tiles, width, width), LOW),
        vm((tiles, width, width), LOW),
        held["query"],
        held["key"],
        held["value"],
        vm((chosen, 2 * width), LOW),
        vm((count, chosen, 2 * width), LOW),
        held["far_key"],
        held["far_value"],
        vm((HEADS, 1, rows), FULL),
        vm((HEADS, 1, rows), FULL),
        vm((HEADS, HEAD_WIDTH, rows), FULL),
        held["weights"],
        held["far_weights"],
        held["scale"],
        held["far_scale"],
        vm((HEADS, HEAD_WIDTH, rows), LOW),
        vm((rows, width), FULL),
        vm((rows, width), FULL),
        vm((rows, LANES), FULL),
        vm((rows, width), LOW),
        held["resid"],
        held["delta"],
        held["slope"],
        vm((2, 4 * count // tiles, owned, width), LOW),
        vm((2, count, owned, width), LOW),
        held["out"],
        pltpu.SemaphoreType.DMA((2 + 2 * tiles,)),
        pltpu.SemaphoreType.DMA((len(outs) + 2 * tiles,)),
        pltpu.SemaphoreType.DMA((count - 1,)),
        pltpu.SemaphoreType.DMA((count - 1,)),
    ]
    results = pl.pallas_call(
        functools.partial(forward_kernel, count),
        out_shape=tuple(outs.values()),
        in_specs=[VMEM, VMEM, ANY, ANY, ANY, ANY, VMEM, VMEM, VMEM, VMEM, SMEM],
        out_specs=tuple(VMEM if name in ("mixed", "gains") else ANY for name in outs),
        scratch_shapes=scratch,
        compiler_params=pltpu.CompilerParams(
            collective_id=1, has_side_effects=True, vmem_limit_bytes=63 << 20
        ),
        name="forward_pass",
    )(tokens, cotangent, qkv_weight, out_weight, up_weight, down_weight, *norms, visible)
    return dict(zip(outs, results))


class Place:
    orders = (("y", "x", "a", "b"), ("x", "a", "b", "y"))

    def __init__(self):
        seq, slide = lax.axis_index("seq"), lax.axis_index("slide")
        self.b, self.a, self.x = seq // 4, (seq // 2) % 2, seq % 2
        self.y, self.c = slide // 2, slide % 2
        self.seq, self.slide = seq, slide
        self.partner = {
            "c": (seq, slide + 1 - 2 * self.c),
            "y": (seq, slide + 2 - 4 * self.y),
            "x": (seq + 1 - 2 * self.x, slide),
            "a": (seq + 2 - 4 * self.a, slide),
            "b": (seq + 4 - 8 * self.b, slide),
        }

    def blocks(self, core, phase, flip):
        order = self.orders[core]
        mine = {"b": self.b, "a": self.a, "x": self.x, "y": self.y}
        choices = []
        for name in ("b", "a", "x", "y"):
            at = order.index(name) + 1
            if at < phase:
                choices.append([mine[name]])
            elif at == phase:
                choices.append([1 - mine[name] if flip else mine[name]])
            else:
                choices.append([0, 1])
        return [
            ((b * 2 + a) * 2 + x) * 2 + y
            for b in choices[0]
            for a in choices[1]
            for x in choices[2]
            for y in choices[3]
        ]


class Reducer:
    slots = {1: (0, 8), 2: (8, 4), 3: (12, 2), 4: (14, 1)}

    def __init__(self, place, away, kept, core_got, got, final, send_sem, recv_sem):
        self.place, self.away, self.kept = place, away, kept
        self.core_got, self.got, self.final = core_got, got, final
        self.send_sem, self.recv_sem = send_sem, recv_sem

    def landing(self, phase):
        if phase == 0:
            return self.core_got
        if phase >= 5:
            return self.final.at[pl.ds(0, phase - 4)]
        first, count = self.slots[phase]
        return self.got.at[pl.ds(first, count)]

    def start(self, phase):
        place = self.place
        send, recv = self.send_sem.at[phase], self.recv_sem.at[phase]
        if phase == 0:
            for owner in range(8):
                target = self.core_got.at[pl.ds(owner * 2, 2)]
                remote(self.away(owner), target, send, recv, place.partner["c"]).start()
        elif phase <= 4:
            first, _ = self.slots[phase]
            for core in range(2):

                @pl.when(place.c == core)
                def _(core=core):
                    partner = place.partner[place.orders[core][phase - 1]]
                    for n, block in enumerate(place.blocks(core, phase, True)):
                        target = self.got.at[first + n]
                        remote(self.kept.at[block], target, send, recv, partner).start()
        elif phase == 5:
            own = self.final.at[pl.ds(place.c * 2 + place.y, 1)]
            remote(own, own, send, recv, place.partner["y"]).start()
        else:
            own = self.final.at[pl.ds(place.c * 2, 2)]
            remote(own, own, send, recv, place.partner["c"]).start()

    def finish(self, phase):
        place = self.place
        whole = self.landing(phase)
        send, recv = self.send_sem.at[phase], self.recv_sem.at[phase]
        wait = remote(whole, whole, send, recv, place.partner["c"])
        wait.wait_recv()
        wait.wait_send()
        if phase == 0:

            @pl.loop(0, 16)
            def _(block):
                self.add(block, self.core_got, block)
        elif phase <= 4:
            first, _ = self.slots[phase]
            for core in range(2):

                @pl.when(place.c == core)
                def _(core=core):
                    for n, block in enumerate(place.blocks(core, phase, False)):
                        self.add(block, self.got, first + n)
            if phase == 4:
                self.final[place.c * 2 + place.y] = self.kept[place.seq * 2 + place.y]

    def add(self, block, source, at):
        total = self.kept[block].astype(FULL) + source[at].astype(FULL)
        self.kept[block] = total.astype(LOW)


class NormSum:
    def __init__(self, place, total, got, send_sem, recv_sem):
        self.place, self.total, self.got = place, total, got
        self.send_sem, self.recv_sem = send_sem, recv_sem

    def start(self, step):
        place = self.place
        send, recv = self.send_sem.at[step], self.recv_sem.at[step]
        for core in range(2):

            @pl.when(place.c == core)
            def _(core=core):
                partner = place.partner[(("c",) + place.orders[core])[step]]
                remote(self.total.at[step], self.got.at[step], send, recv, partner).start()

    def finish(self, step):
        got = self.got.at[step]
        send, recv = self.send_sem.at[step], self.recv_sem.at[step]
        wait = remote(got, got, send, recv, self.place.partner["c"])
        wait.wait_recv()
        wait.wait_send()
        self.total[step + 1] = self.total[step] + self.got[step]


LAST = 6


def backward_kernel(
    count, mixed_names, *refs
):
    (
        query_in, key_in, value_in, far_key_in, far_value_in, weights_in, far_weights_in,
        scale, far_scale, delta, slope_in, normed_in, norm_in, spread_in, resid_in,
        down_in, up_in, out_in, gains, gain_one, qkv_weight,
        tokens_out, sums_out, norm_out,
        query, key, value, far_key, far_value, weights, far_weights, slope, normed, norm_one,
        spread_one, resid, wqkv,
        far_query, far_send, far_got, near_low, slopes, given, wide,
        kept, third, core_got, got, final, stage, totals, norm_got,
        load_sem, store_sem, send_sem, recv_sem, norm_send, norm_recv, far_send_sem, far_recv_sem,
    ) = refs
    place = Place()
    seq, slide, core = place.seq, place.slide, place.c
    rows, width = resid.shape
    chosen = rows // DILATION_STEP
    distant = count * chosen
    loads = []

    def load(source, target):
        copy = pltpu.make_async_copy(source, target, load_sem.at[len(loads)])
        copy.start()
        loads.append(copy)
        return len(loads) - 1

    far_loads = [
        load(far_value_in, far_value),
        load(far_key_in, far_key),
        load(slope_in, slope),
        load(far_weights_in, far_weights),
        load(query_in, query),
    ]
    piece_loads = [
        [load(source.at[:, pl.ds(core * 2, 2)], kept.at[p])] for p, source in ((0, down_in), (1, up_in))
    ]
    near_loads = [load(key_in, key), load(value_in, value), load(weights_in, weights)]
    last_loads = [
        load(normed_in, normed),
        load(norm_in, norm_one),
        load(spread_in, spread_one),
        load(resid_in, resid),
        load(qkv_weight, wqkv),
        load(out_in, third.at[(core + 1) % 2, :, 1]),
    ]
    peers = row_peers(count)
    others = [place.partner["c"], place.partner["y"]] + peers
    greet(others)

    pieces = []
    for p in range(3):
        if p < 2:
            source = (down_in, up_in)[p]

            def away(owner, source=source):
                return source.at[owner, pl.ds((1 - core) * 2, 2)]

        else:

            def away(owner):
                return third.at[1, owner]

        own = kept.at[p] if p < 2 else third.at[0]
        pieces.append(
            Reducer(
                place,
                away,
                own.reshape(16, *own.shape[2:]),
                core_got.at[p % 2],
                got.at[p],
                final.at[p],
                send_sem.at[p],
                recv_sem.at[p],
            )
        )
    norm = NormSum(place, totals, norm_got, norm_send, norm_recv)

    def finish_piece(p):
        if p:
            loads_out[-1].wait()
        stage[...] = final[p].astype(FULL)
        copy = pltpu.make_async_copy(stage, sums_out.at[p], store_sem.at[p])
        copy.start()
        loads_out.append(copy)

    loads_out = []

    def turn(number, skip=()):
        for p in (0, 1):
            phase = number - p
            if phase == 0:
                for n in piece_loads[p]:
                    loads[n].wait()
            if 1 <= phase <= LAST + 1:
                pieces[p].finish(phase - 1)
            if 0 <= phase <= LAST:
                pieces[p].start(phase)
            if phase == LAST + 1:
                finish_piece(p)

    turn(0)
    for n in far_loads:
        loads[n].wait()

    @pl.loop(0, HEADS // 4)
    def _(group):
        for member in range(4):
            head = group * 4 + member
            first_slope = slope[head][:, :LANES]
            low = far_weights[head]
            change = tn(far_value[head], first_slope) - delta[head][:, :LANES]
            score_slope = (low.astype(FULL) * far_scale[head] * change).astype(LOW)
            far_query[head] = nn(far_key[head], score_slope)[:HEAD_WIDTH]
            scaled = (first_slope.astype(FULL) * far_scale[head]).astype(LOW)
            given[0, head, :, :distant] = nt(query[head][:HEAD_WIDTH, :LANES], score_slope).astype(LOW)
            given[1, head, :, :distant] = nt(scaled, low).astype(LOW)

    for part in range(2):
        flat = given[part, :, :, :distant].reshape(width, distant).T
        far_send[:, :, part * width : (part + 1) * width] = flat.reshape(count, chosen, width)
    sends = [
        remote(far_send.at[peer[0]], far_got.at[n], far_send_sem.at[n], far_recv_sem.at[n], peer)
        for n, peer in enumerate(peers)
    ]
    for send in sends:
        send.start()
    for n in near_loads:
        loads[n].wait()
    turn(1)
    for group in range(4):
        for member in range(4):
            head = group * 4 + member
            low = weights[head]
            change = tn(value[head], slope[head]) - delta[head]
            score_slope = (low.astype(FULL) * scale[head] * change).astype(LOW)
            query_slope = nn(key[head], score_slope)[:HEAD_WIDTH]
            key_slope = nt(query[head][:HEAD_WIDTH], score_slope)
            scaled = (slope[head].astype(FULL) * scale[head]).astype(LOW)
            value_slope = nt(scaled, low)
            first = query_slope[:, :LANES] + far_query[head]
            query_slope = jnp.concatenate([first, query_slope[:, LANES:]], axis=1)
            slopes[0, head] = (query_slope * HEAD_WIDTH ** (-0.5)).astype(LOW)
            near_low[0, head] = key_slope[:, :LANES]
            near_low[1, head] = value_slope[:, :LANES]
            slopes[1, head, :, LANES:] = key_slope[:, LANES:].astype(LOW)
            slopes[2, head, :, LANES:] = value_slope[:, LANES:].astype(LOW)
        turn(2 + group)

    total = far_send[seq].astype(FULL)
    for n in range(count - 1):
        wait = remote(far_got.at[n], far_got.at[n], far_send_sem.at[n], far_recv_sem.at[n], peers[0])
        wait.wait_recv()
        wait.wait_send()
        total = total + far_got[n].astype(FULL)
    total = jnp.concatenate([total, jnp.zeros((LANES - chosen, 2 * width), FULL)], axis=0).T
    total = total.reshape(2, HEADS, HEAD_WIDTH, LANES)
    slopes[1:, :, :, :LANES] = (near_low[...] + total).astype(LOW)
    for n in last_loads:
        loads[n].wait()
    for part in range(3):
        flat = slopes[part].reshape(width, rows)
        grads = nt(normed[...], flat).astype(LOW)
        third[(part // 2 + core) % 2, :, part % 2] = grads.reshape(count, -1, width)
    turn(6)
    pieces[2].start(0)
    into = nn(wqkv[:, :width], slopes[0].reshape(width, rows))
    for part in (1, 2):
        into += nn(wqkv[:, part * width : (part + 1) * width], slopes[part].reshape(width, rows))
    norm_one_in = wide
    spread(norm_one_in, into.T)
    totals[0, 2:] = gains[...]
    totals[0, :2] = jnp.zeros((2,) + totals.shape[2:], FULL)

    @pl.loop(0, DILATION_STEP)
    def _(step):
        at = pl.ds(pl.multiple_of(step * chosen, chosen), chosen)
        groups = [wide[group, at, :] for group in range(width // LANES)]
        here = jnp.concatenate(groups, axis=1)
        normal = norm_one[at]
        totals[0, 0] += fold_rows(here * normal)
        totals[0, 1] += fold_rows(here)
        scaled = here * gain_one[...]
        part = scaled - row_mean(scaled) - normal * row_mean(scaled * normal)
        resid[at] += spread_one[at][:, :1] * part

    pieces[2].finish(0)
    pieces[2].start(1)
    norm.start(0)

    @pl.loop(0, DILATION_STEP)
    def _(step):
        at = pl.ds(pl.multiple_of(step * chosen, chosen), chosen)
        strided_store(wide, step, chosen, resid[at])

    for group in range(width // LANES):
        tokens_out[:, group * LANES : (group + 1) * LANES] = wide[group].astype(LOW)
    turn(7)
    turn(8)
    norm.finish(0)
    for step in range(1, 6):
        if step < 5:
            norm.start(step)
        pieces[2].finish(step)
        pieces[2].start(step + 1)
        if step < 5:
            norm.finish(step)
    pieces[2].finish(LAST)
    finish_piece(2)
    norm_out[...] = totals[5]
    loads_out[-1].wait()


def backward_pass(count, held, gain_one, qkv_weight):
    rows, width = held["resid"].shape
    chosen = rows // DILATION_STEP
    distant = count * chosen
    owned = width // count
    vm = pltpu.VMEM

    def like(name):
        return vm(held[name].shape, held[name].dtype)

    names = (
        "query", "key", "value", "far_key", "far_value", "weights", "far_weights",
        "scale", "far_scale", "delta", "slope", "normed", "norm_one", "spread_one", "resid",
        "down", "up", "out", "gains",
    )
    near = ("scale", "far_scale", "delta", "gains")
    held = dict(held, down=held["down"].reshape(count, 4, owned, width))
    scratch = [
        like(name)
        for name in (
            "query", "key", "value", "far_key", "far_value", "weights", "far_weights", "slope",
            "normed", "norm_one", "spread_one", "resid",
        )
    ]
    scratch += [
        vm(qkv_weight.shape, LOW),
        vm((HEADS, HEAD_WIDTH, LANES), FULL),
        vm((count, chosen, 2 * width), LOW),
        vm((count - 1, chosen, 2 * width), LOW),
        vm((2, HEADS, HEAD_WIDTH, LANES), FULL),
        vm((3, HEADS, HEAD_WIDTH, rows), LOW),
        vm((2, HEADS, HEAD_WIDTH, distant), LOW),
        vm((width // LANES, rows, LANES), FULL),
        vm((2, count, 2, owned, width), LOW),
        vm((2, count, 2, owned, width), LOW),
        vm((2, 16, owned, width), LOW),
        vm((3, 15, owned, width), LOW),
        vm((3, 4, owned, width), LOW),
        vm((4, owned, width), FULL),
        vm((6, 4, 8, width), FULL),
        vm((5, 4, 8, width), FULL),
        pltpu.SemaphoreType.DMA((20,)),
        pltpu.SemaphoreType.DMA((3,)),
        pltpu.SemaphoreType.DMA((3, 7)),
        pltpu.SemaphoreType.DMA((3, 7)),
        pltpu.SemaphoreType.DMA((5,)),
        pltpu.SemaphoreType.DMA((5,)),
        pltpu.SemaphoreType.DMA((count - 1,)),
        pltpu.SemaphoreType.DMA((count - 1,)),
    ]
    return pl.pallas_call(
        functools.partial(backward_kernel, count, names),
        out_shape=(
            jax.ShapeDtypeStruct((rows, width), LOW),
            jax.ShapeDtypeStruct((3, 4, owned, width), FULL),
            jax.ShapeDtypeStruct((4, 8, width), FULL),
        ),
        in_specs=[VMEM if name in near else ANY for name in names] + [VMEM, ANY],
        out_specs=(VMEM, ANY, VMEM),
        scratch_shapes=scratch,
        compiler_params=pltpu.CompilerParams(
            collective_id=2, has_side_effects=True, vmem_limit_bytes=63 << 20
        ),
        name="backward_pass",
    )(*[held[name] for name in names], gain_one, qkv_weight)


def fused_device(
    tokens,
    qkv_weight,
    out_weight,
    up_weight,
    down_weight,
    norm1_gain,
    norm1_bias,
    norm2_gain,
    norm2_bias,
    visible,
    cotangent,
):
    count = lax.axis_size("seq")
    width = tokens.shape[2]
    norms = [norm[None] for norm in (norm1_gain, norm1_bias, norm2_gain, norm2_bias)]
    held = forward_pass(
        count, tokens[0], cotangent[0], qkv_weight, out_weight, up_weight, down_weight, norms, visible
    )
    mixed = held.pop("mixed")
    tokens_grad, sums, norm_sums = backward_pass(count, held, norms[0], qkv_weight)
    rows = width // count
    norm_grads = jnp.sum(norm_sums, axis=1)

    def wide_again(blocks):
        return blocks.transpose(1, 0, 2).reshape(rows, -1)

    return (
        mixed[None],
        tokens_grad[None],
        wide_again(sums[2, :3]),
        sums[2, 3],
        wide_again(sums[1]),
        sums[0].reshape(-1, width),
        norm_grads[0],
        norm_grads[1],
        norm_grads[2],
        norm_grads[3],
    )


def solution(mesh):
    placed = (
        P("slide", "seq", None),
        P(),
        P(),
        P(),
        P(),
        P(),
        P(),
        P(),
        P(),
        P("slide"),
        P("slide", "seq", None),
    )
    fused = mesh.shape["seq"] == 8 and mesh.shape["slide"] == 4
    return jax.shard_map(
        fused_device if fused else plain_device,
        mesh=mesh,
        in_specs=placed,
        out_specs=(
            P("slide", "seq", None),
            P("slide", "seq", None),
            P("seq", None),
            P("seq", None),
            P("seq", None),
            P("seq", None),
            P(),
            P(),
            P(),
            P(),
        ),
        check_vma=False,
    )
```

```python
import functools

import jax
import jax.numpy as jnp
from jax import lax
from jax.experimental import pallas as pl
from jax.experimental.pallas import tpu as pltpu
from jax.sharding import PartitionSpec as P

HEADS = 16
HEAD_WIDTH = 48
SEG = 512
QB = 512
DILATION_STEP = 16


epsilon = 1e-05


def layer_norm(values, norm_gain, norm_shift):
    average = jnp.mean(values, axis=-1, keepdims=True)
    centered = values - average
    variance = jnp.mean(centered * centered, axis=-1, keepdims=True)
    return centered * lax.rsqrt(variance + epsilon) * norm_gain + norm_shift


def exact_gelu(values):
    return jax.nn.gelu(values, approximate=False)


def block_scores(query_block, seg_keys, seg_valid, distant_keys, distant_valid):
    nearby_scores = jnp.einsum(
        "iyo,uyo->yiu", query_block, seg_keys, preferred_element_type=jnp.float32
    )
    nearby_scores = jnp.where(seg_valid[None, None, :], nearby_scores, -1000000000.0)
    far_scores = jnp.einsum(
        "iyo,uyo->yiu",
        query_block[::DILATION_STEP],
        distant_keys,
        preferred_element_type=jnp.float32,
    )
    far_scores = jnp.where(distant_valid[None, None, :], far_scores, -1000000000.0)
    return (nearby_scores, far_scores)


def block_forward(
    query_block, seg_keys, seg_values, seg_valid, distant_keys, distant_values, distant_valid
):
    nearby_scores, far_scores = block_scores(
        query_block, seg_keys, seg_valid, distant_keys, distant_valid
    )
    head_number = nearby_scores.shape[0]
    row_number = nearby_scores.shape[1]
    chosen_count = row_number // DILATION_STEP
    maximum_table = jnp.max(nearby_scores, axis=-1).reshape(
        head_number, chosen_count, DILATION_STEP
    )
    combined_top = jnp.maximum(maximum_table[:, :, 0], jnp.max(far_scores, axis=-1))
    row_maximum = maximum_table.at[:, :, 0].set(combined_top).reshape(head_number, row_number)
    nearby_exponent = jnp.exp(nearby_scores - row_maximum[:, :, None])
    far_exp = jnp.exp(far_scores - combined_top[:, :, None])
    exponent_sums = jnp.sum(nearby_exponent, axis=-1).reshape(
        head_number, chosen_count, DILATION_STEP
    )
    combined_total = exponent_sums[:, :, 0] + jnp.sum(far_exp, axis=-1)
    row_sum_total = exponent_sums.at[:, :, 0].set(combined_total).reshape(head_number, row_number)
    local_weights = (nearby_exponent / row_sum_total[:, :, None]).astype(jnp.bfloat16)
    far_weights = (far_exp / combined_total[:, :, None]).astype(jnp.bfloat16)
    attended_rows = jnp.einsum(
        "hqk,khd->qhd", local_weights, seg_values, preferred_element_type=jnp.float32
    )
    distant_attended = jnp.einsum(
        "hqk,khd->qhd", far_weights, distant_values, preferred_element_type=jnp.float32
    )
    attended_rows = (
        attended_rows.reshape(chosen_count, DILATION_STEP, head_number, HEAD_WIDTH)
        .at[:, 0]
        .add(distant_attended)
    )
    return (attended_rows.reshape(row_number, head_number, HEAD_WIDTH), row_maximum, row_sum_total)


def block_backward(
    query_block,
    seg_keys,
    seg_values,
    seg_valid,
    distant_keys,
    distant_values,
    distant_valid,
    gradient_block,
    row_maximum,
    row_sum_total,
):
    nearby_scores, far_scores = block_scores(
        query_block, seg_keys, seg_valid, distant_keys, distant_valid
    )
    head_number = row_maximum.shape[0]
    row_number = row_maximum.shape[1]
    chosen_count = row_number // DILATION_STEP
    combined_top = row_maximum.reshape(head_number, chosen_count, DILATION_STEP)[:, :, 0]
    combined_total = row_sum_total.reshape(head_number, chosen_count, DILATION_STEP)[:, :, 0]
    nearby_probability = (
        jnp.exp(nearby_scores - row_maximum[:, :, None]) / row_sum_total[:, :, None]
    )
    far_prob = jnp.exp(far_scores - combined_top[:, :, None]) / combined_total[:, :, None]
    local_weights = nearby_probability.astype(jnp.bfloat16)
    gradient_sampled = gradient_block[::DILATION_STEP]
    value_grad = jnp.einsum(
        "mns,nmg->smg", local_weights, gradient_block, preferred_element_type=jnp.float32
    )
    nearby_dots = jnp.einsum(
        "iyo,uyo->yiu", gradient_block, seg_values, preferred_element_type=jnp.float32
    )
    far_dots = jnp.einsum(
        "iyo,uyo->yiu", gradient_sampled, distant_values, preferred_element_type=jnp.float32
    )
    delta_table = jnp.sum(nearby_probability * nearby_dots, axis=-1).reshape(
        head_number, chosen_count, DILATION_STEP
    )
    joint_delta = delta_table[:, :, 0] + jnp.sum(far_prob * far_dots, axis=-1)
    row_delta = delta_table.at[:, :, 0].set(joint_delta).reshape(head_number, row_number)
    local_slope = (nearby_probability * (nearby_dots - row_delta[:, :, None])).astype(jnp.bfloat16)
    distant_slope = (far_prob * (far_dots - joint_delta[:, :, None])).astype(jnp.bfloat16)
    query_gradient = jnp.einsum(
        "hqk,khd->qhd", local_slope, seg_keys, preferred_element_type=jnp.float32
    )
    distant_query = jnp.einsum(
        "hqk,khd->qhd", distant_slope, distant_keys, preferred_element_type=jnp.float32
    )
    query_gradient = (
        query_gradient.reshape(chosen_count, DILATION_STEP, head_number, HEAD_WIDTH)
        .at[:, 0]
        .add(distant_query)
    )
    key_grad = jnp.einsum(
        "mns,nmg->smg", local_slope, query_block, preferred_element_type=jnp.float32
    )
    far_weights = far_prob.astype(jnp.bfloat16)
    far_value_grad = jnp.einsum(
        "mns,nmg->smg", far_weights, gradient_sampled, preferred_element_type=jnp.float32
    )
    far_key_grad = jnp.einsum(
        "mns,nmg->smg",
        distant_slope,
        query_block[::DILATION_STEP],
        preferred_element_type=jnp.float32,
    )
    return (
        query_gradient.reshape(row_number, head_number, HEAD_WIDTH),
        key_grad,
        value_grad,
        far_key_grad,
        far_value_grad,
    )


def plain_device(
    tokens,
    qkv_weight,
    out_weight,
    up_weight,
    down_weight,
    norm1_gain,
    norm1_bias,
    norm2_gain,
    norm2_bias,
    visible,
    cotangent,
):
    row_number = tokens.shape[1]
    embedding_width = tokens.shape[2]
    query_scale = HEAD_WIDTH ** (-0.5)
    first_row = lax.axis_index("seq") * row_number
    positions = first_row + jnp.arange(row_number, dtype=jnp.int32)
    row_validity = positions < visible[0]
    inputs = tokens[0].astype(jnp.float32)
    norm_one, pull_one = jax.vjp(layer_norm, inputs, norm1_gain, norm1_bias)
    normed = norm_one.astype(jnp.bfloat16)
    projected = jnp.dot(normed, qkv_weight, preferred_element_type=jnp.float32)
    query_rows = (
        (projected[:, :embedding_width] * query_scale)
        .astype(jnp.bfloat16)
        .reshape(row_number, HEADS, HEAD_WIDTH)
    )
    flat_keys = projected[:, embedding_width : 2 * embedding_width].astype(jnp.bfloat16)
    flat_values = projected[:, 2 * embedding_width :].astype(jnp.bfloat16)
    key_matrix = flat_keys.reshape(row_number, HEADS, HEAD_WIDTH)
    value_matrix = flat_values.reshape(row_number, HEADS, HEAD_WIDTH)
    gathered_keys, gathered_values = (
        lax.all_gather(flat_keys[::DILATION_STEP], "seq", axis=0, tiled=True),
        lax.all_gather(flat_values[::DILATION_STEP], "seq", axis=0, tiled=True),
    )
    distant_count = gathered_keys.shape[0]
    distant_valid = jnp.arange(distant_count, dtype=jnp.int32) * DILATION_STEP < visible[0]
    distant_keys = gathered_keys.reshape(distant_count, HEADS, HEAD_WIDTH)
    distant_values = gathered_values.reshape(distant_count, HEADS, HEAD_WIDTH)
    per_segment = SEG // QB
    attended_rows, row_maximum, row_sum_total = block_forward(
        query_rows,
        key_matrix,
        value_matrix,
        row_validity,
        distant_keys,
        distant_values,
        distant_valid,
    )
    attn_low = attended_rows.reshape(row_number, embedding_width).astype(jnp.bfloat16)
    after_attn = inputs + jnp.dot(attn_low, out_weight, preferred_element_type=jnp.float32)
    norm_two, pull_two = jax.vjp(layer_norm, after_attn, norm2_gain, norm2_bias)
    normed_two = norm_two.astype(jnp.bfloat16)
    up_cols = jnp.dot(normed_two, up_weight, preferred_element_type=jnp.float32)
    activated, pull_gelu = jax.vjp(exact_gelu, up_cols)
    hidden = activated.astype(jnp.bfloat16)
    result = after_attn + jnp.dot(hidden, down_weight, preferred_element_type=jnp.float32)
    mixed_out = jnp.where(row_validity[:, None], result, 0.0).astype(jnp.bfloat16)[None]
    grad_out = jnp.where(row_validity[:, None], cotangent[0], jnp.zeros_like(cotangent[0]))
    down_grad = jnp.einsum("tf,td->fd", hidden, grad_out, preferred_element_type=jnp.float32)
    hidden_grad = jnp.einsum("td,fd->tf", grad_out, down_weight, preferred_element_type=jnp.float32)
    (up_slope,) = pull_gelu(hidden_grad)
    up_low = up_slope.astype(jnp.bfloat16)
    up_grad = jnp.einsum("td,tf->df", normed_two, up_low, preferred_element_type=jnp.float32)
    norm_two_in = jnp.einsum("tf,df->td", up_low, up_weight, preferred_element_type=jnp.float32)
    after_part, gain_two_grad, shift_two_grad = pull_two(norm_two_in)
    resid_grad = grad_out.astype(jnp.float32) + after_part
    resid_low = resid_grad.astype(jnp.bfloat16)
    out_grad = jnp.einsum("td,te->de", attn_low, resid_low, preferred_element_type=jnp.float32)
    attn_grad = jnp.einsum("te,de->td", resid_low, out_weight, preferred_element_type=jnp.float32)
    attn_grad = attn_grad.astype(jnp.bfloat16).reshape(row_number, HEADS, HEAD_WIDTH)
    query_gradient, key_grad, value_grad, far_key_grad, far_value_grad = block_backward(
        query_rows,
        key_matrix,
        value_matrix,
        row_validity,
        distant_keys,
        distant_values,
        distant_valid,
        attn_grad,
        row_maximum,
        row_sum_total,
    )
    key_list = [key_grad]
    value_list = [value_grad]
    owned_keys, owned_values = (
        lax.psum_scatter(
            far_key_grad.reshape(distant_count, embedding_width),
            "seq",
            scatter_dimension=0,
            tiled=True,
        ),
        lax.psum_scatter(
            far_value_grad.reshape(distant_count, embedding_width),
            "seq",
            scatter_dimension=0,
            tiled=True,
        ),
    )
    chosen_count = row_number // DILATION_STEP
    segment_count = row_number // SEG
    nearby_keys = jnp.sum(
        jnp.stack(key_list).reshape(segment_count, per_segment, SEG, embedding_width), axis=1
    )
    nearby_values = jnp.sum(
        jnp.stack(value_list).reshape(segment_count, per_segment, SEG, embedding_width), axis=1
    )
    key_total = (
        nearby_keys.reshape(chosen_count, DILATION_STEP, embedding_width)
        .at[:, 0]
        .add(owned_keys)
        .reshape(row_number, embedding_width)
    )
    value_total = (
        nearby_values.reshape(chosen_count, DILATION_STEP, embedding_width)
        .at[:, 0]
        .add(owned_values)
        .reshape(row_number, embedding_width)
    )
    query_total = query_gradient.reshape(row_number, embedding_width)
    mixed_grad = jnp.concatenate(
        [
            (query_total * query_scale).astype(jnp.bfloat16),
            key_total.astype(jnp.bfloat16),
            value_total.astype(jnp.bfloat16),
        ],
        axis=1,
    )
    qkv_grad = jnp.einsum("td,tf->df", normed, mixed_grad, preferred_element_type=jnp.float32)
    norm_one_in = jnp.einsum(
        "tf,df->td", mixed_grad, qkv_weight, preferred_element_type=jnp.float32
    )
    input_part, gain_one_grad, shift_one_grad = pull_one(norm_one_in)
    tokens_grad = (resid_grad + input_part).astype(jnp.bfloat16)[None]
    weight_grads = (qkv_grad, out_grad, up_grad, down_grad)
    row_parts = (
        lax.psum_scatter(weight_grads[0], "seq", scatter_dimension=0, tiled=True),
        lax.psum_scatter(weight_grads[1], "seq", scatter_dimension=0, tiled=True),
        lax.psum_scatter(weight_grads[2], "seq", scatter_dimension=0, tiled=True),
        lax.psum_scatter(weight_grads[3], "seq", scatter_dimension=0, tiled=True),
    )
    final_grads = (
        lax.psum(row_parts[0].astype(jnp.bfloat16), "slide").astype(jnp.float32),
        lax.psum(row_parts[1].astype(jnp.bfloat16), "slide").astype(jnp.float32),
        lax.psum(row_parts[2].astype(jnp.bfloat16), "slide").astype(jnp.float32),
        lax.psum(row_parts[3].astype(jnp.bfloat16), "slide").astype(jnp.float32),
    )
    norm_grads = lax.psum(
        (gain_one_grad, shift_one_grad, gain_two_grad, shift_two_grad), ("seq", "slide")
    )
    return (
        mixed_out,
        tokens_grad,
        final_grads[0],
        final_grads[1],
        final_grads[2],
        final_grads[3],
        norm_grads[0],
        norm_grads[1],
        norm_grads[2],
        norm_grads[3],
    )


MESH = pl.DeviceIdType.MESH
LOW = jnp.bfloat16
FULL = jnp.float32
AUG = 64
LANES = 128
NEVER = -1000000000.0
ANY = pl.BlockSpec(memory_space=pl.ANY)
VMEM = pl.BlockSpec(memory_space=pltpu.VMEM)
SMEM = pl.BlockSpec(memory_space=pltpu.SMEM)


def nn(left, right):
    return jnp.dot(left, right, preferred_element_type=FULL)


def nt(left, right):
    return lax.dot_general(left, right, (((1,), (1,)), ((), ())), preferred_element_type=FULL)


def tn(left, right):
    return lax.dot_general(left, right, (((0,), (0,)), ((), ())), preferred_element_type=FULL)


def remote(src, dst, send_sem, recv_sem, device):
    return pltpu.make_async_remote_copy(
        src_ref=src,
        dst_ref=dst,
        send_sem=send_sem,
        recv_sem=recv_sem,
        device_id=device,
        device_id_type=MESH,
    )


def greet(devices):
    barrier = pltpu.get_barrier_semaphore()
    for device in devices:
        pl.semaphore_signal(barrier, inc=1, device_id=device, device_id_type=MESH)
    pl.semaphore_wait(barrier, len(devices))


def row_peers(count):
    seq, slide = lax.axis_index("seq"), lax.axis_index("slide")
    return [(lax.rem(seq + step, count), slide) for step in range(1, count)]


def spread(ref, values):
    for group in range(ref.shape[0]):
        ref[group] = values[:, group * LANES : (group + 1) * LANES]


def strided_rows(ref, step, count):
    groups = [
        ref[group, pl.ds(step, count, stride=DILATION_STEP), :] for group in range(ref.shape[0])
    ]
    return jnp.concatenate(groups, axis=1)


def strided_store(ref, step, count, values):
    for group in range(ref.shape[0]):
        ref[group, pl.ds(step, count, stride=DILATION_STEP), :] = values[
            :, group * LANES : (group + 1) * LANES
        ]


def chunk(step, size):
    return pl.ds(pl.multiple_of(step * size, size), size)


def steps(body):
    @pl.loop(0, DILATION_STEP // 4)
    def _(group):
        for member in range(4):
            body(group * 4 + member)


def row_mean(values):
    return jnp.mean(values, axis=-1, keepdims=True)


def fold_rows(values):
    return jnp.sum(values.reshape(-1, 8, values.shape[-1]), axis=0)


def mask_rows(ref, bias):
    first = lax.broadcasted_iota(jnp.int32, (AUG - HEAD_WIDTH, ref.shape[2]), 0) == 0
    ref[:, HEAD_WIDTH:, :] = jnp.broadcast_to(
        jnp.where(first, bias, 0.0).astype(LOW), (HEADS, AUG - HEAD_WIDTH, ref.shape[2])
    )


def attend_kernel(
    count, tokens, qkv_weight, out_weight, gain_one, shift_one, visible,
    after_out, far_key_out, far_value_out, query_out, key_out, value_out, weights_out,
    far_weights_out, scale_out, far_scale_out, normed_out, far_normed_out, norm_out, spread_out, attn_out,
    wide, held_n1, held_r1, h1, h1_t, far_h1_t, wqkv, wo, query, key, value, all_far,
    far_key, far_value, top, total, attended, weights, far_weights, scale, far_scale, attn_t,
    after, load_sem, store_sem, send_sem, recv_sem,
):
    seq, slide = lax.axis_index("seq"), lax.axis_index("slide")
    rows, width = tokens.shape
    chosen = rows // DILATION_STEP
    loads = [
        pltpu.make_async_copy(
            qkv_weight.at[:, pl.ds(part * width, width)],
            wqkv.at[part],
            load_sem.at[part],
        )
        for part in range(3)
    ]
    loads.append(pltpu.make_async_copy(out_weight, wo, load_sem.at[3]))
    for n in (1, 2, 0, 3):
        loads[n].start()
    stores = []

    def store(source, target):
        copy = pltpu.make_async_copy(source, target, store_sem.at[len(stores)])
        copy.start()
        stores.append(copy)

    peers = row_peers(count)
    barrier = pltpu.get_barrier_semaphore()
    for peer in peers:
        pl.semaphore_signal(barrier, inc=1, device_id=peer, device_id_type=MESH)
    first_row = seq * rows
    limit = visible[0]
    spread(wide, tokens[...].astype(FULL))

    def normalize(step):
        at = chunk(step, chosen)
        values = strided_rows(wide, step, chosen)
        centered = values - row_mean(values)
        inverse = lax.rsqrt(row_mean(centered * centered) + epsilon)
        normal = centered * inverse
        after[at] = values
        held_n1[at] = normal
        held_r1[at] = jnp.broadcast_to(inverse, (chosen, LANES))
        low = (normal * gain_one[...][None] + shift_one[...][None]).astype(LOW)
        h1[at] = low
        return low

    all_far[seq] = normalize(0)
    pl.semaphore_wait(barrier, len(peers))
    for n, peer in enumerate(peers):
        mine = all_far.at[seq]
        remote(mine, mine, send_sem.at[n], recv_sem.at[n], peer).start()

    @pl.loop(0, 5)
    def _(group):
        for member in range(3):
            normalize(group * 3 + member + 1)

    store(held_n1, norm_out)
    store(held_r1, spread_out)
    for part, ref in ((1, key), (2, value)):
        loads[part].wait()
        projected = nn(h1[...], wqkv[part]).astype(LOW)
        ref[:, :HEAD_WIDTH, :] = projected.T.reshape(HEADS, HEAD_WIDTH, rows)
    loads[0].wait()
    projected = (nn(h1[...], wqkv[0]) * HEAD_WIDTH ** (-0.5)).astype(LOW)
    query[:, :HEAD_WIDTH, :] = projected.T.reshape(HEADS, HEAD_WIDTH, rows)
    places = lax.broadcasted_iota(jnp.int32, (1, rows), 1)
    places = first_row + (places % chosen) * DILATION_STEP + places // chosen
    mask_rows(key, jnp.where(places < limit, 0.0, NEVER))
    mask_rows(query, jnp.ones((1, rows), FULL))
    h1_t[...] = h1[...].T
    store(h1_t, normed_out)
    store(query.at[:, pl.ds(0, HEAD_WIDTH)], query_out)
    store(key.at[:, pl.ds(0, HEAD_WIDTH)], key_out)
    store(value, value_out)

    @pl.loop(0, HEADS // 4)
    def _(group):
        for member in range(4):
            head = group * 4 + member
            scores = tn(key[head], query[head])
            highest = jnp.max(scores, axis=0, keepdims=True)
            exponent = jnp.exp(scores - highest)
            top[head] = highest
            total[head] = jnp.sum(exponent, axis=0, keepdims=True)
            low = exponent.astype(LOW)
            weights[head] = low
            attended[head] = nn(value[head], low)

    store(weights, weights_out)
    for n in range(count - 1):
        source = lax.rem(seq + count - 1 - n, count)
        wait = remote(all_far.at[seq], all_far.at[source], send_sem.at[n], recv_sem.at[n], peers[0])
        wait.wait_recv()
        wait.wait_send()
    distant = count * chosen
    flat = all_far[...].reshape(distant, width)
    for part, ref in ((1, far_key), (2, far_value)):
        projected = nn(flat, wqkv[part]).astype(LOW)
        ref[:, :HEAD_WIDTH, :] = projected.T.reshape(HEADS, HEAD_WIDTH, distant)
    far_h1_t[...] = flat.T
    store(far_h1_t, far_normed_out)
    places = lax.broadcasted_iota(jnp.int32, (1, distant), 1) * DILATION_STEP
    mask_rows(far_key, jnp.where(places < limit, 0.0, NEVER))
    store(far_key.at[:, pl.ds(0, HEAD_WIDTH)], far_key_out)
    store(far_value, far_value_out)
    lane_mask = jnp.where(lax.broadcasted_iota(jnp.int32, (1, LANES), 1) < chosen, 0.0, NEVER)

    @pl.loop(0, HEADS // 4)
    def _(group):
        for member in range(4):
            head = group * 4 + member
            scores = tn(far_key[head], query[head][:, :LANES]) + lane_mask
            highest = jnp.max(scores, axis=0, keepdims=True)
            exponent = jnp.exp(scores - highest)
            low = exponent.astype(LOW)
            far_weights[head] = low
            near = top[head][:, :LANES]
            joint = jnp.maximum(near, highest)
            near_part, far_part = jnp.exp(near - joint), jnp.exp(highest - joint)
            joint_total = total[head][:, :LANES] * near_part + far_part * jnp.sum(
                exponent, axis=0, keepdims=True
            )
            near_part, far_part = near_part / joint_total, far_part / joint_total
            far_scale[head] = far_part
            local = jnp.concatenate([near_part, 1.0 / total[head][:, LANES:]], axis=1)
            scale[head] = local
            result = attended[head] * local
            with_far = result[:, :LANES] + nn(far_value[head], low) * far_part
            result = jnp.concatenate([with_far, result[:, LANES:]], axis=1)
            attn_t[head] = result.astype(LOW)

    store(far_weights, far_weights_out)
    store(scale, scale_out)
    store(far_scale, far_scale_out)
    store(attn_t, attn_out)
    loads[3].wait()
    after[...] += nn(attn_t[...].reshape(width, rows).T, wo[...])
    store(after, after_out)
    for copy in stores:
        copy.wait()


def attend_pass(count, tokens, qkv_weight, out_weight, norms, visible):
    rows, width = tokens.shape
    chosen = rows // DILATION_STEP
    distant = count * chosen

    def low(*shape):
        return jax.ShapeDtypeStruct(shape, LOW)

    def full(*shape):
        return jax.ShapeDtypeStruct(shape, FULL)

    outs = {
        "after": full(rows, width),
        "far_key": low(HEADS, HEAD_WIDTH, distant),
        "far_value": low(HEADS, HEAD_WIDTH, distant),
        "query": low(HEADS, HEAD_WIDTH, rows),
        "key": low(HEADS, HEAD_WIDTH, rows),
        "value": low(HEADS, HEAD_WIDTH, rows),
        "weights": low(HEADS, rows, rows),
        "far_weights": low(HEADS, distant, LANES),
        "scale": full(HEADS, 1, rows),
        "far_scale": full(HEADS, 1, LANES),
        "normed": low(width, rows),
        "far_normed": low(width, distant),
        "norm_one": full(rows, width),
        "spread_one": full(rows, LANES),
        "attn": low(HEADS, HEAD_WIDTH, rows),
    }
    vm = pltpu.VMEM

    def like(name):
        return vm(outs[name].shape, outs[name].dtype)

    scratch = [
        vm((width // LANES, rows, LANES), FULL),
        like("norm_one"),
        like("spread_one"),
        vm((rows, width), LOW),
        like("normed"),
        like("far_normed"),
        vm((3, width, width), LOW),
        vm(out_weight.shape, LOW),
        vm((HEADS, AUG, rows), LOW),
        vm((HEADS, AUG, rows), LOW),
        like("value"),
        vm((count, chosen, width), LOW),
        vm((HEADS, AUG, distant), LOW),
        like("far_value"),
        vm((HEADS, 1, rows), FULL),
        vm((HEADS, 1, rows), FULL),
        vm((HEADS, HEAD_WIDTH, rows), FULL),
        like("weights"),
        like("far_weights"),
        like("scale"),
        like("far_scale"),
        like("attn"),
        like("after"),
        pltpu.SemaphoreType.DMA((4,)),
        pltpu.SemaphoreType.DMA((len(outs),)),
        pltpu.SemaphoreType.DMA((count - 1,)),
        pltpu.SemaphoreType.DMA((count - 1,)),
    ]
    results = pl.pallas_call(
        functools.partial(attend_kernel, count),
        out_shape=tuple(outs.values()),
        in_specs=[VMEM, ANY, ANY, VMEM, VMEM, SMEM],
        out_specs=tuple(ANY for _ in outs),
        scratch_shapes=scratch,
        compiler_params=pltpu.CompilerParams(
            collective_id=1, has_side_effects=True, vmem_limit_bytes=60 << 20
        ),
        name="attend_pass",
    )(tokens, qkv_weight, out_weight, *norms, visible)
    return dict(zip(outs, results))


class Place:
    def __init__(self):
        seq, slide = lax.axis_index("seq"), lax.axis_index("slide")
        self.seq, self.slide = seq, slide
        self.z, self.x = seq // 2, seq % 2
        self.y, self.c = slide // 2, slide % 2
        self.sibling = (seq, slide + 1 - 2 * self.c)
        self.across_y = (seq, slide + 2 - 4 * self.y)
        self.diagonal = (seq, 3 - slide)
        self.across_x = (seq + 1 - 2 * self.x, slide)
        self.slide_peers = (self.sibling, self.across_y, self.diagonal)

    def layer(self, step):
        return (self.z + step) % 4


class Part:
    spans = {1: ((0, 8), (0, 8)), 2: ((8, 4), (8, 6)), 3: ((14, 3), (14, 1))}

    def __init__(self, place, both, core_got, got, final, send_sem, recv_sem):
        self.place, self.both, self.core_got, self.got, self.final = place, both, core_got, got, final
        self.send_sem, self.recv_sem = send_sem, recv_sem

    def transfers(self, core, phase):
        place, kept, got = self.place, self.both.at[0], self.got
        x, y = place.x, place.y
        if core == 0:
            if phase == 1:
                return [(kept.at[o, 1 - y], got.at[o], place.across_y) for o in range(8)]
            if phase == 2:
                return [
                    (kept.at[2 * z + 1 - x, y], got.at[8 + z], place.across_x) for z in range(4)
                ]
            return [
                (
                    kept.at[2 * place.layer(k) + x, y],
                    got.at[13 + k],
                    (2 * place.layer(k) + x, place.slide),
                )
                for k in (1, 2, 3)
            ]
        if phase == 1:
            return [
                (kept.at[2 * z + 1 - x], got.at[pl.ds(2 * z, 2)], place.across_x) for z in range(4)
            ]
        if phase == 2:
            return [
                (
                    kept.at[2 * place.layer(k) + x],
                    got.at[pl.ds(6 + 2 * k, 2)],
                    (2 * place.layer(k) + x, place.slide),
                )
                for k in (1, 2, 3)
            ]
        return [(kept.at[place.seq, 1 - y], got.at[14], place.across_y)]

    def start(self, phase, merged):
        place, send, recv = self.place, self.send_sem.at[phase], self.recv_sem.at[phase]
        if phase == 0:
            remote(self.both.at[1], self.core_got, send, recv, place.sibling).start()
        elif phase <= 3:
            for core in range(2):

                @pl.when(place.c == core)
                def _(core=core):
                    for source, target, device in self.transfers(core, phase):
                        remote(source, target, send, recv, device).start()
        elif phase == 4:
            own = self.final.at[place.c * 2 + place.y]
            for device in place.slide_peers if merged else (place.across_y,):
                remote(own, own, send, recv, device).start()
        else:
            own = self.final.at[pl.ds(place.c * 2, 2)]
            remote(own, own, send, recv, place.sibling).start()

    def wait(self, phase, whole):
        both_ways = remote(
            whole, whole, self.send_sem.at[phase], self.recv_sem.at[phase], self.place.sibling
        )
        both_ways.wait_recv()
        both_ways.wait_send()

    def finish(self, phase, merged):
        place, both, got = self.place, self.both, self.got
        x, y = place.x, place.y
        if phase == 0:
            self.wait(phase, self.core_got)

            @pl.loop(0, 8)
            def _(owner):
                for row in range(2):
                    self.add(owner, row, [self.core_got.at[owner, row]])
        elif phase <= 3:
            for core in range(2):

                @pl.when(place.c == core)
                def _(core=core):
                    first, number = self.spans[phase][core]
                    self.wait(phase, got.at[pl.ds(first, number)])
                    if phase == 1 and core == 0:
                        for owner in range(8):
                            self.add(owner, y, [got.at[owner]])
                    elif phase == 1:
                        for z in range(4):
                            for row in range(2):
                                self.add(2 * z + x, row, [got.at[2 * z + row]])
                    elif phase == 2 and core == 0:
                        for z in range(4):
                            self.add(2 * z + x, y, [got.at[8 + z]])
                    elif phase == 2:
                        for row in range(2):
                            self.add(place.seq, row, [got.at[8 + 2 * k + row] for k in range(3)])
                    else:
                        extra = [got.at[first + n] for n in range(number)]
                        self.add(place.seq, y, extra, self.final.at[core * 2 + y])
        elif phase == 4:
            self.wait(phase, self.final.at[pl.ds(0, 3 if merged else 1)])
        else:
            self.wait(phase, self.final.at[pl.ds(0, 2)])

    def add(self, owner, row, extra, target=None):
        total = self.both[0, owner, row].astype(FULL)
        for ref in extra:
            total = total + ref[...].astype(FULL)
        if target is None:
            self.both[0, owner, row] = total.astype(LOW)
        else:
            target[...] = total.astype(LOW)


class Piece:
    def __init__(self, parts, merged, outs, out_sem):
        self.parts, self.merged, self.outs, self.out_sem = parts, merged, outs, out_sem
        self.last = 4 if merged else 5
        self.phase = -1

    @property
    def done(self):
        return self.phase > self.last

    def advance(self):
        if self.done:
            return
        if self.phase >= 0:
            for part in self.parts:
                part.finish(self.phase, self.merged)
        self.phase += 1
        if not self.done:
            for part in self.parts:
                part.start(self.phase, self.merged)
            return
        for n in range(len(self.parts)):
            self.out_copy(n).start()

    def out_copy(self, n):
        return pltpu.make_async_copy(self.parts[n].final, self.outs[n], self.out_sem.at[n])


TILES = 3
PIECES = 5
HOOKS = {
    "tile1": (0,),
    "tile2": (1,),
    "after0": (2, 0),
    "after1": (),
    "far": (0,),
    "near0": (1,),
    "near1": (0,),
    "near2": (2, 1),
    "near3": (0,),
    "query": (0, 3),
    "into": (1, 2),
    "norm": (4,),
}


def main_kernel(
    count, names, cotangent, up_weight, down_weight, out_weight, qkv_weight,
    gain_one, gain_two, shift_two, visible, *refs
):
    held = dict(zip(names, refs))
    refs = refs[len(names) :]
    (
        mixed_out, tokens_out, down_sums, up_sums, last_sums, norm_out,
        normed, far_normed, query, key, value, far_key, far_value, far_weights, scale, far_scale, attn,
        delta, slope, resid, wo, wide, staged, far_got, sums, around, across,
        down_both, up_both, last_both, down_core, up_core, last_core,
        down_got, up_got, last_got, down_final, up_final, last_final,
        load_sem, tile_sem, store_sem, out_sem, send_sem, recv_sem,
        far_send_sem, far_recv_sem, norm_send_sem, norm_recv_sem,
    ) = refs
    place = Place()
    seq, core = place.seq, place.c
    rows, width = resid.shape
    chosen = rows // DILATION_STEP
    distant = count * chosen
    group_lanes = LANES
    tile_width = count * group_lanes
    first_row = seq * rows
    limit = visible[0]
    loads = []

    def load(source, target):
        loads.append((source, target))
        load_copy(len(loads) - 1).start()
        return len(loads) - 1

    def load_copy(n):
        return pltpu.make_async_copy(*loads[n], load_sem.at[n])

    peers = row_peers(count)
    others = list(place.slide_peers) + peers
    barrier = pltpu.get_barrier_semaphore()
    for other in others:
        pl.semaphore_signal(barrier, inc=1, device_id=other, device_id_type=MESH)

    def valid_rows(step):
        places = lax.broadcasted_iota(jnp.int32, (chosen, 1), 0) * DILATION_STEP + step
        return first_row + places < limit

    pieces = []
    for n in range(TILES):
        parts = [
            Part(
                place,
                both.at[n],
                core_got.at[n % 2],
                got.at[n],
                final.at[n],
                send_sem.at[n, which],
                recv_sem.at[n, which],
            )
            for which, (both, core_got, got, final) in enumerate(
                (
                    (down_both, down_core, down_got, down_final),
                    (up_both, up_core, up_got, up_final),
                )
            )
        ]
        pieces.append(Piece(parts, False, (down_sums.at[n], up_sums.at[n]), out_sem.at[n]))
    for n in range(2):
        part = Part(
            place,
            last_both.at[n],
            last_core.at[n],
            last_got.at[n],
            last_final.at[n],
            send_sem.at[TILES + n, 0],
            recv_sem.at[TILES + n, 0],
        )
        pieces.append(Piece([part], True, (last_sums.at[n],), out_sem.at[TILES + n]))

    def hook(name):
        for n in HOOKS.get(name, ()):
            if pieces[n].phase >= 0:
                pieces[n].advance()

    def split_last(n, side, grads):
        half = width // 2
        low = grads.astype(LOW).reshape(count, -1, width)
        for column in range(2):
            target = last_both.at[n, (side + core) % 2]
            target[:, column] = low[:, :, column * half : (column + 1) * half]

    def forward_part(after, norm_two, spread_two, h2, h2_t, dyb, active, low_slope, wup, wdown):
        load(cotangent, h2)
        load(held["after"], after)
        tile_loads = {}
        halves = 2
        per_half = tile_width // halves

        def load_tile(number):
            tile, half = divmod(number, halves)
            slot = number % 2
            for local in range(count // halves):
                owner = half * (count // halves) + local
                at = pl.ds(owner * TILES * group_lanes + tile * group_lanes, group_lanes)
                to = pl.ds(local * group_lanes, group_lanes)
                pltpu.make_async_copy(
                    up_weight.at[:, at], wup.at[slot, :, to], tile_sem.at[slot, 0]
                ).start()
                pltpu.make_async_copy(
                    down_weight.at[at], wdown.at[slot, to], tile_sem.at[slot, 1]
                ).start()

        def wait_tile(number):
            slot = number % 2
            pltpu.make_async_copy(wup.at[slot], wup.at[slot], tile_sem.at[slot, 0]).wait()
            pltpu.make_async_copy(wdown.at[slot], wdown.at[slot], tile_sem.at[slot, 1]).wait()

        load_tile(0)
        load_tile(1)
        load(held["attn"], attn)
        load(out_weight, wo)
        for name, ref in (
            ("far_value", far_value), ("far_key", far_key), ("far_weights", far_weights),
            ("query", query), ("scale", scale), ("far_scale", far_scale),
            ("value", value), ("key", key), ("normed", normed), ("far_normed", far_normed),
        ):
            load(held[name], ref)
        load_copy(0).wait()
        spread(wide, h2[...].astype(FULL))

        @steps
        def _(step):
            at = chunk(step, chosen)
            dyb[at] = jnp.where(valid_rows(step), strided_rows(wide, step, chosen), 0.0).astype(LOW)

        load_copy(1).wait()

        @steps
        def _(step):
            at = chunk(step, chosen)
            values = after[at]
            centered = values - row_mean(values)
            inverse = lax.rsqrt(row_mean(centered * centered) + epsilon)
            normal = centered * inverse
            norm_two[at] = normal
            spread_two[at] = jnp.broadcast_to(inverse, (chosen, LANES))
            h2[at] = (normal * gain_two[...][None] + shift_two[...][None]).astype(LOW)
            resid[at] = jnp.zeros((chosen, width), FULL)

        h2_t[...] = h2[...].T
        for tile in range(TILES):
            for half in range(halves):
                number = tile * halves + half
                slot = number % 2
                wait_tile(number)
                for part in range(2):
                    at = slice(part * per_half // 2, (part + 1) * per_half // 2)
                    to = slice(
                        half * per_half + part * per_half // 2,
                        half * per_half + (part + 1) * per_half // 2,
                    )
                    hidden = nn(h2[...], wup[slot, :, at])
                    hidden_slope = nt(dyb[...], wdown[slot, at])
                    share = 0.5 * (1.0 + lax.erf(hidden * 0.7071067811865476))
                    active[:, to] = (hidden * share).astype(LOW)
                    density = hidden * jnp.exp(-0.5 * hidden * hidden) * 0.3989422804014327
                    low_slope[:, to] = (hidden_slope * (share + density)).astype(LOW)
                to = slice(half * per_half, (half + 1) * per_half)
                after[...] += nn(active[:, to], wdown[slot])
                resid[...] += nt(low_slope[:, to], wup[slot])
                if number + 2 < TILES * halves:
                    load_tile(number + 2)
                if half == 0:
                    hook("tile%d" % tile)
            for part in range(4):
                at = slice(part * tile_width // 4, (part + 1) * tile_width // 4)
                grads = nn(h2_t[...], low_slope[:, at]).astype(LOW)
                side, row = divmod(part, 2)
                up_both.at[tile, (side + core) % 2][:, row] = grads.reshape(count, -1, grads.shape[1])
                grads = tn(active[:, at], dyb[...]).astype(LOW)
                owners = count // 4
                grads = grads.reshape(owners, 2, 2, -1, width)
                for side in range(2):
                    target = down_both.at[tile, (side + core) % 2]
                    target[part * owners : (part + 1) * owners] = grads[:, side]
            if tile == 0:
                pl.semaphore_wait(barrier, len(others))
            pieces[tile].advance()
        sums[...] = jnp.zeros_like(sums)
        hook("after0")

        @steps
        def _(step):
            at = chunk(step, chosen)
            strided_store(wide, step, chosen, jnp.where(valid_rows(step), after[at], 0.0))
            given, normal = resid[at], norm_two[at]
            sums[2] += fold_rows(given * normal)
            sums[3] += fold_rows(given)
            scaled = given * gain_two[...][None]
            part = scaled - row_mean(scaled) - normal * row_mean(scaled * normal)
            value_here = dyb[at].astype(FULL) + spread_two[at][:, :1] * part
            resid[at] = value_here
            h2[at] = value_here.astype(LOW)

        for group in range(width // LANES):
            staged[:, group * LANES : (group + 1) * LANES] = wide[group].astype(LOW)
        pltpu.make_async_copy(staged, mixed_out, store_sem.at[0]).start()
        load_copy(2).wait()
        load_copy(3).wait()
        split_last(0, 1, nn(attn[...].reshape(width, rows), h2[...]))
        slope[...] = nt(wo[...], h2[...]).astype(LOW).reshape(HEADS, HEAD_WIDTH, rows)

        @pl.loop(0, HEADS)
        def _(head):
            product = slope[head].astype(FULL) * attn[head].astype(FULL)
            delta[head] = jnp.sum(product, axis=0, keepdims=True)

        hook("after1")

    vm = pltpu.VMEM
    pl.run_scoped(
        forward_part,
        vm((rows, width), FULL),
        vm((rows, width), FULL),
        vm((rows, LANES), FULL),
        vm((rows, width), LOW),
        vm((width, rows), LOW),
        vm((rows, width), LOW),
        vm((rows, tile_width), LOW),
        vm((rows, tile_width), LOW),
        vm((2, width, tile_width // 2), LOW),
        vm((2, tile_width // 2, width), LOW),
    )

    def backward_part(
        weights, slopes, far_query, far_send, given, norm_one, spread_one, wqkv,
        group_sem,
    ):
        members = weights.shape[1]

        def load_group(group):
            source = held["weights"].at[pl.ds(group * members, members)]
            return pltpu.make_async_copy(source, weights.at[group % 2], group_sem.at[group % 2])

        load_group(0).start()
        load_group(1).start()
        for n in range(4, 14):
            load_copy(n).wait()
        late = [
            load(held["norm_one"], norm_one),
            load(held["spread_one"], spread_one),
            load(qkv_weight, wqkv),
        ]

        @pl.loop(0, HEADS // 4)
        def _(group):
            for member in range(4):
                head = group * 4 + member
                first_slope = slope[head][:, :LANES]
                low = far_weights[head]
                change = tn(far_value[head], first_slope) - delta[head][:, :LANES]
                score_slope = (low.astype(FULL) * far_scale[head] * change).astype(LOW)
                far_query[head] = nn(far_key[head], score_slope)
                scaled = (first_slope.astype(FULL) * far_scale[head]).astype(LOW)
                given[0, head] = nt(query[head][:, :LANES], score_slope).astype(LOW)
                given[1, head] = nt(scaled, low).astype(LOW)

        for n in late:
            load_copy(n).wait()

        def flat_given(part):
            return given[part].reshape(width, distant)

        into = nn(wqkv[:, width : 2 * width], flat_given(0))
        into += nn(wqkv[:, 2 * width :], flat_given(1))
        far_send[...] = into.T.astype(LOW).reshape(count, chosen, width)
        for n, peer in enumerate(peers):
            remote(
                far_send.at[peer[0]], far_got.at[n], far_send_sem.at[n], far_recv_sem.at[n], peer
            ).start()
        hook("far")
        for group in range(HEADS // members):
            load_group(group).wait()
            for member in range(members):
                head = group * members + member
                low = weights[group % 2, member]
                change = tn(value[head], slope[head]) - delta[head]
                score_slope = (low.astype(FULL) * scale[head] * change).astype(LOW)
                query_slope = nn(key[head], score_slope)
                key_slope = nt(query[head], score_slope)
                scaled = (slope[head].astype(FULL) * scale[head]).astype(LOW)
                value_slope = nt(scaled, low)
                first = query_slope[:, :LANES] + far_query[head]
                query_slope = jnp.concatenate([first, query_slope[:, LANES:]], axis=1)
                slopes[0, head] = (query_slope * HEAD_WIDTH ** (-0.5)).astype(LOW)
                slopes[1, head] = key_slope.astype(LOW)
                slopes[2, head] = value_slope.astype(LOW)
            if (group + 2) * members < HEADS:
                load_group(group + 2).start()
            hook("near%d" % group)

        def flat_slopes(part):
            return slopes[part].reshape(width, rows)

        split_last(0, 0, nt(normed[...], flat_slopes(0)))
        pieces[TILES].advance()
        hook("query")
        for part in (1, 2):
            grads = nt(normed[...], flat_slopes(part))
            split_last(1, part - 1, grads + nt(far_normed[...], flat_given(part - 1)))
        pieces[TILES + 1].advance()
        into = nn(wqkv[:, :width], flat_slopes(0))
        into += nn(wqkv[:, width : 2 * width], flat_slopes(1))
        into += nn(wqkv[:, 2 * width :], flat_slopes(2))
        pltpu.make_async_copy(staged, mixed_out, store_sem.at[0]).wait()
        spread(wide, into.T)
        hook("into")
        total = far_send[seq].astype(FULL)
        for n in range(count - 1):
            wait = remote(
                far_got.at[n], far_got.at[n], far_send_sem.at[n], far_recv_sem.at[n], peers[0]
            )
            wait.wait_recv()
            wait.wait_send()
            total = total + far_got[n].astype(FULL)
        for group in range(width // LANES):
            wide[group, :chosen] += total[:, group * LANES : (group + 1) * LANES]

        @steps
        def _(step):
            at = chunk(step, chosen)
            here = jnp.concatenate([wide[group, at, :] for group in range(width // LANES)], axis=1)
            normal = norm_one[at]
            sums[0] += fold_rows(here * normal)
            sums[1] += fold_rows(here)
            scaled = here * gain_one[...][None]
            part = scaled - row_mean(scaled) - normal * row_mean(scaled * normal)
            resid[at] += spread_one[at][:, :1] * part

    pl.run_scoped(
        backward_part,
        vm((2, 4, rows, rows), LOW),
        vm((3, HEADS, HEAD_WIDTH, rows), LOW),
        vm((HEADS, HEAD_WIDTH, LANES), FULL),
        vm((count, chosen, width), LOW),
        vm((2, HEADS, HEAD_WIDTH, distant), LOW),
        vm((rows, width), FULL),
        vm((rows, LANES), FULL),
        vm(qkv_weight.shape, LOW),
        pltpu.SemaphoreType.DMA((2,)),
    )
    for n in range(4):
        around[seq, pl.ds(n, 1)] = jnp.sum(sums[n], axis=0, keepdims=True)
    for n, peer in enumerate(peers):
        mine = around.at[seq]
        remote(mine, mine, norm_send_sem.at[n], norm_recv_sem.at[n], peer).start()
    hook("norm")

    @steps
    def _(step):
        strided_store(wide, step, chosen, resid[chunk(step, chosen)])

    for group in range(width // LANES):
        staged[:, group * LANES : (group + 1) * LANES] = wide[group].astype(LOW)
    tokens_copy = pltpu.make_async_copy(staged, tokens_out, store_sem.at[1])
    tokens_copy.start()
    for n in range(count - 1):
        mine = around.at[seq]
        wait = remote(mine, mine, norm_send_sem.at[n], norm_recv_sem.at[n], peers[0])
        wait.wait_recv()
        wait.wait_send()
    total = around[0]
    for n in range(1, count):
        total = total + around[n]
    across[place.slide] = total
    for n, peer in enumerate(place.slide_peers):
        mine, at = across.at[place.slide], count - 1 + n
        remote(mine, mine, norm_send_sem.at[at], norm_recv_sem.at[at], peer).start()
    turns = 0
    while not all(piece.done for piece in pieces):
        for piece in pieces:
            piece.advance()
        turns += 1
        if turns == 1:
            for n in range(3):
                mine, at = across.at[0], count - 1 + n
                wait = remote(mine, mine, norm_send_sem.at[at], norm_recv_sem.at[at], peers[0])
                wait.wait_recv()
                wait.wait_send()
            norm_out[...] = (across[0] + across[1]) + (across[2] + across[3])
    for piece in pieces:
        for n in range(len(piece.parts)):
            piece.out_copy(n).wait()
    tokens_copy.wait()


def main_pass(count, held, cotangent, weights, norms, visible):
    up_weight, down_weight, out_weight, qkv_weight = weights
    rows, width = cotangent.shape
    chosen = rows // DILATION_STEP
    owned = width // count
    vm = pltpu.VMEM

    def like(name):
        return vm(held[name].shape, held[name].dtype)

    names = tuple(held)
    down_block, up_block, last_block = (LANES // 4, width), (owned, 2 * LANES), (owned, width // 2)
    blocks = ((TILES, down_block), (TILES, up_block), (2, last_block))
    scratch = [
        like(name)
        for name in (
            "normed", "far_normed", "query", "key", "value", "far_key", "far_value", "far_weights", "scale",
            "far_scale", "attn", "scale", "query",
        )
    ]
    scratch += [
        vm((rows, width), FULL),
        vm(out_weight.shape, LOW),
        vm((width // LANES, rows, LANES), FULL),
        vm((rows, width), LOW),
        vm((count - 1, chosen, width), LOW),
        vm((4, 8, width), FULL),
        vm((count, 8, width), FULL),
        vm((4, 8, width), FULL),
    ]
    scratch += [vm((n, 2, count, 2) + block, LOW) for n, block in blocks]
    scratch += [vm((2, count, 2) + block, LOW) for n, block in blocks]
    scratch += [vm((n, 17) + block, LOW) for n, block in blocks]
    scratch += [vm((n, 4) + block, LOW) for n, block in blocks]
    dma = pltpu.SemaphoreType.DMA
    scratch += [
        dma((17,)), dma((2, 2)), dma((2,)), dma((PIECES, 2)), dma((PIECES, 2, 6)), dma((PIECES, 2, 6)),
        dma((count - 1,)), dma((count - 1,)), dma((count + 2,)), dma((count + 2,)),
    ]
    sums = [jax.ShapeDtypeStruct((n, 4) + block, LOW) for n, block in blocks]
    return pl.pallas_call(
        functools.partial(main_kernel, count, names),
        out_shape=(
            jax.ShapeDtypeStruct((rows, width), LOW),
            jax.ShapeDtypeStruct((rows, width), LOW),
            *sums,
            jax.ShapeDtypeStruct((8, width), FULL),
        ),
        in_specs=[ANY] * 5 + [VMEM] * 3 + [SMEM] + [ANY] * len(names),
        out_specs=(ANY, ANY, ANY, ANY, ANY, VMEM),
        scratch_shapes=scratch,
        compiler_params=pltpu.CompilerParams(
            collective_id=2, has_side_effects=True, vmem_limit_bytes=63 << 20
        ),
        name="main_pass",
    )(cotangent, up_weight, down_weight, out_weight, qkv_weight, *norms, visible, *held.values())


def finish_kernel(
    mixed, tokens_grad, down_sums, up_sums, last_sums, norms,
    mixed_out, tokens_out, qkv_out, out_out, up_out, down_out, *norm_outs
):
    mixed_out[...] = mixed[...]
    tokens_out[...] = tokens_grad[...]
    tiles, blocks, rows, _ = down_sums.shape
    for tile in range(tiles):
        for block in range(blocks):
            first = (tile * blocks + block) * rows
            down_out[first : first + rows] = down_sums[tile, block].astype(FULL)
            for half in range(2):
                first = ((block * 2 + half) * tiles + tile) * LANES
                part = up_sums[tile, block][:, half * LANES : (half + 1) * LANES]
                up_out[:, first : first + LANES] = part.astype(FULL)
    columns = last_sums.shape[-1]
    order = [(0, 0), (0, 1), (1, 0), (1, 1), (1, 2), (1, 3)]
    for n, (piece, block) in enumerate(order):
        qkv_out[:, n * columns : (n + 1) * columns] = last_sums[piece, block].astype(FULL)
    for n in range(2):
        out_out[:, n * columns : (n + 1) * columns] = last_sums[0, 2 + n].astype(FULL)
    for n, out in enumerate(norm_outs):
        out[...] = norms[n]


def finish_pass(count, results):
    rows, width = results[0].shape
    owned = width // count

    def full(*shape):
        return jax.ShapeDtypeStruct(shape, FULL)

    return pl.pallas_call(
        finish_kernel,
        out_shape=(
            jax.ShapeDtypeStruct((rows, width), LOW),
            jax.ShapeDtypeStruct((rows, width), LOW),
            full(owned, 3 * width),
            full(owned, width),
            full(owned, TILES * count * LANES),
            full(TILES * LANES, width),
            *[full(width)] * 4,
        ),
        in_specs=[VMEM] * 6,
        out_specs=tuple([VMEM] * 10),
        compiler_params=pltpu.CompilerParams(vmem_limit_bytes=63 << 20),
        name="finish_pass",
    )(*results)


def fused_device(
    tokens,
    qkv_weight,
    out_weight,
    up_weight,
    down_weight,
    norm1_gain,
    norm1_bias,
    norm2_gain,
    norm2_bias,
    visible,
    cotangent,
):
    count = lax.axis_size("seq")
    held = attend_pass(
        count, tokens[0], qkv_weight, out_weight, (norm1_gain, norm1_bias), visible
    )
    results = main_pass(
        count,
        held,
        cotangent[0],
        (up_weight, down_weight, out_weight, qkv_weight),
        (norm1_gain, norm2_gain, norm2_bias),
        visible,
    )
    mixed, tokens_grad, *grads = finish_pass(count, results)
    return (mixed[None], tokens_grad[None], *grads)


def solution(mesh):
    placed = (
        P("slide", "seq", None),
        P(),
        P(),
        P(),
        P(),
        P(),
        P(),
        P(),
        P(),
        P("slide"),
        P("slide", "seq", None),
    )
    fused = mesh.shape["seq"] == 8 and mesh.shape["slide"] == 4
    return jax.shard_map(
        fused_device if fused else plain_device,
        mesh=mesh,
        in_specs=placed,
        out_specs=(
            P("slide", "seq", None),
            P("slide", "seq", None),
            P("seq", None),
            P("seq", None),
            P("seq", None),
            P("seq", None),
            P(),
            P(),
            P(),
            P(),
        ),
        check_vma=False,
    )
```

```python
import functools

import jax
import jax.numpy as jnp
from jax import lax
from jax.experimental import pallas as pl
from jax.experimental.pallas import tpu as pltpu
from jax.sharding import PartitionSpec as P

HEADS = 16
HEAD_WIDTH = 48
SEG = 512
QB = 512
DILATION_STEP = 16


epsilon = 1e-05


def layer_norm(values, norm_gain, norm_shift):
    average = jnp.mean(values, axis=-1, keepdims=True)
    centered = values - average
    variance = jnp.mean(centered * centered, axis=-1, keepdims=True)
    return centered * lax.rsqrt(variance + epsilon) * norm_gain + norm_shift


def exact_gelu(values):
    return jax.nn.gelu(values, approximate=False)


def block_scores(query_block, seg_keys, seg_valid, distant_keys, distant_valid):
    nearby_scores = jnp.einsum(
        "iyo,uyo->yiu", query_block, seg_keys, preferred_element_type=jnp.float32
    )
    nearby_scores = jnp.where(seg_valid[None, None, :], nearby_scores, -1000000000.0)
    far_scores = jnp.einsum(
        "iyo,uyo->yiu",
        query_block[::DILATION_STEP],
        distant_keys,
        preferred_element_type=jnp.float32,
    )
    far_scores = jnp.where(distant_valid[None, None, :], far_scores, -1000000000.0)
    return (nearby_scores, far_scores)


def block_forward(
    query_block, seg_keys, seg_values, seg_valid, distant_keys, distant_values, distant_valid
):
    nearby_scores, far_scores = block_scores(
        query_block, seg_keys, seg_valid, distant_keys, distant_valid
    )
    head_number = nearby_scores.shape[0]
    row_number = nearby_scores.shape[1]
    chosen_count = row_number // DILATION_STEP
    maximum_table = jnp.max(nearby_scores, axis=-1).reshape(
        head_number, chosen_count, DILATION_STEP
    )
    combined_top = jnp.maximum(maximum_table[:, :, 0], jnp.max(far_scores, axis=-1))
    row_maximum = maximum_table.at[:, :, 0].set(combined_top).reshape(head_number, row_number)
    nearby_exponent = jnp.exp(nearby_scores - row_maximum[:, :, None])
    far_exp = jnp.exp(far_scores - combined_top[:, :, None])
    exponent_sums = jnp.sum(nearby_exponent, axis=-1).reshape(
        head_number, chosen_count, DILATION_STEP
    )
    combined_total = exponent_sums[:, :, 0] + jnp.sum(far_exp, axis=-1)
    row_sum_total = exponent_sums.at[:, :, 0].set(combined_total).reshape(head_number, row_number)
    local_weights = (nearby_exponent / row_sum_total[:, :, None]).astype(jnp.bfloat16)
    far_weights = (far_exp / combined_total[:, :, None]).astype(jnp.bfloat16)
    attended_rows = jnp.einsum(
        "hqk,khd->qhd", local_weights, seg_values, preferred_element_type=jnp.float32
    )
    distant_attended = jnp.einsum(
        "hqk,khd->qhd", far_weights, distant_values, preferred_element_type=jnp.float32
    )
    attended_rows = (
        attended_rows.reshape(chosen_count, DILATION_STEP, head_number, HEAD_WIDTH)
        .at[:, 0]
        .add(distant_attended)
    )
    return (attended_rows.reshape(row_number, head_number, HEAD_WIDTH), row_maximum, row_sum_total)


def block_backward(
    query_block,
    seg_keys,
    seg_values,
    seg_valid,
    distant_keys,
    distant_values,
    distant_valid,
    gradient_block,
    row_maximum,
    row_sum_total,
):
    nearby_scores, far_scores = block_scores(
        query_block, seg_keys, seg_valid, distant_keys, distant_valid
    )
    head_number = row_maximum.shape[0]
    row_number = row_maximum.shape[1]
    chosen_count = row_number // DILATION_STEP
    combined_top = row_maximum.reshape(head_number, chosen_count, DILATION_STEP)[:, :, 0]
    combined_total = row_sum_total.reshape(head_number, chosen_count, DILATION_STEP)[:, :, 0]
    nearby_probability = (
        jnp.exp(nearby_scores - row_maximum[:, :, None]) / row_sum_total[:, :, None]
    )
    far_prob = jnp.exp(far_scores - combined_top[:, :, None]) / combined_total[:, :, None]
    local_weights = nearby_probability.astype(jnp.bfloat16)
    gradient_sampled = gradient_block[::DILATION_STEP]
    value_grad = jnp.einsum(
        "mns,nmg->smg", local_weights, gradient_block, preferred_element_type=jnp.float32
    )
    nearby_dots = jnp.einsum(
        "iyo,uyo->yiu", gradient_block, seg_values, preferred_element_type=jnp.float32
    )
    far_dots = jnp.einsum(
        "iyo,uyo->yiu", gradient_sampled, distant_values, preferred_element_type=jnp.float32
    )
    delta_table = jnp.sum(nearby_probability * nearby_dots, axis=-1).reshape(
        head_number, chosen_count, DILATION_STEP
    )
    joint_delta = delta_table[:, :, 0] + jnp.sum(far_prob * far_dots, axis=-1)
    row_delta = delta_table.at[:, :, 0].set(joint_delta).reshape(head_number, row_number)
    local_slope = (nearby_probability * (nearby_dots - row_delta[:, :, None])).astype(jnp.bfloat16)
    distant_slope = (far_prob * (far_dots - joint_delta[:, :, None])).astype(jnp.bfloat16)
    query_gradient = jnp.einsum(
        "hqk,khd->qhd", local_slope, seg_keys, preferred_element_type=jnp.float32
    )
    distant_query = jnp.einsum(
        "hqk,khd->qhd", distant_slope, distant_keys, preferred_element_type=jnp.float32
    )
    query_gradient = (
        query_gradient.reshape(chosen_count, DILATION_STEP, head_number, HEAD_WIDTH)
        .at[:, 0]
        .add(distant_query)
    )
    key_grad = jnp.einsum(
        "mns,nmg->smg", local_slope, query_block, preferred_element_type=jnp.float32
    )
    far_weights = far_prob.astype(jnp.bfloat16)
    far_value_grad = jnp.einsum(
        "mns,nmg->smg", far_weights, gradient_sampled, preferred_element_type=jnp.float32
    )
    far_key_grad = jnp.einsum(
        "mns,nmg->smg",
        distant_slope,
        query_block[::DILATION_STEP],
        preferred_element_type=jnp.float32,
    )
    return (
        query_gradient.reshape(row_number, head_number, HEAD_WIDTH),
        key_grad,
        value_grad,
        far_key_grad,
        far_value_grad,
    )


def plain_device(
    tokens,
    qkv_weight,
    out_weight,
    up_weight,
    down_weight,
    norm1_gain,
    norm1_bias,
    norm2_gain,
    norm2_bias,
    visible,
    cotangent,
):
    row_number = tokens.shape[1]
    embedding_width = tokens.shape[2]
    query_scale = HEAD_WIDTH ** (-0.5)
    first_row = lax.axis_index("seq") * row_number
    positions = first_row + jnp.arange(row_number, dtype=jnp.int32)
    row_validity = positions < visible[0]
    inputs = tokens[0].astype(jnp.float32)
    norm_one, pull_one = jax.vjp(layer_norm, inputs, norm1_gain, norm1_bias)
    normed = norm_one.astype(jnp.bfloat16)
    projected = jnp.dot(normed, qkv_weight, preferred_element_type=jnp.float32)
    query_rows = (
        (projected[:, :embedding_width] * query_scale)
        .astype(jnp.bfloat16)
        .reshape(row_number, HEADS, HEAD_WIDTH)
    )
    flat_keys = projected[:, embedding_width : 2 * embedding_width].astype(jnp.bfloat16)
    flat_values = projected[:, 2 * embedding_width :].astype(jnp.bfloat16)
    key_matrix = flat_keys.reshape(row_number, HEADS, HEAD_WIDTH)
    value_matrix = flat_values.reshape(row_number, HEADS, HEAD_WIDTH)
    gathered_keys, gathered_values = (
        lax.all_gather(flat_keys[::DILATION_STEP], "seq", axis=0, tiled=True),
        lax.all_gather(flat_values[::DILATION_STEP], "seq", axis=0, tiled=True),
    )
    distant_count = gathered_keys.shape[0]
    distant_valid = jnp.arange(distant_count, dtype=jnp.int32) * DILATION_STEP < visible[0]
    distant_keys = gathered_keys.reshape(distant_count, HEADS, HEAD_WIDTH)
    distant_values = gathered_values.reshape(distant_count, HEADS, HEAD_WIDTH)
    per_segment = SEG // QB
    attended_rows, row_maximum, row_sum_total = block_forward(
        query_rows,
        key_matrix,
        value_matrix,
        row_validity,
        distant_keys,
        distant_values,
        distant_valid,
    )
    attn_low = attended_rows.reshape(row_number, embedding_width).astype(jnp.bfloat16)
    after_attn = inputs + jnp.dot(attn_low, out_weight, preferred_element_type=jnp.float32)
    norm_two, pull_two = jax.vjp(layer_norm, after_attn, norm2_gain, norm2_bias)
    normed_two = norm_two.astype(jnp.bfloat16)
    up_cols = jnp.dot(normed_two, up_weight, preferred_element_type=jnp.float32)
    activated, pull_gelu = jax.vjp(exact_gelu, up_cols)
    hidden = activated.astype(jnp.bfloat16)
    result = after_attn + jnp.dot(hidden, down_weight, preferred_element_type=jnp.float32)
    mixed_out = jnp.where(row_validity[:, None], result, 0.0).astype(jnp.bfloat16)[None]
    grad_out = jnp.where(row_validity[:, None], cotangent[0], jnp.zeros_like(cotangent[0]))
    down_grad = jnp.einsum("tf,td->fd", hidden, grad_out, preferred_element_type=jnp.float32)
    hidden_grad = jnp.einsum("td,fd->tf", grad_out, down_weight, preferred_element_type=jnp.float32)
    (up_slope,) = pull_gelu(hidden_grad)
    up_low = up_slope.astype(jnp.bfloat16)
    up_grad = jnp.einsum("td,tf->df", normed_two, up_low, preferred_element_type=jnp.float32)
    norm_two_in = jnp.einsum("tf,df->td", up_low, up_weight, preferred_element_type=jnp.float32)
    after_part, gain_two_grad, shift_two_grad = pull_two(norm_two_in)
    resid_grad = grad_out.astype(jnp.float32) + after_part
    resid_low = resid_grad.astype(jnp.bfloat16)
    out_grad = jnp.einsum("td,te->de", attn_low, resid_low, preferred_element_type=jnp.float32)
    attn_grad = jnp.einsum("te,de->td", resid_low, out_weight, preferred_element_type=jnp.float32)
    attn_grad = attn_grad.astype(jnp.bfloat16).reshape(row_number, HEADS, HEAD_WIDTH)
    query_gradient, key_grad, value_grad, far_key_grad, far_value_grad = block_backward(
        query_rows,
        key_matrix,
        value_matrix,
        row_validity,
        distant_keys,
        distant_values,
        distant_valid,
        attn_grad,
        row_maximum,
        row_sum_total,
    )
    key_list = [key_grad]
    value_list = [value_grad]
    owned_keys, owned_values = (
        lax.psum_scatter(
            far_key_grad.reshape(distant_count, embedding_width),
            "seq",
            scatter_dimension=0,
            tiled=True,
        ),
        lax.psum_scatter(
            far_value_grad.reshape(distant_count, embedding_width),
            "seq",
            scatter_dimension=0,
            tiled=True,
        ),
    )
    chosen_count = row_number // DILATION_STEP
    segment_count = row_number // SEG
    nearby_keys = jnp.sum(
        jnp.stack(key_list).reshape(segment_count, per_segment, SEG, embedding_width), axis=1
    )
    nearby_values = jnp.sum(
        jnp.stack(value_list).reshape(segment_count, per_segment, SEG, embedding_width), axis=1
    )
    key_total = (
        nearby_keys.reshape(chosen_count, DILATION_STEP, embedding_width)
        .at[:, 0]
        .add(owned_keys)
        .reshape(row_number, embedding_width)
    )
    value_total = (
        nearby_values.reshape(chosen_count, DILATION_STEP, embedding_width)
        .at[:, 0]
        .add(owned_values)
        .reshape(row_number, embedding_width)
    )
    query_total = query_gradient.reshape(row_number, embedding_width)
    mixed_grad = jnp.concatenate(
        [
            (query_total * query_scale).astype(jnp.bfloat16),
            key_total.astype(jnp.bfloat16),
            value_total.astype(jnp.bfloat16),
        ],
        axis=1,
    )
    qkv_grad = jnp.einsum("td,tf->df", normed, mixed_grad, preferred_element_type=jnp.float32)
    norm_one_in = jnp.einsum(
        "tf,df->td", mixed_grad, qkv_weight, preferred_element_type=jnp.float32
    )
    input_part, gain_one_grad, shift_one_grad = pull_one(norm_one_in)
    tokens_grad = (resid_grad + input_part).astype(jnp.bfloat16)[None]
    weight_grads = (qkv_grad, out_grad, up_grad, down_grad)
    row_parts = (
        lax.psum_scatter(weight_grads[0], "seq", scatter_dimension=0, tiled=True),
        lax.psum_scatter(weight_grads[1], "seq", scatter_dimension=0, tiled=True),
        lax.psum_scatter(weight_grads[2], "seq", scatter_dimension=0, tiled=True),
        lax.psum_scatter(weight_grads[3], "seq", scatter_dimension=0, tiled=True),
    )
    final_grads = (
        lax.psum(row_parts[0].astype(jnp.bfloat16), "slide").astype(jnp.float32),
        lax.psum(row_parts[1].astype(jnp.bfloat16), "slide").astype(jnp.float32),
        lax.psum(row_parts[2].astype(jnp.bfloat16), "slide").astype(jnp.float32),
        lax.psum(row_parts[3].astype(jnp.bfloat16), "slide").astype(jnp.float32),
    )
    norm_grads = lax.psum(
        (gain_one_grad, shift_one_grad, gain_two_grad, shift_two_grad), ("seq", "slide")
    )
    return (
        mixed_out,
        tokens_grad,
        final_grads[0],
        final_grads[1],
        final_grads[2],
        final_grads[3],
        norm_grads[0],
        norm_grads[1],
        norm_grads[2],
        norm_grads[3],
    )


MESH = pl.DeviceIdType.MESH
LOW = jnp.bfloat16
FULL = jnp.float32
AUG = 64
LANES = 128
NEVER = -1000000000.0
ANY = pl.BlockSpec(memory_space=pl.ANY)
VMEM = pl.BlockSpec(memory_space=pltpu.VMEM)
SMEM = pl.BlockSpec(memory_space=pltpu.SMEM)


def nn(left, right):
    return jnp.dot(left, right, preferred_element_type=FULL)


def nt(left, right):
    return lax.dot_general(left, right, (((1,), (1,)), ((), ())), preferred_element_type=FULL)


def tn(left, right):
    return lax.dot_general(left, right, (((0,), (0,)), ((), ())), preferred_element_type=FULL)


def remote(src, dst, send_sem, recv_sem, device):
    return pltpu.make_async_remote_copy(
        src_ref=src,
        dst_ref=dst,
        send_sem=send_sem,
        recv_sem=recv_sem,
        device_id=device,
        device_id_type=MESH,
    )


def greet(devices):
    barrier = pltpu.get_barrier_semaphore()
    for device in devices:
        pl.semaphore_signal(barrier, inc=1, device_id=device, device_id_type=MESH)
    pl.semaphore_wait(barrier, len(devices))


def row_peers(count):
    seq, slide = lax.axis_index("seq"), lax.axis_index("slide")
    return [(lax.rem(seq + step, count), slide) for step in range(1, count)]


def spread(ref, values):
    for group in range(ref.shape[0]):
        ref[group] = values[:, group * LANES : (group + 1) * LANES]


def strided_rows(ref, step, count):
    groups = [
        ref[group, pl.ds(step, count, stride=DILATION_STEP), :] for group in range(ref.shape[0])
    ]
    return jnp.concatenate(groups, axis=1)


def strided_store(ref, step, count, values):
    for group in range(ref.shape[0]):
        ref[group, pl.ds(step, count, stride=DILATION_STEP), :] = values[
            :, group * LANES : (group + 1) * LANES
        ]


def chunk(step, size):
    return pl.ds(pl.multiple_of(step * size, size), size)


def steps(body):
    @pl.loop(0, DILATION_STEP // 4)
    def _(group):
        for member in range(4):
            body(group * 4 + member)


def row_mean(values):
    return jnp.mean(values, axis=-1, keepdims=True)


def fold_rows(values):
    return jnp.sum(values.reshape(-1, 8, values.shape[-1]), axis=0)


def mask_rows(ref, bias):
    first = lax.broadcasted_iota(jnp.int32, (AUG - HEAD_WIDTH, ref.shape[2]), 0) == 0
    ref[:, HEAD_WIDTH:, :] = jnp.broadcast_to(
        jnp.where(first, bias, 0.0).astype(LOW), (HEADS, AUG - HEAD_WIDTH, ref.shape[2])
    )


class Place:
    def __init__(self):
        seq, slide = lax.axis_index("seq"), lax.axis_index("slide")
        self.seq, self.slide = seq, slide
        self.z, self.x = seq // 2, seq % 2
        self.y, self.c = slide // 2, slide % 2
        self.sibling = (seq, slide + 1 - 2 * self.c)
        self.across_y = (seq, slide + 2 - 4 * self.y)
        self.diagonal = (seq, 3 - slide)
        self.across_x = (seq + 1 - 2 * self.x, slide)
        self.slide_peers = (self.sibling, self.across_y, self.diagonal)

    def layer(self, step):
        return (self.z + step) % 4


class Part:
    def __init__(self, place, orders, both, core_got, got, final, send_sem, recv_sem):
        self.place, self.orders, self.both = place, orders, both
        self.core_got, self.got, self.final = core_got, got, final
        self.send_sem, self.recv_sem = send_sem, recv_sem

    def blocks(self, core, phase, value):
        order = self.orders[core]
        choices = {}
        for at, name in enumerate(order, 1):
            if at < phase:
                choices[name] = [getattr(self.place, name)]
            elif at == phase:
                choices[name] = [value]
            else:
                choices[name] = list(range(4 if name == "z" else 2))
        return [(2 * z + x, y) for z in choices["z"] for x in choices["x"] for y in choices["y"]]

    def partners(self, core, phase):
        place, name = self.place, self.orders[core][phase - 1]
        if name == "x":
            return [(1 - place.x, place.across_x)]
        if name == "y":
            return [(1 - place.y, place.across_y)]
        layers = [place.layer(k) for k in (1, 2, 3)]
        return [(z, (2 * z + place.x, place.slide)) for z in layers]

    def span(self, core, phase):
        first, left = 0, 16
        for at, name in enumerate(self.orders[core], 1):
            left //= 4 if name == "z" else 2
            number = left * (3 if name == "z" else 1)
            if at == phase:
                return first, number
            first += number

    def transfers(self, core, phase):
        kept, got = self.both.at[0], self.got
        slot = self.span(core, phase)[0]
        pairs = "y" in self.orders[core][phase:]
        moves = []
        for value, device in self.partners(core, phase):
            for owner, y in self.blocks(core, phase, value):
                if not pairs:
                    moves.append((kept.at[owner, y], got.at[slot], device))
                elif y == 0:
                    moves.append((kept.at[owner], got.at[pl.ds(slot, 2)], device))
                slot += 1
        return moves

    def start(self, phase, merged):
        place, send, recv = self.place, self.send_sem.at[phase], self.recv_sem.at[phase]
        if phase == 0:
            remote(self.both.at[1], self.core_got, send, recv, place.sibling).start()
        elif phase <= 3:
            for core in range(2):

                @pl.when(place.c == core)
                def _(core=core):
                    for source, target, device in self.transfers(core, phase):
                        remote(source, target, send, recv, device).start()
        elif phase == 4:
            own = self.final.at[place.c * 2 + place.y]
            for device in place.slide_peers if merged else (place.across_y,):
                remote(own, own, send, recv, device).start()
        else:
            own = self.final.at[pl.ds(place.c * 2, 2)]
            remote(own, own, send, recv, place.sibling).start()

    def wait(self, phase, whole):
        both_ways = remote(
            whole, whole, self.send_sem.at[phase], self.recv_sem.at[phase], self.place.sibling
        )
        both_ways.wait_recv()
        both_ways.wait_send()

    def finish(self, phase, merged):
        place = self.place
        if phase == 0:
            self.wait(phase, self.core_got)

            @pl.loop(0, 8)
            def _(owner):
                for row in range(2):
                    self.both[0, owner, row] += self.core_got[owner, row]
        elif phase <= 3:
            for core in range(2):

                @pl.when(place.c == core)
                def _(core=core):
                    first, number = self.span(core, phase)
                    self.wait(phase, self.got.at[pl.ds(first, number)])
                    name = self.orders[core][phase - 1]
                    blocks = self.blocks(core, phase, getattr(place, name))
                    for n, (owner, y) in enumerate(blocks):
                        slots = range(first + n, first + number, len(blocks))
                        self.add(owner, y, slots, core if phase == 3 else None)
        elif phase == 4:
            self.wait(phase, self.final.at[pl.ds(0, 3 if merged else 1)])
        else:
            self.wait(phase, self.final.at[pl.ds(0, 2)])

    def add(self, owner, y, slots, core):
        if len(slots) == 1:
            total = self.both[0, owner, y] + self.got[slots[0]]
        else:
            total = self.both[0, owner, y].astype(FULL)
            for slot in slots:
                total = total + self.got[slot].astype(FULL)
            total = total.astype(LOW)
        if core is None:
            self.both[0, owner, y] = total
        else:
            self.final[core * 2 + self.place.y] = total


class Piece:
    def __init__(self, parts, merged, outs, out_sem):
        self.parts, self.merged, self.outs, self.out_sem = parts, merged, outs, out_sem
        self.last = 4 if merged else 5
        self.phase = -1

    @property
    def done(self):
        return self.phase > self.last

    def advance(self):
        if self.done:
            return
        if self.phase >= 0:
            for part in self.parts:
                part.finish(self.phase, self.merged)
        self.phase += 1
        if not self.done:
            for part in self.parts:
                part.start(self.phase, self.merged)
            return
        for n in range(len(self.parts)):
            self.out_copy(n).start()

    def out_copy(self, n):
        return pltpu.make_async_copy(self.parts[n].final, self.outs[n], self.out_sem.at[n])


TILES = 3
LASTS = 4
PIECES = TILES + LASTS
ORDERS = (
    ("xyz", "zxy"),
    ("yxz", "xzy"),
    ("yxz", "xyz"),
    ("zxy", "yxz"),
    ("xyz", "yxz"),
    ("yxz", "yxz"),
    ("xyz", "xyz"),
)
HOOKS = {
    "tile1.1": (0,),
    "tile2.1": (1,),
    "after2": (2,),
    "far": (1,),
    "near0": (0,),
    "near4": (3,),
    "near5": (1, 2, 4),
    "near6": (0,),
    "into": (3, 5, 6),
    "norm": (1, 2, 4),
}
TAIL = (3, 0, 6, 5, 1, 4, 2, 1, 3, 0, 5, 0, 6, 4, 2, 3, 5, 2, 4, 6, 5, 6)

def main_kernel(
    count, tokens, cotangent, qkv_weight, out_weight, up_weight, down_weight,
    gain_one, shift_one, gain_two, shift_two, visible,
    mixed_out, tokens_out, down_sums, up_sums, last_sums, norm_out, weights_kept, norm_kept,
    normed, far_normed, query, key, value, far_key, far_value, far_weights, scale, far_scale, attn,
    delta, slope, resid, after, dyb, wqkv, wo, wide, staged, all_far, far_got, spread_one,
    sums, around, across,
    down_both, up_both, last_both, down_core, up_core, last_core,
    down_got, up_got, last_got, down_final, up_final, last_final,
    load_sem, tile_sem, group_sem, store_sem, out_sem, send_sem, recv_sem,
    gather_send_sem, gather_recv_sem, far_send_sem, far_recv_sem, norm_send_sem, norm_recv_sem,
):
    place = Place()
    seq, core = place.seq, place.c
    rows, width = resid.shape
    chosen = rows // DILATION_STEP
    group_lanes = LANES
    tile_width = count * group_lanes
    first_row = seq * rows
    limit = visible[0]
    peers = row_peers(count)
    others = list(place.slide_peers) + peers
    barrier = pltpu.get_barrier_semaphore()
    for other in others:
        pl.semaphore_signal(barrier, inc=1, device_id=other, device_id_type=MESH)

    def valid_rows(step):
        places = lax.broadcasted_iota(jnp.int32, (chosen, 1), 0) * DILATION_STEP + step
        return first_row + places < limit

    def landed(n):
        sources = (
            (tokens, staged),
            (qkv_weight.at[:, pl.ds(width, width)], wqkv.at[1]),
            (qkv_weight.at[:, pl.ds(2 * width, width)], wqkv.at[2]),
            (qkv_weight.at[:, pl.ds(0, width)], wqkv.at[0]),
            (out_weight, wo),
            (cotangent, staged),
        )
        return pltpu.make_async_copy(*sources[n], load_sem.at[n])

    for n in range(5):
        landed(n).start()
    distant = count * chosen
    members = 4

    def kept_group(group, slots):
        kept = weights_kept.at[pl.ds(group * members, members)]
        return slots.at[group % 2], kept, group_sem.at[group % 2]

    pieces = []
    for n in range(TILES):
        parts = [
            Part(
                place,
                ORDERS[n],
                both.at[n],
                core_got.at[n],
                got.at[n],
                final.at[n],
                send_sem.at[n, which],
                recv_sem.at[n, which],
            )
            for which, (both, core_got, got, final) in enumerate(
                (
                    (down_both, down_core, down_got, down_final),
                    (up_both, up_core, up_got, up_final),
                )
            )
        ]
        pieces.append(Piece(parts, False, (down_sums.at[n], up_sums.at[n]), out_sem.at[n]))
    for n in range(LASTS):
        part = Part(
            place,
            ORDERS[TILES + n],
            last_both.at[n],
            last_core.at[n],
            last_got.at[n],
            last_final.at[n],
            send_sem.at[TILES + n, 0],
            recv_sem.at[TILES + n, 0],
        )
        pieces.append(Piece([part], True, (last_sums.at[n],), out_sem.at[TILES + n]))

    def hook(name):
        for n in HOOKS.get(name, ()):
            if pieces[n].phase >= 0:
                pieces[n].advance()

    def split_last(n, side, grads):
        target = last_both.at[n, (side + core) % 2]
        target[...] = grads.astype(LOW).reshape(count, 2, -1, grads.shape[1])

    def attend_part(h1, top, total, attended, weights):
        landed(0).wait()
        spread(wide, staged[...].astype(FULL))
        landed(5).start()

        def normalize(step):
            at = chunk(step, chosen)
            values = strided_rows(wide, step, chosen)
            centered = values - row_mean(values)
            inverse = lax.rsqrt(row_mean(centered * centered) + epsilon)
            normal = centered * inverse
            after[at] = values
            resid[at] = normal
            spread_one[at] = jnp.broadcast_to(inverse, (chosen, LANES))
            low = (normal * gain_one[...][None] + shift_one[...][None]).astype(LOW)
            h1[at] = low
            return low

        all_far[seq] = normalize(0)

        @pl.loop(0, 5)
        def _(group):
            for member in range(3):
                normalize(group * 3 + member + 1)

        pltpu.make_async_copy(resid, norm_kept, store_sem.at[0]).start()
        for part, ref in ((1, key), (2, value)):
            landed(part).wait()
            projected = nn(h1[...], wqkv[part]).astype(LOW)
            ref[:, :HEAD_WIDTH, :] = projected.T.reshape(HEADS, HEAD_WIDTH, rows)
            if part == 1:
                pl.semaphore_wait(barrier, len(others))
                for n, peer in enumerate(peers):
                    mine = all_far.at[seq]
                    send, recv = gather_send_sem.at[n], gather_recv_sem.at[n]
                    remote(mine, mine, send, recv, peer).start()
        landed(3).wait()
        projected = (nn(h1[...], wqkv[0]) * HEAD_WIDTH ** (-0.5)).astype(LOW)
        query[:, :HEAD_WIDTH, :] = projected.T.reshape(HEADS, HEAD_WIDTH, rows)
        places = lax.broadcasted_iota(jnp.int32, (1, rows), 1)
        places = first_row + (places % chosen) * DILATION_STEP + places // chosen
        mask_rows(key, jnp.where(places < limit, 0.0, NEVER))
        mask_rows(query, jnp.ones((1, rows), FULL))
        for group in range(HEADS // members):
            slot, kept, sem = kept_group(group, weights)
            if group >= 2:
                pltpu.make_async_copy(slot, kept, sem).wait()
            for member in range(members):
                head = group * members + member
                scores = tn(key[head], query[head])
                highest = jnp.max(scores, axis=0, keepdims=True)
                exponent = jnp.exp(scores - highest)
                top[head] = highest
                total[head] = jnp.sum(exponent, axis=0, keepdims=True)
                low = exponent.astype(LOW)
                weights[group % 2, member] = low
                attended[head] = nn(value[head], low)
            pltpu.make_async_copy(slot, kept, sem).start()
        normed[...] = h1[...].T
        landed(5).wait()
        spread(wide, staged[...].astype(FULL))

        @steps
        def _(step):
            at = chunk(step, chosen)
            dyb[at] = jnp.where(valid_rows(step), strided_rows(wide, step, chosen), 0.0).astype(LOW)

        for n in range(count - 1):
            source = lax.rem(seq + count - 1 - n, count)
            mine, theirs = all_far.at[seq], all_far.at[source]
            wait = remote(mine, theirs, gather_send_sem.at[n], gather_recv_sem.at[n], peers[0])
            wait.wait_recv()
            wait.wait_send()
        flat = all_far[...].reshape(distant, width)
        for part, ref in ((1, far_key), (2, far_value)):
            projected = nn(flat, wqkv[part]).astype(LOW)
            ref[:, :HEAD_WIDTH, :] = projected.T.reshape(HEADS, HEAD_WIDTH, distant)
        places = lax.broadcasted_iota(jnp.int32, (1, distant), 1) * DILATION_STEP
        mask_rows(far_key, jnp.where(places < limit, 0.0, NEVER))
        lane_mask = jnp.where(lax.broadcasted_iota(jnp.int32, (1, LANES), 1) < chosen, 0.0, NEVER)

        @pl.loop(0, HEADS // 4)
        def _(group):
            for member in range(4):
                head = group * 4 + member
                scores = tn(far_key[head], query[head][:, :LANES]) + lane_mask
                highest = jnp.max(scores, axis=0, keepdims=True)
                exponent = jnp.exp(scores - highest)
                low = exponent.astype(LOW)
                far_weights[head] = low
                near = top[head][:, :LANES]
                joint = jnp.maximum(near, highest)
                near_part, far_part = jnp.exp(near - joint), jnp.exp(highest - joint)
                joint_total = total[head][:, :LANES] * near_part + far_part * jnp.sum(
                    exponent, axis=0, keepdims=True
                )
                near_part, far_part = near_part / joint_total, far_part / joint_total
                far_scale[head] = far_part
                local = jnp.concatenate([near_part, 1.0 / total[head][:, LANES:]], axis=1)
                scale[head] = local
                result = attended[head] * local
                with_far = result[:, :LANES] + nn(far_value[head], low) * far_part
                result = jnp.concatenate([with_far, result[:, LANES:]], axis=1)
                attn[head] = result.astype(LOW)

        for group in (2, 3):
            slot, kept, sem = kept_group(group, weights)
            pltpu.make_async_copy(slot, kept, sem).wait()
        pltpu.make_async_copy(resid, norm_kept, store_sem.at[0]).wait()

    vm = pltpu.VMEM
    pl.run_scoped(
        attend_part,
        vm((rows, width), LOW),
        vm((HEADS, 1, rows), FULL),
        vm((HEADS, 1, rows), FULL),
        vm((HEADS, HEAD_WIDTH, rows), FULL),
        vm((2, members, rows, rows), LOW),
    )

    def forward_part(norm_two, spread_two, h2, h2_t, active, low_slope, wup, wdown):
        halves = 2
        per_half = tile_width // halves

        def load_tile(number):
            tile, half = divmod(number, halves)
            slot = number % 2
            for local in range(count // halves):
                owner = half * (count // halves) + local
                at = pl.ds(owner * TILES * group_lanes + tile * group_lanes, group_lanes)
                to = pl.ds(local * group_lanes, group_lanes)
                pltpu.make_async_copy(
                    up_weight.at[:, at], wup.at[slot, :, to], tile_sem.at[slot, 0]
                ).start()
                pltpu.make_async_copy(
                    down_weight.at[at], wdown.at[slot, to], tile_sem.at[slot, 1]
                ).start()

        def wait_tile(number):
            slot = number % 2
            pltpu.make_async_copy(wup.at[slot], wup.at[slot], tile_sem.at[slot, 0]).wait()
            pltpu.make_async_copy(wdown.at[slot], wdown.at[slot], tile_sem.at[slot, 1]).wait()

        load_tile(0)
        load_tile(1)
        landed(4).wait()
        after[...] += nn(attn[...].reshape(width, rows).T, wo[...])

        @steps
        def _(step):
            at = chunk(step, chosen)
            values = after[at]
            centered = values - row_mean(values)
            inverse = lax.rsqrt(row_mean(centered * centered) + epsilon)
            normal = centered * inverse
            norm_two[at] = normal
            spread_two[at] = jnp.broadcast_to(inverse, (chosen, LANES))
            h2[at] = (normal * gain_two[...][None] + shift_two[...][None]).astype(LOW)
            resid[at] = jnp.zeros((chosen, width), FULL)

        h2_t[...] = h2[...].T
        for tile in range(TILES):
            for half in range(halves):
                number = tile * halves + half
                slot = number % 2
                wait_tile(number)
                for part in range(2):
                    at = slice(part * per_half // 2, (part + 1) * per_half // 2)
                    to = slice(
                        half * per_half + part * per_half // 2,
                        half * per_half + (part + 1) * per_half // 2,
                    )
                    hidden = nn(h2[...], wup[slot, :, at])
                    hidden_slope = nt(dyb[...], wdown[slot, at])
                    share = 0.5 * (1.0 + lax.erf(hidden * 0.7071067811865476))
                    active[:, to] = (hidden * share).astype(LOW)
                    density = hidden * jnp.exp(-0.5 * hidden * hidden) * 0.3989422804014327
                    low_slope[:, to] = (hidden_slope * (share + density)).astype(LOW)
                to = slice(half * per_half, (half + 1) * per_half)
                after[...] += nn(active[:, to], wdown[slot])
                resid[...] += nt(low_slope[:, to], wup[slot])
                if number + 2 < TILES * halves:
                    load_tile(number + 2)
                hook("tile%d.%d" % (tile, half))
            for part in range(4):
                at = slice(part * tile_width // 4, (part + 1) * tile_width // 4)
                grads = nn(h2_t[...], low_slope[:, at]).astype(LOW)
                side, row = divmod(part, 2)
                up_both.at[tile, (side + core) % 2][:, row] = grads.reshape(count, -1, grads.shape[1])
                grads = tn(active[:, at], dyb[...]).astype(LOW)
                owners = count // 4
                grads = grads.reshape(owners, 2, 2, -1, width)
                for side in range(2):
                    target = down_both.at[tile, (side + core) % 2]
                    target[part * owners : (part + 1) * owners] = grads[:, side]
                if part == 1:
                    hook("tile%d.2" % tile)
            pieces[tile].advance()
            hook("tile%d.3" % tile)
        sums[...] = jnp.zeros_like(sums)
        hook("after0")

        @steps
        def _(step):
            at = chunk(step, chosen)
            strided_store(wide, step, chosen, jnp.where(valid_rows(step), after[at], 0.0))
            given, normal = resid[at], norm_two[at]
            sums[2] += fold_rows(given * normal)
            sums[3] += fold_rows(given)
            scaled = given * gain_two[...][None]
            part = scaled - row_mean(scaled) - normal * row_mean(scaled * normal)
            value_here = dyb[at].astype(FULL) + spread_two[at][:, :1] * part
            resid[at] = value_here
            h2[at] = value_here.astype(LOW)

        for group in range(width // LANES):
            staged[:, group * LANES : (group + 1) * LANES] = wide[group].astype(LOW)
        pltpu.make_async_copy(staged, mixed_out, store_sem.at[1]).start()
        half = width // 2
        hook("after1")
        for n in range(2):
            at = slice(n * half, (n + 1) * half)
            split_last(2 * n + 1, 1, nn(attn[...].reshape(width, rows), h2[:, at]))
        slope[...] = nt(wo[...], h2[...]).astype(LOW).reshape(HEADS, HEAD_WIDTH, rows)

        @pl.loop(0, HEADS)
        def _(head):
            product = slope[head].astype(FULL) * attn[head].astype(FULL)
            delta[head] = jnp.sum(product, axis=0, keepdims=True)

        hook("after2")

    pl.run_scoped(
        forward_part,
        vm((rows, width), FULL),
        vm((rows, LANES), FULL),
        vm((rows, width), LOW),
        vm((width, rows), LOW),
        vm((rows, tile_width), LOW),
        vm((rows, tile_width), LOW),
        vm((2, width, tile_width // 2), LOW),
        vm((2, tile_width // 2, width), LOW),
    )

    def backward_part(weights, slopes, far_query, far_send, given):
        norm_one = after

        def load_group(group):
            slot, kept, sem = kept_group(group, weights)
            return pltpu.make_async_copy(kept, slot, sem)

        load_group(0).start()
        load_group(1).start()
        norm_load = pltpu.make_async_copy(norm_kept, norm_one, store_sem.at[0])
        norm_load.start()

        @pl.loop(0, HEADS // 4)
        def _(group):
            for member in range(4):
                head = group * 4 + member
                first_slope = slope[head][:, :LANES]
                low = far_weights[head]
                change = tn(far_value[head], first_slope) - delta[head][:, :LANES]
                score_slope = (low.astype(FULL) * far_scale[head] * change).astype(LOW)
                far_query[head] = nn(far_key[head, :HEAD_WIDTH], score_slope)
                scaled = (first_slope.astype(FULL) * far_scale[head]).astype(LOW)
                given[0, head] = nt(query[head, :HEAD_WIDTH, :LANES], score_slope).astype(LOW)
                given[1, head] = nt(scaled, low).astype(LOW)

        hook("far0")
        far_normed[...] = all_far[...].reshape(distant, width).T
        into = nn(wqkv[1], given[0].reshape(width, distant))
        into += nn(wqkv[2], given[1].reshape(width, distant))
        far_send[...] = into.T.astype(LOW).reshape(count, chosen, width)
        for n, peer in enumerate(peers):
            remote(
                far_send.at[peer[0]], far_got.at[n], far_send_sem.at[n], far_recv_sem.at[n], peer
            ).start()
        hook("far")

        def weight_slopes(half):
            at = slice(half * HEADS // 2, (half + 1) * HEADS // 2)
            for part, (n, side) in enumerate(((0, 0), (0, 1), (1, 0))):
                grads = nt(normed[...], slopes[part, at].reshape(width // 2, rows))
                if part:
                    far = given[part - 1, at].reshape(width // 2, distant)
                    grads += nt(far_normed[...], far)
                split_last(2 * half + n, side, grads)
                if part:
                    pieces[TILES + 2 * half + n].advance()
                    hook("last%d" % (2 * half + n))

        for group in range(HEADS // members):
            load_group(group).wait()
            for member in range(members):
                head = group * members + member
                low = weights[group % 2, member]
                change = tn(value[head], slope[head]) - delta[head]
                score_slope = (low.astype(FULL) * scale[head] * change).astype(LOW)
                query_slope = nn(key[head, :HEAD_WIDTH], score_slope)
                key_slope = nt(query[head, :HEAD_WIDTH], score_slope)
                scaled = (slope[head].astype(FULL) * scale[head]).astype(LOW)
                value_slope = nt(scaled, low)
                first = query_slope[:, :LANES] + far_query[head]
                query_slope = jnp.concatenate([first, query_slope[:, LANES:]], axis=1)
                slopes[0, head] = (query_slope * HEAD_WIDTH ** (-0.5)).astype(LOW)
                slopes[1, head] = key_slope.astype(LOW)
                slopes[2, head] = value_slope.astype(LOW)
                if member % 2:
                    hook("near%d" % (head // 2))
            if (group + 2) * members < HEADS:
                load_group(group + 2).start()
            if group % 2:
                weight_slopes(group // 2)

        def flat_slopes(part):
            return slopes[part].reshape(width, rows)

        into = nn(wqkv[0], flat_slopes(0))
        into += nn(wqkv[1], flat_slopes(1))
        into += nn(wqkv[2], flat_slopes(2))
        norm_load.wait()
        pltpu.make_async_copy(staged, mixed_out, store_sem.at[1]).wait()
        spread(wide, into.T)
        hook("into")
        total = far_send[seq].astype(FULL)
        for n in range(count - 1):
            wait = remote(
                far_got.at[n], far_got.at[n], far_send_sem.at[n], far_recv_sem.at[n], peers[0]
            )
            wait.wait_recv()
            wait.wait_send()
            total = total + far_got[n].astype(FULL)
        for group in range(width // LANES):
            wide[group, :chosen] += total[:, group * LANES : (group + 1) * LANES]

        @steps
        def _(step):
            at = chunk(step, chosen)
            here = jnp.concatenate([wide[group, at, :] for group in range(width // LANES)], axis=1)
            normal = norm_one[at]
            sums[0] += fold_rows(here * normal)
            sums[1] += fold_rows(here)
            scaled = here * gain_one[...][None]
            part = scaled - row_mean(scaled) - normal * row_mean(scaled * normal)
            resid[at] += spread_one[at][:, :1] * part

    pl.run_scoped(
        backward_part,
        vm((2, members, rows, rows), LOW),
        vm((3, HEADS, HEAD_WIDTH, rows), LOW),
        vm((HEADS, HEAD_WIDTH, LANES), FULL),
        vm((count, chosen, width), LOW),
        vm((2, HEADS, HEAD_WIDTH, distant), LOW),
    )
    for n in range(4):
        around[seq, pl.ds(n, 1)] = jnp.sum(sums[n], axis=0, keepdims=True)
    for n, peer in enumerate(peers):
        mine = around.at[seq]
        remote(mine, mine, norm_send_sem.at[n], norm_recv_sem.at[n], peer).start()
    hook("norm")

    @steps
    def _(step):
        strided_store(wide, step, chosen, resid[chunk(step, chosen)])

    for group in range(width // LANES):
        staged[:, group * LANES : (group + 1) * LANES] = wide[group].astype(LOW)
    tokens_copy = pltpu.make_async_copy(staged, tokens_out, store_sem.at[2])
    tokens_copy.start()
    for n in range(count - 1):
        mine = around.at[seq]
        wait = remote(mine, mine, norm_send_sem.at[n], norm_recv_sem.at[n], peers[0])
        wait.wait_recv()
        wait.wait_send()
    total = around[0]
    for n in range(1, count):
        total = total + around[n]
    across[place.slide] = total
    for n, peer in enumerate(place.slide_peers):
        mine, at = across.at[place.slide], count - 1 + n
        remote(mine, mine, norm_send_sem.at[at], norm_recv_sem.at[at], peer).start()
    for n in TAIL + tuple(range(PIECES)) * 6:
        pieces[n].advance()
    for n in range(3):
        mine, at = across.at[0], count - 1 + n
        wait = remote(mine, mine, norm_send_sem.at[at], norm_recv_sem.at[at], peers[0])
        wait.wait_recv()
        wait.wait_send()
    norm_out[...] = (across[0] + across[1]) + (across[2] + across[3])
    for piece in pieces:
        for n in range(len(piece.parts)):
            piece.out_copy(n).wait()
    tokens_copy.wait()


def main_pass(count, tokens, cotangent, weights, norms, visible):
    rows, width = tokens.shape
    chosen = rows // DILATION_STEP
    distant = count * chosen
    owned = width // count
    vm, dma = pltpu.VMEM, pltpu.SemaphoreType.DMA
    down_block, up_block = (LANES // 4, width), (owned, 2 * LANES)
    last_block = (owned // 2, width // 2)
    blocks = ((TILES, down_block), (TILES, up_block), (LASTS, last_block))
    low = [
        (width, rows), (width, distant), (HEADS, AUG, rows), (HEADS, AUG, rows),
        (HEADS, HEAD_WIDTH, rows), (HEADS, AUG, distant), (HEADS, HEAD_WIDTH, distant),
        (HEADS, distant, LANES),
    ]
    scratch = [vm(shape, LOW) for shape in low]
    scratch += [
        vm((HEADS, 1, rows), FULL),
        vm((HEADS, 1, LANES), FULL),
        vm((HEADS, HEAD_WIDTH, rows), LOW),
        vm((HEADS, 1, rows), FULL),
        vm((HEADS, HEAD_WIDTH, rows), LOW),
        vm((rows, width), FULL),
        vm((rows, width), FULL),
        vm((rows, width), LOW),
        vm((3, width, width), LOW),
        vm((width, width), LOW),
        vm((width // LANES, rows, LANES), FULL),
        vm((rows, width), LOW),
        vm((count, chosen, width), LOW),
        vm((count - 1, chosen, width), LOW),
        vm((rows, LANES), FULL),
        vm((4, 8, width), FULL),
        vm((count, 8, width), FULL),
        vm((4, 8, width), FULL),
    ]
    scratch += [vm((n, 2, count, 2) + block, LOW) for n, block in blocks]
    scratch += [vm((n, count, 2) + block, LOW) for n, block in blocks]
    scratch += [vm((n, 15) + block, LOW) for n, block in blocks]
    scratch += [vm((n, 4) + block, LOW) for n, block in blocks]
    scratch += [
        dma((6,)), dma((2, 2)), dma((2,)), dma((3,)), dma((PIECES, 2)),
        dma((PIECES, 2, 6)), dma((PIECES, 2, 6)),
        dma((count - 1,)), dma((count - 1,)), dma((count - 1,)), dma((count - 1,)),
        dma((count + 2,)), dma((count + 2,)),
    ]
    sums = [jax.ShapeDtypeStruct((n, 4) + block, LOW) for n, block in blocks]
    results = pl.pallas_call(
        functools.partial(main_kernel, count),
        out_shape=(
            jax.ShapeDtypeStruct((rows, width), LOW),
            jax.ShapeDtypeStruct((rows, width), LOW),
            *sums,
            jax.ShapeDtypeStruct((8, width), FULL),
            jax.ShapeDtypeStruct((HEADS, rows, rows), LOW),
            jax.ShapeDtypeStruct((rows, width), FULL),
        ),
        in_specs=[ANY] * 6 + [VMEM] * 4 + [SMEM],
        out_specs=(ANY, ANY, ANY, ANY, ANY, VMEM, ANY, ANY),
        scratch_shapes=scratch,
        compiler_params=pltpu.CompilerParams(
            collective_id=1, has_side_effects=True, vmem_limit_bytes=64 << 20
        ),
        name="main_pass",
    )(tokens, cotangent, *weights, *norms, visible)
    return results[:6]


def finish_kernel(
    mixed, tokens_grad, down_sums, up_sums, last_sums, norms,
    mixed_out, tokens_out, qkv_out, out_out, up_out, down_out, *norm_outs
):
    mixed_out[...] = mixed[...]
    tokens_out[...] = tokens_grad[...]
    tiles, blocks, rows, _ = down_sums.shape
    for tile in range(tiles):
        for block in range(blocks):
            first = (tile * blocks + block) * rows
            down_out[first : first + rows] = down_sums[tile, block].astype(FULL)
            for half in range(2):
                first = ((block * 2 + half) * tiles + tile) * LANES
                part = up_sums[tile, block][:, half * LANES : (half + 1) * LANES]
                up_out[:, first : first + LANES] = part.astype(FULL)
    rows, columns = last_sums.shape[2:]
    for piece in range(last_sums.shape[0]):
        half, pair = divmod(piece, 2)
        for block in range(blocks):
            side, row = divmod(block, 2)
            at = slice(row * rows, (row + 1) * rows)
            first = half * columns
            out = out_out
            if pair == 0 or side == 0:
                out, first = qkv_out, first + 2 * columns * (2 * pair + side)
            out[at, first : first + columns] = last_sums[piece, block].astype(FULL)
    for n, out in enumerate(norm_outs):
        out[...] = norms[n]


def finish_pass(count, results):
    rows, width = results[0].shape
    owned = width // count

    def full(*shape):
        return jax.ShapeDtypeStruct(shape, FULL)

    return pl.pallas_call(
        finish_kernel,
        out_shape=(
            jax.ShapeDtypeStruct((rows, width), LOW),
            jax.ShapeDtypeStruct((rows, width), LOW),
            full(owned, 3 * width),
            full(owned, width),
            full(owned, TILES * count * LANES),
            full(TILES * LANES, width),
            *[full(width)] * 4,
        ),
        in_specs=[VMEM] * 6,
        out_specs=tuple([VMEM] * 10),
        compiler_params=pltpu.CompilerParams(vmem_limit_bytes=63 << 20),
        name="finish_pass",
    )(*results)


def fused_device(
    tokens,
    qkv_weight,
    out_weight,
    up_weight,
    down_weight,
    norm1_gain,
    norm1_bias,
    norm2_gain,
    norm2_bias,
    visible,
    cotangent,
):
    count = lax.axis_size("seq")
    results = main_pass(
        count,
        tokens[0],
        cotangent[0],
        (qkv_weight, out_weight, up_weight, down_weight),
        (norm1_gain, norm1_bias, norm2_gain, norm2_bias),
        visible,
    )
    mixed, tokens_grad, *grads = finish_pass(count, results)
    return (mixed[None], tokens_grad[None], *grads)


def solution(mesh):
    placed = (
        P("slide", "seq", None),
        P(),
        P(),
        P(),
        P(),
        P(),
        P(),
        P(),
        P(),
        P("slide"),
        P("slide", "seq", None),
    )
    fused = mesh.shape["seq"] == 8 and mesh.shape["slide"] == 4
    return jax.shard_map(
        fused_device if fused else plain_device,
        mesh=mesh,
        in_specs=placed,
        out_specs=(
            P("slide", "seq", None),
            P("slide", "seq", None),
            P("seq", None),
            P("seq", None),
            P("seq", None),
            P("seq", None),
            P(),
            P(),
            P(),
            P(),
        ),
        check_vma=False,
    )
```

```python
import functools

import jax
import jax.numpy as jnp
from jax import lax
from jax.experimental import pallas as pl
from jax.experimental.pallas import tpu as pltpu
from jax.sharding import PartitionSpec as P

HEADS = 16
HEAD_WIDTH = 48
SEG = 512
QB = 512
DILATION_STEP = 16


epsilon = 1e-05


def layer_norm(values, norm_gain, norm_shift):
    average = jnp.mean(values, axis=-1, keepdims=True)
    centered = values - average
    variance = jnp.mean(centered * centered, axis=-1, keepdims=True)
    return centered * lax.rsqrt(variance + epsilon) * norm_gain + norm_shift


def exact_gelu(values):
    return jax.nn.gelu(values, approximate=False)


def block_scores(query_block, seg_keys, seg_valid, distant_keys, distant_valid):
    nearby_scores = jnp.einsum(
        "iyo,uyo->yiu", query_block, seg_keys, preferred_element_type=jnp.float32
    )
    nearby_scores = jnp.where(seg_valid[None, None, :], nearby_scores, -1000000000.0)
    far_scores = jnp.einsum(
        "iyo,uyo->yiu",
        query_block[::DILATION_STEP],
        distant_keys,
        preferred_element_type=jnp.float32,
    )
    far_scores = jnp.where(distant_valid[None, None, :], far_scores, -1000000000.0)
    return (nearby_scores, far_scores)


def block_forward(
    query_block, seg_keys, seg_values, seg_valid, distant_keys, distant_values, distant_valid
):
    nearby_scores, far_scores = block_scores(
        query_block, seg_keys, seg_valid, distant_keys, distant_valid
    )
    head_number = nearby_scores.shape[0]
    row_number = nearby_scores.shape[1]
    chosen_count = row_number // DILATION_STEP
    maximum_table = jnp.max(nearby_scores, axis=-1).reshape(
        head_number, chosen_count, DILATION_STEP
    )
    combined_top = jnp.maximum(maximum_table[:, :, 0], jnp.max(far_scores, axis=-1))
    row_maximum = maximum_table.at[:, :, 0].set(combined_top).reshape(head_number, row_number)
    nearby_exponent = jnp.exp(nearby_scores - row_maximum[:, :, None])
    far_exp = jnp.exp(far_scores - combined_top[:, :, None])
    exponent_sums = jnp.sum(nearby_exponent, axis=-1).reshape(
        head_number, chosen_count, DILATION_STEP
    )
    combined_total = exponent_sums[:, :, 0] + jnp.sum(far_exp, axis=-1)
    row_sum_total = exponent_sums.at[:, :, 0].set(combined_total).reshape(head_number, row_number)
    local_weights = (nearby_exponent / row_sum_total[:, :, None]).astype(jnp.bfloat16)
    far_weights = (far_exp / combined_total[:, :, None]).astype(jnp.bfloat16)
    attended_rows = jnp.einsum(
        "hqk,khd->qhd", local_weights, seg_values, preferred_element_type=jnp.float32
    )
    distant_attended = jnp.einsum(
        "hqk,khd->qhd", far_weights, distant_values, preferred_element_type=jnp.float32
    )
    attended_rows = (
        attended_rows.reshape(chosen_count, DILATION_STEP, head_number, HEAD_WIDTH)
        .at[:, 0]
        .add(distant_attended)
    )
    return (attended_rows.reshape(row_number, head_number, HEAD_WIDTH), row_maximum, row_sum_total)


def block_backward(
    query_block,
    seg_keys,
    seg_values,
    seg_valid,
    distant_keys,
    distant_values,
    distant_valid,
    gradient_block,
    row_maximum,
    row_sum_total,
):
    nearby_scores, far_scores = block_scores(
        query_block, seg_keys, seg_valid, distant_keys, distant_valid
    )
    head_number = row_maximum.shape[0]
    row_number = row_maximum.shape[1]
    chosen_count = row_number // DILATION_STEP
    combined_top = row_maximum.reshape(head_number, chosen_count, DILATION_STEP)[:, :, 0]
    combined_total = row_sum_total.reshape(head_number, chosen_count, DILATION_STEP)[:, :, 0]
    nearby_probability = (
        jnp.exp(nearby_scores - row_maximum[:, :, None]) / row_sum_total[:, :, None]
    )
    far_prob = jnp.exp(far_scores - combined_top[:, :, None]) / combined_total[:, :, None]
    local_weights = nearby_probability.astype(jnp.bfloat16)
    gradient_sampled = gradient_block[::DILATION_STEP]
    value_grad = jnp.einsum(
        "mns,nmg->smg", local_weights, gradient_block, preferred_element_type=jnp.float32
    )
    nearby_dots = jnp.einsum(
        "iyo,uyo->yiu", gradient_block, seg_values, preferred_element_type=jnp.float32
    )
    far_dots = jnp.einsum(
        "iyo,uyo->yiu", gradient_sampled, distant_values, preferred_element_type=jnp.float32
    )
    delta_table = jnp.sum(nearby_probability * nearby_dots, axis=-1).reshape(
        head_number, chosen_count, DILATION_STEP
    )
    joint_delta = delta_table[:, :, 0] + jnp.sum(far_prob * far_dots, axis=-1)
    row_delta = delta_table.at[:, :, 0].set(joint_delta).reshape(head_number, row_number)
    local_slope = (nearby_probability * (nearby_dots - row_delta[:, :, None])).astype(jnp.bfloat16)
    distant_slope = (far_prob * (far_dots - joint_delta[:, :, None])).astype(jnp.bfloat16)
    query_gradient = jnp.einsum(
        "hqk,khd->qhd", local_slope, seg_keys, preferred_element_type=jnp.float32
    )
    distant_query = jnp.einsum(
        "hqk,khd->qhd", distant_slope, distant_keys, preferred_element_type=jnp.float32
    )
    query_gradient = (
        query_gradient.reshape(chosen_count, DILATION_STEP, head_number, HEAD_WIDTH)
        .at[:, 0]
        .add(distant_query)
    )
    key_grad = jnp.einsum(
        "mns,nmg->smg", local_slope, query_block, preferred_element_type=jnp.float32
    )
    far_weights = far_prob.astype(jnp.bfloat16)
    far_value_grad = jnp.einsum(
        "mns,nmg->smg", far_weights, gradient_sampled, preferred_element_type=jnp.float32
    )
    far_key_grad = jnp.einsum(
        "mns,nmg->smg",
        distant_slope,
        query_block[::DILATION_STEP],
        preferred_element_type=jnp.float32,
    )
    return (
        query_gradient.reshape(row_number, head_number, HEAD_WIDTH),
        key_grad,
        value_grad,
        far_key_grad,
        far_value_grad,
    )


def plain_device(
    tokens,
    qkv_weight,
    out_weight,
    up_weight,
    down_weight,
    norm1_gain,
    norm1_bias,
    norm2_gain,
    norm2_bias,
    visible,
    cotangent,
):
    row_number = tokens.shape[1]
    embedding_width = tokens.shape[2]
    query_scale = HEAD_WIDTH ** (-0.5)
    first_row = lax.axis_index("seq") * row_number
    positions = first_row + jnp.arange(row_number, dtype=jnp.int32)
    row_validity = positions < visible[0]
    inputs = tokens[0].astype(jnp.float32)
    norm_one, pull_one = jax.vjp(layer_norm, inputs, norm1_gain, norm1_bias)
    normed = norm_one.astype(jnp.bfloat16)
    projected = jnp.dot(normed, qkv_weight, preferred_element_type=jnp.float32)
    query_rows = (
        (projected[:, :embedding_width] * query_scale)
        .astype(jnp.bfloat16)
        .reshape(row_number, HEADS, HEAD_WIDTH)
    )
    flat_keys = projected[:, embedding_width : 2 * embedding_width].astype(jnp.bfloat16)
    flat_values = projected[:, 2 * embedding_width :].astype(jnp.bfloat16)
    key_matrix = flat_keys.reshape(row_number, HEADS, HEAD_WIDTH)
    value_matrix = flat_values.reshape(row_number, HEADS, HEAD_WIDTH)
    gathered_keys, gathered_values = (
        lax.all_gather(flat_keys[::DILATION_STEP], "seq", axis=0, tiled=True),
        lax.all_gather(flat_values[::DILATION_STEP], "seq", axis=0, tiled=True),
    )
    distant_count = gathered_keys.shape[0]
    distant_valid = jnp.arange(distant_count, dtype=jnp.int32) * DILATION_STEP < visible[0]
    distant_keys = gathered_keys.reshape(distant_count, HEADS, HEAD_WIDTH)
    distant_values = gathered_values.reshape(distant_count, HEADS, HEAD_WIDTH)
    per_segment = SEG // QB
    attended_rows, row_maximum, row_sum_total = block_forward(
        query_rows,
        key_matrix,
        value_matrix,
        row_validity,
        distant_keys,
        distant_values,
        distant_valid,
    )
    attn_low = attended_rows.reshape(row_number, embedding_width).astype(jnp.bfloat16)
    after_attn = inputs + jnp.dot(attn_low, out_weight, preferred_element_type=jnp.float32)
    norm_two, pull_two = jax.vjp(layer_norm, after_attn, norm2_gain, norm2_bias)
    normed_two = norm_two.astype(jnp.bfloat16)
    up_cols = jnp.dot(normed_two, up_weight, preferred_element_type=jnp.float32)
    activated, pull_gelu = jax.vjp(exact_gelu, up_cols)
    hidden = activated.astype(jnp.bfloat16)
    result = after_attn + jnp.dot(hidden, down_weight, preferred_element_type=jnp.float32)
    mixed_out = jnp.where(row_validity[:, None], result, 0.0).astype(jnp.bfloat16)[None]
    grad_out = jnp.where(row_validity[:, None], cotangent[0], jnp.zeros_like(cotangent[0]))
    down_grad = jnp.einsum("tf,td->fd", hidden, grad_out, preferred_element_type=jnp.float32)
    hidden_grad = jnp.einsum("td,fd->tf", grad_out, down_weight, preferred_element_type=jnp.float32)
    (up_slope,) = pull_gelu(hidden_grad)
    up_low = up_slope.astype(jnp.bfloat16)
    up_grad = jnp.einsum("td,tf->df", normed_two, up_low, preferred_element_type=jnp.float32)
    norm_two_in = jnp.einsum("tf,df->td", up_low, up_weight, preferred_element_type=jnp.float32)
    after_part, gain_two_grad, shift_two_grad = pull_two(norm_two_in)
    resid_grad = grad_out.astype(jnp.float32) + after_part
    resid_low = resid_grad.astype(jnp.bfloat16)
    out_grad = jnp.einsum("td,te->de", attn_low, resid_low, preferred_element_type=jnp.float32)
    attn_grad = jnp.einsum("te,de->td", resid_low, out_weight, preferred_element_type=jnp.float32)
    attn_grad = attn_grad.astype(jnp.bfloat16).reshape(row_number, HEADS, HEAD_WIDTH)
    query_gradient, key_grad, value_grad, far_key_grad, far_value_grad = block_backward(
        query_rows,
        key_matrix,
        value_matrix,
        row_validity,
        distant_keys,
        distant_values,
        distant_valid,
        attn_grad,
        row_maximum,
        row_sum_total,
    )
    key_list = [key_grad]
    value_list = [value_grad]
    owned_keys, owned_values = (
        lax.psum_scatter(
            far_key_grad.reshape(distant_count, embedding_width),
            "seq",
            scatter_dimension=0,
            tiled=True,
        ),
        lax.psum_scatter(
            far_value_grad.reshape(distant_count, embedding_width),
            "seq",
            scatter_dimension=0,
            tiled=True,
        ),
    )
    chosen_count = row_number // DILATION_STEP
    segment_count = row_number // SEG
    nearby_keys = jnp.sum(
        jnp.stack(key_list).reshape(segment_count, per_segment, SEG, embedding_width), axis=1
    )
    nearby_values = jnp.sum(
        jnp.stack(value_list).reshape(segment_count, per_segment, SEG, embedding_width), axis=1
    )
    key_total = (
        nearby_keys.reshape(chosen_count, DILATION_STEP, embedding_width)
        .at[:, 0]
        .add(owned_keys)
        .reshape(row_number, embedding_width)
    )
    value_total = (
        nearby_values.reshape(chosen_count, DILATION_STEP, embedding_width)
        .at[:, 0]
        .add(owned_values)
        .reshape(row_number, embedding_width)
    )
    query_total = query_gradient.reshape(row_number, embedding_width)
    mixed_grad = jnp.concatenate(
        [
            (query_total * query_scale).astype(jnp.bfloat16),
            key_total.astype(jnp.bfloat16),
            value_total.astype(jnp.bfloat16),
        ],
        axis=1,
    )
    qkv_grad = jnp.einsum("td,tf->df", normed, mixed_grad, preferred_element_type=jnp.float32)
    norm_one_in = jnp.einsum(
        "tf,df->td", mixed_grad, qkv_weight, preferred_element_type=jnp.float32
    )
    input_part, gain_one_grad, shift_one_grad = pull_one(norm_one_in)
    tokens_grad = (resid_grad + input_part).astype(jnp.bfloat16)[None]
    weight_grads = (qkv_grad, out_grad, up_grad, down_grad)
    row_parts = (
        lax.psum_scatter(weight_grads[0], "seq", scatter_dimension=0, tiled=True),
        lax.psum_scatter(weight_grads[1], "seq", scatter_dimension=0, tiled=True),
        lax.psum_scatter(weight_grads[2], "seq", scatter_dimension=0, tiled=True),
        lax.psum_scatter(weight_grads[3], "seq", scatter_dimension=0, tiled=True),
    )
    final_grads = (
        lax.psum(row_parts[0].astype(jnp.bfloat16), "slide").astype(jnp.float32),
        lax.psum(row_parts[1].astype(jnp.bfloat16), "slide").astype(jnp.float32),
        lax.psum(row_parts[2].astype(jnp.bfloat16), "slide").astype(jnp.float32),
        lax.psum(row_parts[3].astype(jnp.bfloat16), "slide").astype(jnp.float32),
    )
    norm_grads = lax.psum(
        (gain_one_grad, shift_one_grad, gain_two_grad, shift_two_grad), ("seq", "slide")
    )
    return (
        mixed_out,
        tokens_grad,
        final_grads[0],
        final_grads[1],
        final_grads[2],
        final_grads[3],
        norm_grads[0],
        norm_grads[1],
        norm_grads[2],
        norm_grads[3],
    )


MESH = pl.DeviceIdType.MESH
LOW = jnp.bfloat16
FULL = jnp.float32
AUG = 64
LANES = 128
NEVER = -1000000000.0
ANY = pl.BlockSpec(memory_space=pl.ANY)
VMEM = pl.BlockSpec(memory_space=pltpu.VMEM)
SMEM = pl.BlockSpec(memory_space=pltpu.SMEM)


def nn(left, right):
    return jnp.dot(left, right, preferred_element_type=FULL)


def nt(left, right):
    return lax.dot_general(left, right, (((1,), (1,)), ((), ())), preferred_element_type=FULL)


def tn(left, right):
    return lax.dot_general(left, right, (((0,), (0,)), ((), ())), preferred_element_type=FULL)


def remote(src, dst, send_sem, recv_sem, device):
    return pltpu.make_async_remote_copy(
        src_ref=src,
        dst_ref=dst,
        send_sem=send_sem,
        recv_sem=recv_sem,
        device_id=device,
        device_id_type=MESH,
    )


def greet(devices):
    barrier = pltpu.get_barrier_semaphore()
    for device in devices:
        pl.semaphore_signal(barrier, inc=1, device_id=device, device_id_type=MESH)
    pl.semaphore_wait(barrier, len(devices))


def row_peers(count):
    seq, slide = lax.axis_index("seq"), lax.axis_index("slide")
    return [(lax.rem(seq + step, count), slide) for step in range(1, count)]


def spread(ref, values):
    for group in range(ref.shape[0]):
        ref[group] = values[:, group * LANES : (group + 1) * LANES]


def strided_rows(ref, step, count):
    groups = [
        ref[group, pl.ds(step, count, stride=DILATION_STEP), :] for group in range(ref.shape[0])
    ]
    return jnp.concatenate(groups, axis=1)


def strided_store(ref, step, count, values):
    for group in range(ref.shape[0]):
        ref[group, pl.ds(step, count, stride=DILATION_STEP), :] = values[
            :, group * LANES : (group + 1) * LANES
        ]


def chunk(step, size):
    return pl.ds(pl.multiple_of(step * size, size), size)


def steps(body):
    @pl.loop(0, DILATION_STEP // 4)
    def _(group):
        for member in range(4):
            body(group * 4 + member)


def row_mean(values):
    return jnp.mean(values, axis=-1, keepdims=True)


def fold_rows(values):
    return jnp.sum(values.reshape(-1, 8, values.shape[-1]), axis=0)


def mask_rows(ref, bias):
    first = lax.broadcasted_iota(jnp.int32, (AUG - HEAD_WIDTH, ref.shape[2]), 0) == 0
    ref[:, HEAD_WIDTH:, :] = jnp.broadcast_to(
        jnp.where(first, bias, 0.0).astype(LOW), (HEADS, AUG - HEAD_WIDTH, ref.shape[2])
    )


class Place:
    def __init__(self):
        seq, slide = lax.axis_index("seq"), lax.axis_index("slide")
        self.seq, self.slide = seq, slide
        self.z, self.x = seq // 2, seq % 2
        self.y, self.c = slide // 2, slide % 2
        self.sibling = (seq, slide + 1 - 2 * self.c)
        self.across_y = (seq, slide + 2 - 4 * self.y)
        self.diagonal = (seq, 3 - slide)
        self.across_x = (seq + 1 - 2 * self.x, slide)
        self.slide_peers = (self.sibling, self.across_y, self.diagonal)

    def layer(self, step):
        return (self.z + step) % 4


class Part:
    def __init__(self, place, orders, both, core_got, got, final, send_sem, recv_sem):
        self.place, self.orders, self.both = place, orders, both
        self.core_got, self.got, self.final = core_got, got, final
        self.send_sem, self.recv_sem = send_sem, recv_sem

    def blocks(self, core, phase, value):
        order = self.orders[core]
        choices = {}
        for at, name in enumerate(order, 1):
            if at < phase:
                choices[name] = [getattr(self.place, name)]
            elif at == phase:
                choices[name] = [value]
            else:
                choices[name] = list(range(4 if name == "z" else 2))
        return [(2 * z + x, y) for z in choices["z"] for x in choices["x"] for y in choices["y"]]

    def partners(self, core, phase):
        place, name = self.place, self.orders[core][phase - 1]
        if name == "x":
            return [(1 - place.x, place.across_x)]
        if name == "y":
            return [(1 - place.y, place.across_y)]
        layers = [place.layer(k) for k in (1, 2, 3)]
        return [(z, (2 * z + place.x, place.slide)) for z in layers]

    def span(self, core, phase):
        first, left = 0, 16
        for at, name in enumerate(self.orders[core], 1):
            left //= 4 if name == "z" else 2
            number = left * (3 if name == "z" else 1)
            if at == phase:
                return first, number
            first += number

    def transfers(self, core, phase):
        kept, got = self.both.at[0], self.got
        slot = self.span(core, phase)[0]
        pairs = "y" in self.orders[core][phase:]
        moves = []
        for value, device in self.partners(core, phase):
            for owner, y in self.blocks(core, phase, value):
                if not pairs:
                    moves.append((kept.at[owner, y], got.at[slot], device))
                elif y == 0:
                    moves.append((kept.at[owner], got.at[pl.ds(slot, 2)], device))
                slot += 1
        return moves

    def start(self, phase, merged):
        place, send, recv = self.place, self.send_sem.at[phase], self.recv_sem.at[phase]
        if phase == 0:
            remote(self.both.at[1], self.core_got, send, recv, place.sibling).start()
        elif phase <= 3:
            for core in range(2):

                @pl.when(place.c == core)
                def _(core=core):
                    for source, target, device in self.transfers(core, phase):
                        remote(source, target, send, recv, device).start()
        elif phase == 4:
            own = self.final.at[place.c * 2 + place.y]
            for device in place.slide_peers if merged else (place.across_y,):
                remote(own, own, send, recv, device).start()
        else:
            own = self.final.at[pl.ds(place.c * 2, 2)]
            remote(own, own, send, recv, place.sibling).start()

    def wait(self, phase, whole):
        both_ways = remote(
            whole, whole, self.send_sem.at[phase], self.recv_sem.at[phase], self.place.sibling
        )
        both_ways.wait_recv()
        both_ways.wait_send()

    def finish(self, phase, merged):
        place = self.place
        if phase == 0:
            self.wait(phase, self.core_got)

            @pl.loop(0, 8)
            def _(owner):
                for row in range(2):
                    self.both[0, owner, row] += self.core_got[owner, row]
        elif phase <= 3:
            for core in range(2):

                @pl.when(place.c == core)
                def _(core=core):
                    first, number = self.span(core, phase)
                    self.wait(phase, self.got.at[pl.ds(first, number)])
                    name = self.orders[core][phase - 1]
                    blocks = self.blocks(core, phase, getattr(place, name))
                    for n, (owner, y) in enumerate(blocks):
                        slots = range(first + n, first + number, len(blocks))
                        self.add(owner, y, slots, core if phase == 3 else None)
        elif phase == 4:
            self.wait(phase, self.final.at[pl.ds(0, 3 if merged else 1)])
        else:
            self.wait(phase, self.final.at[pl.ds(0, 2)])

    def add(self, owner, y, slots, core):
        if len(slots) == 1:
            total = self.both[0, owner, y] + self.got[slots[0]]
        else:
            total = self.both[0, owner, y].astype(FULL)
            for slot in slots:
                total = total + self.got[slot].astype(FULL)
            total = total.astype(LOW)
        if core is None:
            self.both[0, owner, y] = total
        else:
            self.final[core * 2 + self.place.y] = total


class Piece:
    def __init__(self, parts, merged, outs, out_sem):
        self.parts, self.merged, self.outs, self.out_sem = parts, merged, outs, out_sem
        self.last = 4 if merged else 5
        self.phase = -1

    @property
    def done(self):
        return self.phase > self.last

    def advance(self):
        if self.done:
            return
        if self.phase >= 0:
            for part in self.parts:
                part.finish(self.phase, self.merged)
        self.phase += 1
        if not self.done:
            for part in self.parts:
                part.start(self.phase, self.merged)
            return
        for n in range(len(self.parts)):
            self.out_copy(n).start()

    def out_copy(self, n):
        return pltpu.make_async_copy(self.parts[n].final, self.outs[n], self.out_sem.at[n])


TILES = 3
LASTS = 4
PIECES = TILES + LASTS
ORDERS = (
    ("xyz", "zxy"),
    ("yxz", "xzy"),
    ("yxz", "xyz"),
    ("zxy", "yxz"),
    ("xyz", "yxz"),
    ("yxz", "yxz"),
    ("xyz", "xyz"),
)
HOOKS = {
    "tile1.1": (0,),
    "tile2.1": (1,),
    "after2": (2,),
    "far": (1,),
    "near0": (0,),
    "near4": (3,),
    "near5": (1, 2, 4),
    "near6": (0,),
    "into": (3, 5, 6),
    "norm": (1, 2, 4),
}
TAIL = (3, 0, 6, 5, 1, 4, 2, 1, 3, 0, 5, 0, 6, 4, 2, 3, 5, 2, 4, 6, 5, 6)

def main_kernel(
    count, tokens, cotangent, qkv_weight, out_weight, up_weight, down_weight,
    gain_one, shift_one, gain_two, shift_two, visible,
    mixed_out, tokens_out, down_sums, up_sums, last_sums, norm_out, weights_kept, norm_kept,
    normed, far_normed, query, key, value, far_key, far_value, far_weights, scale, far_scale, attn,
    delta, slope, resid, after, dyb, wqkv, wo, wide, staged, all_far, far_got, spread_one,
    sums, around, across,
    down_both, up_both, last_both, down_core, up_core, last_core,
    down_got, up_got, last_got, down_final, up_final, last_final,
    load_sem, tile_sem, group_sem, store_sem, out_sem, send_sem, recv_sem,
    gather_send_sem, gather_recv_sem, far_send_sem, far_recv_sem, norm_send_sem, norm_recv_sem,
):
    place = Place()
    seq, core = place.seq, place.c
    rows, width = resid.shape
    chosen = rows // DILATION_STEP
    group_lanes = LANES
    tile_width = count * group_lanes
    first_row = seq * rows
    limit = visible[0]
    peers = row_peers(count)
    others = list(place.slide_peers) + peers
    barrier = pltpu.get_barrier_semaphore()
    for other in others:
        pl.semaphore_signal(barrier, inc=1, device_id=other, device_id_type=MESH)

    def valid_rows(step):
        places = lax.broadcasted_iota(jnp.int32, (chosen, 1), 0) * DILATION_STEP + step
        return first_row + places < limit

    def landed(n):
        sources = (
            (tokens, staged),
            (qkv_weight.at[:, pl.ds(width, width)], wqkv.at[1]),
            (qkv_weight.at[:, pl.ds(2 * width, width)], wqkv.at[2]),
            (qkv_weight.at[:, pl.ds(0, width)], wqkv.at[0]),
            (out_weight, wo),
            (cotangent, staged),
        )
        return pltpu.make_async_copy(*sources[n], load_sem.at[n])

    for n in range(5):
        landed(n).start()
    distant = count * chosen
    members = 4

    def kept_group(group, slots):
        kept = weights_kept.at[pl.ds(group * members, members)]
        return slots.at[group % 2], kept, group_sem.at[group % 2]

    pieces = []
    for n in range(TILES):
        parts = [
            Part(
                place,
                ORDERS[n],
                both.at[n],
                core_got.at[n],
                got.at[n],
                final.at[n],
                send_sem.at[n, which],
                recv_sem.at[n, which],
            )
            for which, (both, core_got, got, final) in enumerate(
                (
                    (down_both, down_core, down_got, down_final),
                    (up_both, up_core, up_got, up_final),
                )
            )
        ]
        pieces.append(Piece(parts, False, (down_sums.at[n], up_sums.at[n]), out_sem.at[n]))
    for n in range(LASTS):
        part = Part(
            place,
            ORDERS[TILES + n],
            last_both.at[n],
            last_core.at[n],
            last_got.at[n],
            last_final.at[n],
            send_sem.at[TILES + n, 0],
            recv_sem.at[TILES + n, 0],
        )
        pieces.append(Piece([part], True, (last_sums.at[n],), out_sem.at[TILES + n]))

    def hook(name):
        for n in HOOKS.get(name, ()):
            if pieces[n].phase >= 0:
                pieces[n].advance()

    def split_last(n, side, grads):
        target = last_both.at[n, (side + core) % 2]
        target[...] = grads.astype(LOW).reshape(count, 2, -1, grads.shape[1])

    def attend_part(h1, top, total, attended, weights):
        landed(0).wait()
        spread(wide, staged[...].astype(FULL))
        landed(5).start()

        def normalize(step):
            at = chunk(step, chosen)
            values = strided_rows(wide, step, chosen)
            centered = values - row_mean(values)
            inverse = lax.rsqrt(row_mean(centered * centered) + epsilon)
            normal = centered * inverse
            after[at] = values
            resid[at] = normal
            spread_one[at] = jnp.broadcast_to(inverse, (chosen, LANES))
            low = (normal * gain_one[...][None] + shift_one[...][None]).astype(LOW)
            h1[at] = low
            return low

        all_far[seq] = normalize(0)

        @pl.loop(0, 5)
        def _(group):
            for member in range(3):
                normalize(group * 3 + member + 1)

        pltpu.make_async_copy(resid, norm_kept, store_sem.at[0]).start()
        for part, ref in ((1, key), (2, value)):
            landed(part).wait()
            projected = nn(h1[...], wqkv[part]).astype(LOW)
            ref[:, :HEAD_WIDTH, :] = projected.T.reshape(HEADS, HEAD_WIDTH, rows)
            if part == 1:
                pl.semaphore_wait(barrier, len(others))
                for n, peer in enumerate(peers):
                    mine = all_far.at[seq]
                    send, recv = gather_send_sem.at[n], gather_recv_sem.at[n]
                    remote(mine, mine, send, recv, peer).start()
        landed(3).wait()
        projected = (nn(h1[...], wqkv[0]) * HEAD_WIDTH ** (-0.5)).astype(LOW)
        query[:, :HEAD_WIDTH, :] = projected.T.reshape(HEADS, HEAD_WIDTH, rows)
        places = lax.broadcasted_iota(jnp.int32, (1, rows), 1)
        places = first_row + (places % chosen) * DILATION_STEP + places // chosen
        mask_rows(key, jnp.where(places < limit, 0.0, NEVER))
        mask_rows(query, jnp.ones((1, rows), FULL))

        @pl.loop(0, HEADS // members)
        def _(group):
            slot, kept, sem = kept_group(group, weights)

            @pl.when(group >= 2)
            def _():
                pltpu.make_async_copy(slot, kept, sem).wait()

            for member in range(members):
                head = group * members + member
                scores = tn(key[head], query[head])
                highest = jnp.max(scores, axis=0, keepdims=True)
                exponent = jnp.exp(scores - highest)
                top[head] = highest
                total[head] = jnp.sum(exponent, axis=0, keepdims=True)
                low = exponent.astype(LOW)
                weights[group % 2, member] = low
                attended[head] = nn(value[head], low)
            pltpu.make_async_copy(slot, kept, sem).start()

        normed[...] = h1[...].T
        landed(5).wait()
        spread(wide, staged[...].astype(FULL))

        @steps
        def _(step):
            at = chunk(step, chosen)
            dyb[at] = jnp.where(valid_rows(step), strided_rows(wide, step, chosen), 0.0).astype(LOW)

        for n in range(count - 1):
            source = lax.rem(seq + count - 1 - n, count)
            mine, theirs = all_far.at[seq], all_far.at[source]
            wait = remote(mine, theirs, gather_send_sem.at[n], gather_recv_sem.at[n], peers[0])
            wait.wait_recv()
            wait.wait_send()
        flat = all_far[...].reshape(distant, width)
        for part, ref in ((1, far_key), (2, far_value)):
            projected = nn(flat, wqkv[part]).astype(LOW)
            ref[:, :HEAD_WIDTH, :] = projected.T.reshape(HEADS, HEAD_WIDTH, distant)
        places = lax.broadcasted_iota(jnp.int32, (1, distant), 1) * DILATION_STEP
        mask_rows(far_key, jnp.where(places < limit, 0.0, NEVER))
        lane_mask = jnp.where(lax.broadcasted_iota(jnp.int32, (1, LANES), 1) < chosen, 0.0, NEVER)

        @pl.loop(0, HEADS // 4)
        def _(group):
            for member in range(4):
                head = group * 4 + member
                scores = tn(far_key[head], query[head][:, :LANES]) + lane_mask
                highest = jnp.max(scores, axis=0, keepdims=True)
                exponent = jnp.exp(scores - highest)
                low = exponent.astype(LOW)
                far_weights[head] = low
                near = top[head][:, :LANES]
                joint = jnp.maximum(near, highest)
                near_part, far_part = jnp.exp(near - joint), jnp.exp(highest - joint)
                joint_total = total[head][:, :LANES] * near_part + far_part * jnp.sum(
                    exponent, axis=0, keepdims=True
                )
                near_part, far_part = near_part / joint_total, far_part / joint_total
                far_scale[head] = far_part
                local = jnp.concatenate([near_part, 1.0 / total[head][:, LANES:]], axis=1)
                scale[head] = local
                result = attended[head] * local
                with_far = result[:, :LANES] + nn(far_value[head], low) * far_part
                result = jnp.concatenate([with_far, result[:, LANES:]], axis=1)
                attn[head] = result.astype(LOW)

        for group in (2, 3):
            slot, kept, sem = kept_group(group, weights)
            pltpu.make_async_copy(slot, kept, sem).wait()
        pltpu.make_async_copy(resid, norm_kept, store_sem.at[0]).wait()

    vm = pltpu.VMEM
    pl.run_scoped(
        attend_part,
        vm((rows, width), LOW),
        vm((HEADS, 1, rows), FULL),
        vm((HEADS, 1, rows), FULL),
        vm((HEADS, HEAD_WIDTH, rows), FULL),
        vm((2, members, rows, rows), LOW),
    )

    def forward_part(norm_two, spread_two, h2, h2_t, active, low_slope, wup, wdown):
        halves = 2
        per_half = tile_width // halves

        def load_tile(tile, half):
            for local in range(count // halves):
                owner = half * (count // halves) + local
                first = owner * TILES * group_lanes + tile * group_lanes
                at = pl.ds(pl.multiple_of(first, LANES), group_lanes)
                to = pl.ds(local * group_lanes, group_lanes)
                pltpu.make_async_copy(
                    up_weight.at[:, at], wup.at[half, :, to], tile_sem.at[half, 0]
                ).start()
                pltpu.make_async_copy(
                    down_weight.at[at], wdown.at[half, to], tile_sem.at[half, 1]
                ).start()

        def wait_tile(half):
            pltpu.make_async_copy(wup.at[half], wup.at[half], tile_sem.at[half, 0]).wait()
            pltpu.make_async_copy(wdown.at[half], wdown.at[half], tile_sem.at[half, 1]).wait()

        load_tile(0, 0)
        load_tile(0, 1)
        landed(4).wait()
        after[...] += nn(attn[...].reshape(width, rows).T, wo[...])

        @steps
        def _(step):
            at = chunk(step, chosen)
            values = after[at]
            centered = values - row_mean(values)
            inverse = lax.rsqrt(row_mean(centered * centered) + epsilon)
            normal = centered * inverse
            norm_two[at] = normal
            spread_two[at] = jnp.broadcast_to(inverse, (chosen, LANES))
            h2[at] = (normal * gain_two[...][None] + shift_two[...][None]).astype(LOW)
            resid[at] = jnp.zeros((chosen, width), FULL)

        h2_t[...] = h2[...].T
        for tile in range(TILES):
            @pl.loop(0, halves)
            def _(half, tile=tile):
                wait_tile(half)
                for part in range(2):
                    at = slice(part * per_half // 2, (part + 1) * per_half // 2)
                    to = pl.ds(
                        pl.multiple_of(half * per_half + part * per_half // 2, LANES), per_half // 2
                    )
                    hidden = nn(h2[...], wup[half, :, at])
                    hidden_slope = nt(dyb[...], wdown[half, at])
                    share = 0.5 * (1.0 + lax.erf(hidden * 0.7071067811865476))
                    active[:, to] = (hidden * share).astype(LOW)
                    density = hidden * jnp.exp(-0.5 * hidden * hidden) * 0.3989422804014327
                    low_slope[:, to] = (hidden_slope * (share + density)).astype(LOW)
                to = pl.ds(pl.multiple_of(half * per_half, LANES), per_half)
                after[...] += nn(active[:, to], wdown[half])
                resid[...] += nt(low_slope[:, to], wup[half])
                if tile + 1 < TILES:
                    load_tile(tile + 1, half)

            hook("tile%d.1" % tile)

            @pl.loop(0, 4)
            def _(part, tile=tile):
                at = pl.ds(pl.multiple_of(part * tile_width // 4, LANES), tile_width // 4)
                grads = nn(h2_t[...], low_slope[:, at]).astype(LOW)
                target = up_both.at[tile, (part // 2 + core) % 2]
                target[:, part % 2] = grads.reshape(count, -1, grads.shape[1])
                grads = tn(active[:, at], dyb[...]).astype(LOW)
                owners = count // 4
                grads = grads.reshape(owners, 2, 2, -1, width)
                for side in range(2):
                    target = down_both.at[tile, (side + core) % 2]
                    target[pl.ds(part * owners, owners)] = grads[:, side]

            pieces[tile].advance()
            hook("tile%d.3" % tile)
        sums[...] = jnp.zeros_like(sums)
        hook("after0")

        @steps
        def _(step):
            at = chunk(step, chosen)
            strided_store(wide, step, chosen, jnp.where(valid_rows(step), after[at], 0.0))
            given, normal = resid[at], norm_two[at]
            sums[2] += fold_rows(given * normal)
            sums[3] += fold_rows(given)
            scaled = given * gain_two[...][None]
            part = scaled - row_mean(scaled) - normal * row_mean(scaled * normal)
            value_here = dyb[at].astype(FULL) + spread_two[at][:, :1] * part
            resid[at] = value_here
            h2[at] = value_here.astype(LOW)

        for group in range(width // LANES):
            staged[:, group * LANES : (group + 1) * LANES] = wide[group].astype(LOW)
        pltpu.make_async_copy(staged, mixed_out, store_sem.at[1]).start()
        half = width // 2
        hook("after1")
        for n in range(2):
            at = slice(n * half, (n + 1) * half)
            split_last(2 * n + 1, 1, nn(attn[...].reshape(width, rows), h2[:, at]))
        slope[...] = nt(wo[...], h2[...]).astype(LOW).reshape(HEADS, HEAD_WIDTH, rows)

        @pl.loop(0, HEADS)
        def _(head):
            product = slope[head].astype(FULL) * attn[head].astype(FULL)
            delta[head] = jnp.sum(product, axis=0, keepdims=True)

        hook("after2")

    pl.run_scoped(
        forward_part,
        vm((rows, width), FULL),
        vm((rows, LANES), FULL),
        vm((rows, width), LOW),
        vm((width, rows), LOW),
        vm((rows, tile_width), LOW),
        vm((rows, tile_width), LOW),
        vm((2, width, tile_width // 2), LOW),
        vm((2, tile_width // 2, width), LOW),
    )

    def backward_part(weights, slopes, far_query, far_send, given):
        norm_one = after

        def load_group(group):
            slot, kept, sem = kept_group(group, weights)
            return pltpu.make_async_copy(kept, slot, sem)

        load_group(0).start()
        load_group(1).start()
        norm_load = pltpu.make_async_copy(norm_kept, norm_one, store_sem.at[0])
        norm_load.start()

        @pl.loop(0, HEADS // 4)
        def _(group):
            for member in range(4):
                head = group * 4 + member
                first_slope = slope[head][:, :LANES]
                low = far_weights[head]
                change = tn(far_value[head], first_slope) - delta[head][:, :LANES]
                score_slope = (low.astype(FULL) * far_scale[head] * change).astype(LOW)
                far_query[head] = nn(far_key[head, :HEAD_WIDTH], score_slope)
                scaled = (first_slope.astype(FULL) * far_scale[head]).astype(LOW)
                given[0, head] = nt(query[head, :HEAD_WIDTH, :LANES], score_slope).astype(LOW)
                given[1, head] = nt(scaled, low).astype(LOW)

        hook("far0")
        far_normed[...] = all_far[...].reshape(distant, width).T
        into = nn(wqkv[1], given[0].reshape(width, distant))
        into += nn(wqkv[2], given[1].reshape(width, distant))
        far_send[...] = into.T.astype(LOW).reshape(count, chosen, width)
        for n, peer in enumerate(peers):
            remote(
                far_send.at[peer[0]], far_got.at[n], far_send_sem.at[n], far_recv_sem.at[n], peer
            ).start()
        hook("far")

        def weight_slopes(half):
            at = slice(half * HEADS // 2, (half + 1) * HEADS // 2)
            for part, (n, side) in enumerate(((0, 0), (0, 1), (1, 0))):
                grads = nt(normed[...], slopes[part, at].reshape(width // 2, rows))
                if part:
                    far = given[part - 1, at].reshape(width // 2, distant)
                    grads += nt(far_normed[...], far)
                split_last(2 * half + n, side, grads)
                if part:
                    pieces[TILES + 2 * half + n].advance()
                    hook("last%d" % (2 * half + n))

        for group in range(HEADS // members):
            load_group(group).wait()
            for member in range(members):
                head = group * members + member
                low = weights[group % 2, member]
                change = tn(value[head], slope[head]) - delta[head]
                score_slope = (low.astype(FULL) * scale[head] * change).astype(LOW)
                query_slope = nn(key[head, :HEAD_WIDTH], score_slope)
                key_slope = nt(query[head, :HEAD_WIDTH], score_slope)
                scaled = (slope[head].astype(FULL) * scale[head]).astype(LOW)
                value_slope = nt(scaled, low)
                first = query_slope[:, :LANES] + far_query[head]
                query_slope = jnp.concatenate([first, query_slope[:, LANES:]], axis=1)
                slopes[0, head] = (query_slope * HEAD_WIDTH ** (-0.5)).astype(LOW)
                slopes[1, head] = key_slope.astype(LOW)
                slopes[2, head] = value_slope.astype(LOW)
                if member % 2:
                    hook("near%d" % (head // 2))
            if (group + 2) * members < HEADS:
                load_group(group + 2).start()
            if group % 2:
                weight_slopes(group // 2)

        def flat_slopes(part):
            return slopes[part].reshape(width, rows)

        into = nn(wqkv[0], flat_slopes(0))
        into += nn(wqkv[1], flat_slopes(1))
        into += nn(wqkv[2], flat_slopes(2))
        norm_load.wait()
        pltpu.make_async_copy(staged, mixed_out, store_sem.at[1]).wait()
        spread(wide, into.T)
        hook("into")
        total = far_send[seq].astype(FULL)
        for n in range(count - 1):
            wait = remote(
                far_got.at[n], far_got.at[n], far_send_sem.at[n], far_recv_sem.at[n], peers[0]
            )
            wait.wait_recv()
            wait.wait_send()
            total = total + far_got[n].astype(FULL)
        for group in range(width // LANES):
            wide[group, :chosen] += total[:, group * LANES : (group + 1) * LANES]

        @steps
        def _(step):
            at = chunk(step, chosen)
            here = jnp.concatenate([wide[group, at, :] for group in range(width // LANES)], axis=1)
            normal = norm_one[at]
            sums[0] += fold_rows(here * normal)
            sums[1] += fold_rows(here)
            scaled = here * gain_one[...][None]
            part = scaled - row_mean(scaled) - normal * row_mean(scaled * normal)
            resid[at] += spread_one[at][:, :1] * part

    pl.run_scoped(
        backward_part,
        vm((2, members, rows, rows), LOW),
        vm((3, HEADS, HEAD_WIDTH, rows), LOW),
        vm((HEADS, HEAD_WIDTH, LANES), FULL),
        vm((count, chosen, width), LOW),
        vm((2, HEADS, HEAD_WIDTH, distant), LOW),
    )
    for n in range(4):
        around[seq, pl.ds(n, 1)] = jnp.sum(sums[n], axis=0, keepdims=True)
    for n, peer in enumerate(peers):
        mine = around.at[seq]
        remote(mine, mine, norm_send_sem.at[n], norm_recv_sem.at[n], peer).start()
    hook("norm")

    @steps
    def _(step):
        strided_store(wide, step, chosen, resid[chunk(step, chosen)])

    for group in range(width // LANES):
        staged[:, group * LANES : (group + 1) * LANES] = wide[group].astype(LOW)
    tokens_copy = pltpu.make_async_copy(staged, tokens_out, store_sem.at[2])
    tokens_copy.start()
    for n in range(count - 1):
        mine = around.at[seq]
        wait = remote(mine, mine, norm_send_sem.at[n], norm_recv_sem.at[n], peers[0])
        wait.wait_recv()
        wait.wait_send()
    total = around[0]
    for n in range(1, count):
        total = total + around[n]
    across[place.slide] = total
    for n, peer in enumerate(place.slide_peers):
        mine, at = across.at[place.slide], count - 1 + n
        remote(mine, mine, norm_send_sem.at[at], norm_recv_sem.at[at], peer).start()
    for n in TAIL + tuple(range(PIECES)) * 6:
        pieces[n].advance()
    for n in range(3):
        mine, at = across.at[0], count - 1 + n
        wait = remote(mine, mine, norm_send_sem.at[at], norm_recv_sem.at[at], peers[0])
        wait.wait_recv()
        wait.wait_send()
    norm_out[...] = (across[0] + across[1]) + (across[2] + across[3])
    for piece in pieces:
        for n in range(len(piece.parts)):
            piece.out_copy(n).wait()
    tokens_copy.wait()


def main_pass(count, tokens, cotangent, weights, norms, visible):
    rows, width = tokens.shape
    chosen = rows // DILATION_STEP
    distant = count * chosen
    owned = width // count
    vm, dma = pltpu.VMEM, pltpu.SemaphoreType.DMA
    down_block, up_block = (LANES // 4, width), (owned, 2 * LANES)
    last_block = (owned // 2, width // 2)
    blocks = ((TILES, down_block), (TILES, up_block), (LASTS, last_block))
    low = [
        (width, rows), (width, distant), (HEADS, AUG, rows), (HEADS, AUG, rows),
        (HEADS, HEAD_WIDTH, rows), (HEADS, AUG, distant), (HEADS, HEAD_WIDTH, distant),
        (HEADS, distant, LANES),
    ]
    scratch = [vm(shape, LOW) for shape in low]
    scratch += [
        vm((HEADS, 1, rows), FULL),
        vm((HEADS, 1, LANES), FULL),
        vm((HEADS, HEAD_WIDTH, rows), LOW),
        vm((HEADS, 1, rows), FULL),
        vm((HEADS, HEAD_WIDTH, rows), LOW),
        vm((rows, width), FULL),
        vm((rows, width), FULL),
        vm((rows, width), LOW),
        vm((3, width, width), LOW),
        vm((width, width), LOW),
        vm((width // LANES, rows, LANES), FULL),
        vm((rows, width), LOW),
        vm((count, chosen, width), LOW),
        vm((count - 1, chosen, width), LOW),
        vm((rows, LANES), FULL),
        vm((4, 8, width), FULL),
        vm((count, 8, width), FULL),
        vm((4, 8, width), FULL),
    ]
    scratch += [vm((n, 2, count, 2) + block, LOW) for n, block in blocks]
    scratch += [vm((n, count, 2) + block, LOW) for n, block in blocks]
    scratch += [vm((n, 15) + block, LOW) for n, block in blocks]
    scratch += [vm((n, 4) + block, LOW) for n, block in blocks]
    scratch += [
        dma((6,)), dma((2, 2)), dma((2,)), dma((3,)), dma((PIECES, 2)),
        dma((PIECES, 2, 6)), dma((PIECES, 2, 6)),
        dma((count - 1,)), dma((count - 1,)), dma((count - 1,)), dma((count - 1,)),
        dma((count + 2,)), dma((count + 2,)),
    ]
    sums = [jax.ShapeDtypeStruct((n, 4) + block, LOW) for n, block in blocks]
    results = pl.pallas_call(
        functools.partial(main_kernel, count),
        out_shape=(
            jax.ShapeDtypeStruct((rows, width), LOW),
            jax.ShapeDtypeStruct((rows, width), LOW),
            *sums,
            jax.ShapeDtypeStruct((8, width), FULL),
            jax.ShapeDtypeStruct((HEADS, rows, rows), LOW),
            jax.ShapeDtypeStruct((rows, width), FULL),
        ),
        in_specs=[ANY] * 6 + [VMEM] * 4 + [SMEM],
        out_specs=(ANY, ANY, ANY, ANY, ANY, VMEM, ANY, ANY),
        scratch_shapes=scratch,
        compiler_params=pltpu.CompilerParams(
            collective_id=1, has_side_effects=True, vmem_limit_bytes=64 << 20
        ),
        name="main_pass",
    )(tokens, cotangent, *weights, *norms, visible)
    return results[:6]


def finish_kernel(
    mixed, tokens_grad, down_sums, up_sums, last_sums, norms,
    mixed_out, tokens_out, qkv_out, out_out, up_out, down_out, *norm_outs
):
    mixed_out[...] = mixed[...]
    tokens_out[...] = tokens_grad[...]
    tiles, blocks, rows, _ = down_sums.shape
    for tile in range(tiles):
        for block in range(blocks):
            first = (tile * blocks + block) * rows
            down_out[first : first + rows] = down_sums[tile, block].astype(FULL)
            for half in range(2):
                first = ((block * 2 + half) * tiles + tile) * LANES
                part = up_sums[tile, block][:, half * LANES : (half + 1) * LANES]
                up_out[:, first : first + LANES] = part.astype(FULL)
    rows, columns = last_sums.shape[2:]
    for piece in range(last_sums.shape[0]):
        half, pair = divmod(piece, 2)
        for block in range(blocks):
            side, row = divmod(block, 2)
            at = slice(row * rows, (row + 1) * rows)
            first = half * columns
            out = out_out
            if pair == 0 or side == 0:
                out, first = qkv_out, first + 2 * columns * (2 * pair + side)
            out[at, first : first + columns] = last_sums[piece, block].astype(FULL)
    for n, out in enumerate(norm_outs):
        out[...] = norms[n]


def finish_pass(count, results):
    rows, width = results[0].shape
    owned = width // count

    def full(*shape):
        return jax.ShapeDtypeStruct(shape, FULL)

    return pl.pallas_call(
        finish_kernel,
        out_shape=(
            jax.ShapeDtypeStruct((rows, width), LOW),
            jax.ShapeDtypeStruct((rows, width), LOW),
            full(owned, 3 * width),
            full(owned, width),
            full(owned, TILES * count * LANES),
            full(TILES * LANES, width),
            *[full(width)] * 4,
        ),
        in_specs=[VMEM] * 6,
        out_specs=tuple([VMEM] * 10),
        compiler_params=pltpu.CompilerParams(vmem_limit_bytes=63 << 20),
        name="finish_pass",
    )(*results)


def fused_device(
    tokens,
    qkv_weight,
    out_weight,
    up_weight,
    down_weight,
    norm1_gain,
    norm1_bias,
    norm2_gain,
    norm2_bias,
    visible,
    cotangent,
):
    count = lax.axis_size("seq")
    results = main_pass(
        count,
        tokens[0],
        cotangent[0],
        (qkv_weight, out_weight, up_weight, down_weight),
        (norm1_gain, norm1_bias, norm2_gain, norm2_bias),
        visible,
    )
    mixed, tokens_grad, *grads = finish_pass(count, results)
    return (mixed[None], tokens_grad[None], *grads)


def solution(mesh):
    placed = (
        P("slide", "seq", None),
        P(),
        P(),
        P(),
        P(),
        P(),
        P(),
        P(),
        P(),
        P("slide"),
        P("slide", "seq", None),
    )
    fused = mesh.shape["seq"] == 8 and mesh.shape["slide"] == 4
    return jax.shard_map(
        fused_device if fused else plain_device,
        mesh=mesh,
        in_specs=placed,
        out_specs=(
            P("slide", "seq", None),
            P("slide", "seq", None),
            P("seq", None),
            P("seq", None),
            P("seq", None),
            P("seq", None),
            P(),
            P(),
            P(),
            P(),
        ),
        check_vma=False,
    )
```

```python
import functools

import jax
import jax.numpy as jnp
from jax import lax
from jax.experimental import pallas as pl
from jax.experimental.pallas import tpu as pltpu
from jax.sharding import PartitionSpec as P

HEADS = 16
HEAD_WIDTH = 48
SEG = 512
QB = 512
DILATION_STEP = 16


epsilon = 1e-05


def layer_norm(values, norm_gain, norm_shift):
    average = jnp.mean(values, axis=-1, keepdims=True)
    centered = values - average
    variance = jnp.mean(centered * centered, axis=-1, keepdims=True)
    return centered * lax.rsqrt(variance + epsilon) * norm_gain + norm_shift


def exact_gelu(values):
    return jax.nn.gelu(values, approximate=False)


def block_scores(query_block, seg_keys, seg_valid, distant_keys, distant_valid):
    nearby_scores = jnp.einsum(
        "iyo,uyo->yiu", query_block, seg_keys, preferred_element_type=jnp.float32
    )
    nearby_scores = jnp.where(seg_valid[None, None, :], nearby_scores, -1000000000.0)
    far_scores = jnp.einsum(
        "iyo,uyo->yiu",
        query_block[::DILATION_STEP],
        distant_keys,
        preferred_element_type=jnp.float32,
    )
    far_scores = jnp.where(distant_valid[None, None, :], far_scores, -1000000000.0)
    return (nearby_scores, far_scores)


def block_forward(
    query_block, seg_keys, seg_values, seg_valid, distant_keys, distant_values, distant_valid
):
    nearby_scores, far_scores = block_scores(
        query_block, seg_keys, seg_valid, distant_keys, distant_valid
    )
    head_number = nearby_scores.shape[0]
    row_number = nearby_scores.shape[1]
    chosen_count = row_number // DILATION_STEP
    maximum_table = jnp.max(nearby_scores, axis=-1).reshape(
        head_number, chosen_count, DILATION_STEP
    )
    combined_top = jnp.maximum(maximum_table[:, :, 0], jnp.max(far_scores, axis=-1))
    row_maximum = maximum_table.at[:, :, 0].set(combined_top).reshape(head_number, row_number)
    nearby_exponent = jnp.exp(nearby_scores - row_maximum[:, :, None])
    far_exp = jnp.exp(far_scores - combined_top[:, :, None])
    exponent_sums = jnp.sum(nearby_exponent, axis=-1).reshape(
        head_number, chosen_count, DILATION_STEP
    )
    combined_total = exponent_sums[:, :, 0] + jnp.sum(far_exp, axis=-1)
    row_sum_total = exponent_sums.at[:, :, 0].set(combined_total).reshape(head_number, row_number)
    local_weights = (nearby_exponent / row_sum_total[:, :, None]).astype(jnp.bfloat16)
    far_weights = (far_exp / combined_total[:, :, None]).astype(jnp.bfloat16)
    attended_rows = jnp.einsum(
        "hqk,khd->qhd", local_weights, seg_values, preferred_element_type=jnp.float32
    )
    distant_attended = jnp.einsum(
        "hqk,khd->qhd", far_weights, distant_values, preferred_element_type=jnp.float32
    )
    attended_rows = (
        attended_rows.reshape(chosen_count, DILATION_STEP, head_number, HEAD_WIDTH)
        .at[:, 0]
        .add(distant_attended)
    )
    return (attended_rows.reshape(row_number, head_number, HEAD_WIDTH), row_maximum, row_sum_total)


def block_backward(
    query_block,
    seg_keys,
    seg_values,
    seg_valid,
    distant_keys,
    distant_values,
    distant_valid,
    gradient_block,
    row_maximum,
    row_sum_total,
):
    nearby_scores, far_scores = block_scores(
        query_block, seg_keys, seg_valid, distant_keys, distant_valid
    )
    head_number = row_maximum.shape[0]
    row_number = row_maximum.shape[1]
    chosen_count = row_number // DILATION_STEP
    combined_top = row_maximum.reshape(head_number, chosen_count, DILATION_STEP)[:, :, 0]
    combined_total = row_sum_total.reshape(head_number, chosen_count, DILATION_STEP)[:, :, 0]
    nearby_probability = (
        jnp.exp(nearby_scores - row_maximum[:, :, None]) / row_sum_total[:, :, None]
    )
    far_prob = jnp.exp(far_scores - combined_top[:, :, None]) / combined_total[:, :, None]
    local_weights = nearby_probability.astype(jnp.bfloat16)
    gradient_sampled = gradient_block[::DILATION_STEP]
    value_grad = jnp.einsum(
        "mns,nmg->smg", local_weights, gradient_block, preferred_element_type=jnp.float32
    )
    nearby_dots = jnp.einsum(
        "iyo,uyo->yiu", gradient_block, seg_values, preferred_element_type=jnp.float32
    )
    far_dots = jnp.einsum(
        "iyo,uyo->yiu", gradient_sampled, distant_values, preferred_element_type=jnp.float32
    )
    delta_table = jnp.sum(nearby_probability * nearby_dots, axis=-1).reshape(
        head_number, chosen_count, DILATION_STEP
    )
    joint_delta = delta_table[:, :, 0] + jnp.sum(far_prob * far_dots, axis=-1)
    row_delta = delta_table.at[:, :, 0].set(joint_delta).reshape(head_number, row_number)
    local_slope = (nearby_probability * (nearby_dots - row_delta[:, :, None])).astype(jnp.bfloat16)
    distant_slope = (far_prob * (far_dots - joint_delta[:, :, None])).astype(jnp.bfloat16)
    query_gradient = jnp.einsum(
        "hqk,khd->qhd", local_slope, seg_keys, preferred_element_type=jnp.float32
    )
    distant_query = jnp.einsum(
        "hqk,khd->qhd", distant_slope, distant_keys, preferred_element_type=jnp.float32
    )
    query_gradient = (
        query_gradient.reshape(chosen_count, DILATION_STEP, head_number, HEAD_WIDTH)
        .at[:, 0]
        .add(distant_query)
    )
    key_grad = jnp.einsum(
        "mns,nmg->smg", local_slope, query_block, preferred_element_type=jnp.float32
    )
    far_weights = far_prob.astype(jnp.bfloat16)
    far_value_grad = jnp.einsum(
        "mns,nmg->smg", far_weights, gradient_sampled, preferred_element_type=jnp.float32
    )
    far_key_grad = jnp.einsum(
        "mns,nmg->smg",
        distant_slope,
        query_block[::DILATION_STEP],
        preferred_element_type=jnp.float32,
    )
    return (
        query_gradient.reshape(row_number, head_number, HEAD_WIDTH),
        key_grad,
        value_grad,
        far_key_grad,
        far_value_grad,
    )


def plain_device(
    tokens,
    qkv_weight,
    out_weight,
    up_weight,
    down_weight,
    norm1_gain,
    norm1_bias,
    norm2_gain,
    norm2_bias,
    visible,
    cotangent,
):
    row_number = tokens.shape[1]
    embedding_width = tokens.shape[2]
    query_scale = HEAD_WIDTH ** (-0.5)
    first_row = lax.axis_index("seq") * row_number
    positions = first_row + jnp.arange(row_number, dtype=jnp.int32)
    row_validity = positions < visible[0]
    inputs = tokens[0].astype(jnp.float32)
    norm_one, pull_one = jax.vjp(layer_norm, inputs, norm1_gain, norm1_bias)
    normed = norm_one.astype(jnp.bfloat16)
    projected = jnp.dot(normed, qkv_weight, preferred_element_type=jnp.float32)
    query_rows = (
        (projected[:, :embedding_width] * query_scale)
        .astype(jnp.bfloat16)
        .reshape(row_number, HEADS, HEAD_WIDTH)
    )
    flat_keys = projected[:, embedding_width : 2 * embedding_width].astype(jnp.bfloat16)
    flat_values = projected[:, 2 * embedding_width :].astype(jnp.bfloat16)
    key_matrix = flat_keys.reshape(row_number, HEADS, HEAD_WIDTH)
    value_matrix = flat_values.reshape(row_number, HEADS, HEAD_WIDTH)
    gathered_keys, gathered_values = (
        lax.all_gather(flat_keys[::DILATION_STEP], "seq", axis=0, tiled=True),
        lax.all_gather(flat_values[::DILATION_STEP], "seq", axis=0, tiled=True),
    )
    distant_count = gathered_keys.shape[0]
    distant_valid = jnp.arange(distant_count, dtype=jnp.int32) * DILATION_STEP < visible[0]
    distant_keys = gathered_keys.reshape(distant_count, HEADS, HEAD_WIDTH)
    distant_values = gathered_values.reshape(distant_count, HEADS, HEAD_WIDTH)
    per_segment = SEG // QB
    attended_rows, row_maximum, row_sum_total = block_forward(
        query_rows,
        key_matrix,
        value_matrix,
        row_validity,
        distant_keys,
        distant_values,
        distant_valid,
    )
    attn_low = attended_rows.reshape(row_number, embedding_width).astype(jnp.bfloat16)
    after_attn = inputs + jnp.dot(attn_low, out_weight, preferred_element_type=jnp.float32)
    norm_two, pull_two = jax.vjp(layer_norm, after_attn, norm2_gain, norm2_bias)
    normed_two = norm_two.astype(jnp.bfloat16)
    up_cols = jnp.dot(normed_two, up_weight, preferred_element_type=jnp.float32)
    activated, pull_gelu = jax.vjp(exact_gelu, up_cols)
    hidden = activated.astype(jnp.bfloat16)
    result = after_attn + jnp.dot(hidden, down_weight, preferred_element_type=jnp.float32)
    mixed_out = jnp.where(row_validity[:, None], result, 0.0).astype(jnp.bfloat16)[None]
    grad_out = jnp.where(row_validity[:, None], cotangent[0], jnp.zeros_like(cotangent[0]))
    down_grad = jnp.einsum("tf,td->fd", hidden, grad_out, preferred_element_type=jnp.float32)
    hidden_grad = jnp.einsum("td,fd->tf", grad_out, down_weight, preferred_element_type=jnp.float32)
    (up_slope,) = pull_gelu(hidden_grad)
    up_low = up_slope.astype(jnp.bfloat16)
    up_grad = jnp.einsum("td,tf->df", normed_two, up_low, preferred_element_type=jnp.float32)
    norm_two_in = jnp.einsum("tf,df->td", up_low, up_weight, preferred_element_type=jnp.float32)
    after_part, gain_two_grad, shift_two_grad = pull_two(norm_two_in)
    resid_grad = grad_out.astype(jnp.float32) + after_part
    resid_low = resid_grad.astype(jnp.bfloat16)
    out_grad = jnp.einsum("td,te->de", attn_low, resid_low, preferred_element_type=jnp.float32)
    attn_grad = jnp.einsum("te,de->td", resid_low, out_weight, preferred_element_type=jnp.float32)
    attn_grad = attn_grad.astype(jnp.bfloat16).reshape(row_number, HEADS, HEAD_WIDTH)
    query_gradient, key_grad, value_grad, far_key_grad, far_value_grad = block_backward(
        query_rows,
        key_matrix,
        value_matrix,
        row_validity,
        distant_keys,
        distant_values,
        distant_valid,
        attn_grad,
        row_maximum,
        row_sum_total,
    )
    key_list = [key_grad]
    value_list = [value_grad]
    owned_keys, owned_values = (
        lax.psum_scatter(
            far_key_grad.reshape(distant_count, embedding_width),
            "seq",
            scatter_dimension=0,
            tiled=True,
        ),
        lax.psum_scatter(
            far_value_grad.reshape(distant_count, embedding_width),
            "seq",
            scatter_dimension=0,
            tiled=True,
        ),
    )
    chosen_count = row_number // DILATION_STEP
    segment_count = row_number // SEG
    nearby_keys = jnp.sum(
        jnp.stack(key_list).reshape(segment_count, per_segment, SEG, embedding_width), axis=1
    )
    nearby_values = jnp.sum(
        jnp.stack(value_list).reshape(segment_count, per_segment, SEG, embedding_width), axis=1
    )
    key_total = (
        nearby_keys.reshape(chosen_count, DILATION_STEP, embedding_width)
        .at[:, 0]
        .add(owned_keys)
        .reshape(row_number, embedding_width)
    )
    value_total = (
        nearby_values.reshape(chosen_count, DILATION_STEP, embedding_width)
        .at[:, 0]
        .add(owned_values)
        .reshape(row_number, embedding_width)
    )
    query_total = query_gradient.reshape(row_number, embedding_width)
    mixed_grad = jnp.concatenate(
        [
            (query_total * query_scale).astype(jnp.bfloat16),
            key_total.astype(jnp.bfloat16),
            value_total.astype(jnp.bfloat16),
        ],
        axis=1,
    )
    qkv_grad = jnp.einsum("td,tf->df", normed, mixed_grad, preferred_element_type=jnp.float32)
    norm_one_in = jnp.einsum(
        "tf,df->td", mixed_grad, qkv_weight, preferred_element_type=jnp.float32
    )
    input_part, gain_one_grad, shift_one_grad = pull_one(norm_one_in)
    tokens_grad = (resid_grad + input_part).astype(jnp.bfloat16)[None]
    weight_grads = (qkv_grad, out_grad, up_grad, down_grad)
    row_parts = (
        lax.psum_scatter(weight_grads[0], "seq", scatter_dimension=0, tiled=True),
        lax.psum_scatter(weight_grads[1], "seq", scatter_dimension=0, tiled=True),
        lax.psum_scatter(weight_grads[2], "seq", scatter_dimension=0, tiled=True),
        lax.psum_scatter(weight_grads[3], "seq", scatter_dimension=0, tiled=True),
    )
    final_grads = (
        lax.psum(row_parts[0].astype(jnp.bfloat16), "slide").astype(jnp.float32),
        lax.psum(row_parts[1].astype(jnp.bfloat16), "slide").astype(jnp.float32),
        lax.psum(row_parts[2].astype(jnp.bfloat16), "slide").astype(jnp.float32),
        lax.psum(row_parts[3].astype(jnp.bfloat16), "slide").astype(jnp.float32),
    )
    norm_grads = lax.psum(
        (gain_one_grad, shift_one_grad, gain_two_grad, shift_two_grad), ("seq", "slide")
    )
    return (
        mixed_out,
        tokens_grad,
        final_grads[0],
        final_grads[1],
        final_grads[2],
        final_grads[3],
        norm_grads[0],
        norm_grads[1],
        norm_grads[2],
        norm_grads[3],
    )


MESH = pl.DeviceIdType.MESH
LOW = jnp.bfloat16
FULL = jnp.float32
AUG = 64
LANES = 128
NEVER = -1000000000.0
ANY = pl.BlockSpec(memory_space=pl.ANY)
VMEM = pl.BlockSpec(memory_space=pltpu.VMEM)
SMEM = pl.BlockSpec(memory_space=pltpu.SMEM)


def nn(left, right):
    return jnp.dot(left, right, preferred_element_type=FULL)


def nt(left, right):
    return lax.dot_general(left, right, (((1,), (1,)), ((), ())), preferred_element_type=FULL)


def tn(left, right):
    return lax.dot_general(left, right, (((0,), (0,)), ((), ())), preferred_element_type=FULL)


def remote(src, dst, send_sem, recv_sem, device):
    return pltpu.make_async_remote_copy(
        src_ref=src,
        dst_ref=dst,
        send_sem=send_sem,
        recv_sem=recv_sem,
        device_id=device,
        device_id_type=MESH,
    )


def greet(devices):
    barrier = pltpu.get_barrier_semaphore()
    for device in devices:
        pl.semaphore_signal(barrier, inc=1, device_id=device, device_id_type=MESH)
    pl.semaphore_wait(barrier, len(devices))


def row_peers(count):
    seq, slide = lax.axis_index("seq"), lax.axis_index("slide")
    return [(lax.rem(seq + step, count), slide) for step in range(1, count)]


def spread(ref, values):
    for group in range(ref.shape[0]):
        ref[group] = values[:, group * LANES : (group + 1) * LANES]


def strided_rows(ref, step, count):
    groups = [
        ref[group, pl.ds(step, count, stride=DILATION_STEP), :] for group in range(ref.shape[0])
    ]
    return jnp.concatenate(groups, axis=1)


def strided_store(ref, step, count, values):
    for group in range(ref.shape[0]):
        ref[group, pl.ds(step, count, stride=DILATION_STEP), :] = values[
            :, group * LANES : (group + 1) * LANES
        ]


def chunk(step, size):
    return pl.ds(pl.multiple_of(step * size, size), size)


def steps(body):
    @pl.loop(0, DILATION_STEP // 4)
    def _(group):
        for member in range(4):
            body(group * 4 + member)


def row_mean(values):
    return jnp.mean(values, axis=-1, keepdims=True)


def fold_rows(values):
    return jnp.sum(values.reshape(-1, 8, values.shape[-1]), axis=0)


def mask_rows(ref, bias):
    first = lax.broadcasted_iota(jnp.int32, (AUG - HEAD_WIDTH, ref.shape[2]), 0) == 0
    ref[:, HEAD_WIDTH:, :] = jnp.broadcast_to(
        jnp.where(first, bias, 0.0).astype(LOW), (HEADS, AUG - HEAD_WIDTH, ref.shape[2])
    )


class Place:
    def __init__(self):
        seq, slide = lax.axis_index("seq"), lax.axis_index("slide")
        self.seq, self.slide = seq, slide
        self.z, self.x = seq // 2, seq % 2
        self.b, self.a = self.z // 2, self.z % 2
        self.y, self.c = slide // 2, slide % 2
        self.sibling = (seq, slide + 1 - 2 * self.c)
        self.across_y = (seq, slide + 2 - 4 * self.y)
        self.diagonal = (seq, 3 - slide)
        self.across_x = (seq + 1 - 2 * self.x, slide)
        self.slide_peers = (self.sibling, self.across_y, self.diagonal)

    def layer(self, step):
        return (self.z + step) % 4


class Part:
    def __init__(self, place, orders, both, core_got, got, final, send_sem, recv_sem):
        self.place, self.orders, self.both = place, orders, both
        self.core_got, self.got, self.final = core_got, got, final
        self.send_sem, self.recv_sem = send_sem, recv_sem
        self.folds = max(len(order) for order in orders)

    def blocks(self, core, phase, value):
        choices = {}
        for at, name in enumerate(self.orders[core], 1):
            if at < phase:
                choices[name] = [getattr(self.place, name)]
            elif at == phase:
                choices[name] = [value]
            else:
                choices[name] = list(range(4 if name == "z" else 2))
        if "z" not in choices:
            choices["z"] = [2 * b + a for b in choices["b"] for a in choices["a"]]
        return [(2 * z + x, y) for z in choices["z"] for x in choices["x"] for y in choices["y"]]

    def partners(self, core, phase):
        place, name = self.place, self.orders[core][phase - 1]
        if name == "x":
            return [(1 - place.x, place.across_x)]
        if name == "y":
            return [(1 - place.y, place.across_y)]
        if name == "a":
            return [(1 - place.a, (place.seq + 2 - 4 * place.a, place.slide))]
        if name == "b":
            return [(1 - place.b, (place.seq + 4 - 8 * place.b, place.slide))]
        layers = [place.layer(k) for k in (1, 2, 3)]
        return [(z, (2 * z + place.x, place.slide)) for z in layers]

    def span(self, core, phase):
        first, left = 0, 16
        for at, name in enumerate(self.orders[core], 1):
            left //= 4 if name == "z" else 2
            number = left * (3 if name == "z" else 1)
            if at == phase:
                return first, number
            first += number

    def transfers(self, core, phase):
        kept, got = self.both.at[0], self.got
        slot = self.span(core, phase)[0]
        pairs = "y" in self.orders[core][phase:]
        moves = []
        for value, device in self.partners(core, phase):
            for owner, y in self.blocks(core, phase, value):
                if not pairs:
                    moves.append((kept.at[owner, y], got.at[slot], device))
                elif y == 0:
                    moves.append((kept.at[owner], got.at[pl.ds(slot, 2)], device))
                slot += 1
        return moves

    def start(self, phase, merged):
        place, send, recv = self.place, self.send_sem.at[phase], self.recv_sem.at[phase]
        if phase == 0:
            remote(self.both.at[1], self.core_got, send, recv, place.sibling).start()
        elif phase <= self.folds:
            for core in range(2):
                if phase > len(self.orders[core]):
                    continue

                @pl.when(place.c == core)
                def _(core=core):
                    for source, target, device in self.transfers(core, phase):
                        remote(source, target, send, recv, device).start()
        elif phase == self.folds + 1:
            own = self.final.at[place.c * 2 + place.y]
            for device in place.slide_peers if merged else (place.across_y,):
                remote(own, own, send, recv, device).start()
        else:
            own = self.final.at[pl.ds(place.c * 2, 2)]
            remote(own, own, send, recv, place.sibling).start()

    def wait(self, phase, whole):
        both_ways = remote(
            whole, whole, self.send_sem.at[phase], self.recv_sem.at[phase], self.place.sibling
        )
        both_ways.wait_recv()
        both_ways.wait_send()

    def finish(self, phase, merged):
        place = self.place
        if phase == 0:
            self.wait(phase, self.core_got)

            @pl.loop(0, 8)
            def _(owner):
                for row in range(2):
                    self.both[0, owner, row] += self.core_got[owner, row]
        elif phase <= self.folds:
            for core in range(2):
                if phase > len(self.orders[core]):
                    continue

                @pl.when(place.c == core)
                def _(core=core):
                    first, number = self.span(core, phase)
                    self.wait(phase, self.got.at[pl.ds(first, number)])
                    name = self.orders[core][phase - 1]
                    blocks = self.blocks(core, phase, getattr(place, name))
                    for n, (owner, y) in enumerate(blocks):
                        slots = range(first + n, first + number, len(blocks))
                        self.add(owner, y, slots, core if phase == len(self.orders[core]) else None)
        elif phase == self.folds + 1:
            self.wait(phase, self.final.at[pl.ds(0, 3 if merged else 1)])
        else:
            self.wait(phase, self.final.at[pl.ds(0, 2)])

    def add(self, owner, y, slots, core):
        if len(slots) == 1:
            total = self.both[0, owner, y] + self.got[slots[0]]
        else:
            total = self.both[0, owner, y].astype(FULL)
            for slot in slots:
                total = total + self.got[slot].astype(FULL)
            total = total.astype(LOW)
        if core is None:
            self.both[0, owner, y] = total
        else:
            self.final[core * 2 + self.place.y] = total


class Piece:
    def __init__(self, parts, merged, outs, out_sem):
        self.parts, self.merged, self.outs, self.out_sem = parts, merged, outs, out_sem
        self.last = parts[0].folds + (1 if merged else 2)
        self.phase = -1

    @property
    def done(self):
        return self.phase > self.last

    def advance(self):
        if self.done:
            return
        if self.phase >= 0:
            for part in self.parts:
                part.finish(self.phase, self.merged)
        self.phase += 1
        if not self.done:
            for part in self.parts:
                part.start(self.phase, self.merged)
            return
        for n in range(len(self.parts)):
            self.out_copy(n).start()

    def out_copy(self, n):
        return pltpu.make_async_copy(self.parts[n].final, self.outs[n], self.out_sem.at[n])


TILES = 3
LASTS = 4
PIECES = TILES + LASTS
ORDERS = (
    ("abxy", "yxz", False),
    ("yxab", "xzy", False),
    ("yxz", "yaxb", False),
    ("yxab", "xyab", True),
    ("yxab", "xyab", True),
    ("yxab", "xyab", True),
    ("yxab", "ayxb", True),
)
HOOKS = {
    "tile1.1": (0,),
    "tile2.1": (1,),
    "after0": (0,),
    "after1": (2,),
    "far": (1,),
    "near0": (0,),
    "near4": (3,),
    "near5": (4,),
    "near6": (2,),
    "last2": (3,),
    "last3": (1, 5),
    "into": (6, 4, 0, 2),
    "norm": (1,),
}
TAIL = (3, 5, 4, 6, 2, 0, 1, 5, 3, 6, 4, 2, 5, 0, 3, 1, 6, 4, 1, 0, 5, 2, 3, 6, 4, 2, 5, 6)

def main_kernel(
    count, tokens, cotangent, qkv_weight, out_weight, up_weight, down_weight,
    gain_one, shift_one, gain_two, shift_two, visible,
    mixed_out, tokens_out, down_sums, up_sums, last_sums, norm_out, weights_kept, norm_kept,
    normed, far_normed, query, key, value, far_key, far_value, far_weights, scale, far_scale, attn,
    delta, slope, resid, after, dyb, wqkv, wo, wide, staged, all_far, far_got, spread_one,
    sums, around, across,
    down_both, up_both, last_both, down_core, up_core, last_core,
    down_got, up_got, last_got, down_final, up_final, last_final,
    load_sem, tile_sem, group_sem, store_sem, out_sem, send_sem, recv_sem,
    gather_send_sem, gather_recv_sem, far_send_sem, far_recv_sem, norm_send_sem, norm_recv_sem,
):
    place = Place()
    seq, core = place.seq, place.c
    rows, width = resid.shape
    chosen = rows // DILATION_STEP
    group_lanes = LANES
    tile_width = count * group_lanes
    first_row = seq * rows
    limit = visible[0]
    peers = row_peers(count)
    others = list(place.slide_peers) + peers
    barrier = pltpu.get_barrier_semaphore()
    for other in others:
        pl.semaphore_signal(barrier, inc=1, device_id=other, device_id_type=MESH)

    def valid_rows(step):
        places = lax.broadcasted_iota(jnp.int32, (chosen, 1), 0) * DILATION_STEP + step
        return first_row + places < limit

    def landed(n):
        sources = (
            (tokens, staged),
            (qkv_weight.at[:, pl.ds(width, width)], wqkv.at[1]),
            (qkv_weight.at[:, pl.ds(2 * width, width)], wqkv.at[2]),
            (qkv_weight.at[:, pl.ds(0, width)], wqkv.at[0]),
            (out_weight, wo),
            (cotangent, staged),
        )
        return pltpu.make_async_copy(*sources[n], load_sem.at[n])

    for n in range(5):
        landed(n).start()
    distant = count * chosen
    members = 4

    def kept_group(group, slots):
        kept = weights_kept.at[pl.ds(group * members, members)]
        return slots.at[group % 2], kept, group_sem.at[group % 2]

    pieces = []
    for n in range(TILES):
        parts = [
            Part(
                place,
                ORDERS[n][:2],
                both.at[n],
                core_got.at[n],
                got.at[n],
                final.at[n],
                send_sem.at[n, which],
                recv_sem.at[n, which],
            )
            for which, (both, core_got, got, final) in enumerate(
                (
                    (down_both, down_core, down_got, down_final),
                    (up_both, up_core, up_got, up_final),
                )
            )
        ]
        pieces.append(Piece(parts, ORDERS[n][2], (down_sums.at[n], up_sums.at[n]), out_sem.at[n]))
    for n in range(LASTS):
        part = Part(
            place,
            ORDERS[TILES + n][:2],
            last_both.at[n],
            last_core.at[n],
            last_got.at[n],
            last_final.at[n],
            send_sem.at[TILES + n, 0],
            recv_sem.at[TILES + n, 0],
        )
        pieces.append(Piece([part], ORDERS[TILES + n][2], (last_sums.at[n],), out_sem.at[TILES + n]))

    def hook(name):
        for n in HOOKS.get(name, ()):
            if pieces[n].phase >= 0:
                pieces[n].advance()

    def split_last(n, side, grads):
        target = last_both.at[n, (side + core) % 2]
        target[...] = grads.astype(LOW).reshape(count, 2, -1, grads.shape[1])

    def attend_part(h1, top, total, attended, weights):
        landed(0).wait()
        spread(wide, staged[...].astype(FULL))
        landed(5).start()

        def normalize(step):
            at = chunk(step, chosen)
            values = strided_rows(wide, step, chosen)
            centered = values - row_mean(values)
            inverse = lax.rsqrt(row_mean(centered * centered) + epsilon)
            normal = centered * inverse
            after[at] = values
            resid[at] = normal
            spread_one[at] = jnp.broadcast_to(inverse, (chosen, LANES))
            low = (normal * gain_one[...][None] + shift_one[...][None]).astype(LOW)
            h1[at] = low
            return low

        all_far[seq] = normalize(0)

        @pl.loop(0, 5)
        def _(group):
            for member in range(3):
                normalize(group * 3 + member + 1)

        pltpu.make_async_copy(resid, norm_kept, store_sem.at[0]).start()
        for part, ref in ((1, key), (2, value)):
            landed(part).wait()
            projected = nn(h1[...], wqkv[part]).astype(LOW)
            ref[:, :HEAD_WIDTH, :] = projected.T.reshape(HEADS, HEAD_WIDTH, rows)
            if part == 1:
                pl.semaphore_wait(barrier, len(others))
                for n, peer in enumerate(peers):
                    mine = all_far.at[seq]
                    send, recv = gather_send_sem.at[n], gather_recv_sem.at[n]
                    remote(mine, mine, send, recv, peer).start()
        landed(3).wait()
        projected = (nn(h1[...], wqkv[0]) * HEAD_WIDTH ** (-0.5)).astype(LOW)
        query[:, :HEAD_WIDTH, :] = projected.T.reshape(HEADS, HEAD_WIDTH, rows)
        places = lax.broadcasted_iota(jnp.int32, (1, rows), 1)
        places = first_row + (places % chosen) * DILATION_STEP + places // chosen
        mask_rows(key, jnp.where(places < limit, 0.0, NEVER))
        mask_rows(query, jnp.ones((1, rows), FULL))

        @pl.loop(0, HEADS // members)
        def _(group):
            slot, kept, sem = kept_group(group, weights)

            @pl.when(group >= 2)
            def _():
                pltpu.make_async_copy(slot, kept, sem).wait()

            for member in range(members):
                head = group * members + member
                scores = tn(key[head], query[head])
                highest = jnp.max(scores, axis=0, keepdims=True)
                exponent = jnp.exp(scores - highest)
                top[head] = highest
                total[head] = jnp.sum(exponent, axis=0, keepdims=True)
                low = exponent.astype(LOW)
                weights[group % 2, member] = low
                attended[head] = nn(value[head], low)
            pltpu.make_async_copy(slot, kept, sem).start()

        normed[...] = h1[...].T
        landed(5).wait()
        spread(wide, staged[...].astype(FULL))

        @steps
        def _(step):
            at = chunk(step, chosen)
            dyb[at] = jnp.where(valid_rows(step), strided_rows(wide, step, chosen), 0.0).astype(LOW)

        for n in range(count - 1):
            source = lax.rem(seq + count - 1 - n, count)
            mine, theirs = all_far.at[seq], all_far.at[source]
            wait = remote(mine, theirs, gather_send_sem.at[n], gather_recv_sem.at[n], peers[0])
            wait.wait_recv()
            wait.wait_send()
        flat = all_far[...].reshape(distant, width)
        for part, ref in ((1, far_key), (2, far_value)):
            projected = nn(flat, wqkv[part]).astype(LOW)
            ref[:, :HEAD_WIDTH, :] = projected.T.reshape(HEADS, HEAD_WIDTH, distant)
        places = lax.broadcasted_iota(jnp.int32, (1, distant), 1) * DILATION_STEP
        mask_rows(far_key, jnp.where(places < limit, 0.0, NEVER))
        lane_mask = jnp.where(lax.broadcasted_iota(jnp.int32, (1, LANES), 1) < chosen, 0.0, NEVER)

        @pl.loop(0, HEADS // 4)
        def _(group):
            for member in range(4):
                head = group * 4 + member
                scores = tn(far_key[head], query[head][:, :LANES]) + lane_mask
                highest = jnp.max(scores, axis=0, keepdims=True)
                exponent = jnp.exp(scores - highest)
                low = exponent.astype(LOW)
                far_weights[head] = low
                near = top[head][:, :LANES]
                joint = jnp.maximum(near, highest)
                near_part, far_part = jnp.exp(near - joint), jnp.exp(highest - joint)
                joint_total = total[head][:, :LANES] * near_part + far_part * jnp.sum(
                    exponent, axis=0, keepdims=True
                )
                near_part, far_part = near_part / joint_total, far_part / joint_total
                far_scale[head] = far_part
                local = jnp.concatenate([near_part, 1.0 / total[head][:, LANES:]], axis=1)
                scale[head] = local
                result = attended[head] * local
                with_far = result[:, :LANES] + nn(far_value[head], low) * far_part
                result = jnp.concatenate([with_far, result[:, LANES:]], axis=1)
                attn[head] = result.astype(LOW)

        for group in (2, 3):
            slot, kept, sem = kept_group(group, weights)
            pltpu.make_async_copy(slot, kept, sem).wait()
        pltpu.make_async_copy(resid, norm_kept, store_sem.at[0]).wait()

    vm = pltpu.VMEM
    pl.run_scoped(
        attend_part,
        vm((rows, width), LOW),
        vm((HEADS, 1, rows), FULL),
        vm((HEADS, 1, rows), FULL),
        vm((HEADS, HEAD_WIDTH, rows), FULL),
        vm((2, members, rows, rows), LOW),
    )

    def forward_part(norm_two, spread_two, h2, h2_t, active, low_slope, wup, wdown):
        halves = 2
        per_half = tile_width // halves

        def load_tile(tile, half):
            for local in range(count // halves):
                owner = half * (count // halves) + local
                first = owner * TILES * group_lanes + tile * group_lanes
                at = pl.ds(pl.multiple_of(first, LANES), group_lanes)
                to = pl.ds(local * group_lanes, group_lanes)
                pltpu.make_async_copy(
                    up_weight.at[:, at], wup.at[half, :, to], tile_sem.at[half, 0]
                ).start()
                pltpu.make_async_copy(
                    down_weight.at[at], wdown.at[half, to], tile_sem.at[half, 1]
                ).start()

        def wait_tile(half):
            pltpu.make_async_copy(wup.at[half], wup.at[half], tile_sem.at[half, 0]).wait()
            pltpu.make_async_copy(wdown.at[half], wdown.at[half], tile_sem.at[half, 1]).wait()

        load_tile(0, 0)
        load_tile(0, 1)
        landed(4).wait()
        after[...] += nn(attn[...].reshape(width, rows).T, wo[...])

        @steps
        def _(step):
            at = chunk(step, chosen)
            values = after[at]
            centered = values - row_mean(values)
            inverse = lax.rsqrt(row_mean(centered * centered) + epsilon)
            normal = centered * inverse
            norm_two[at] = normal
            spread_two[at] = jnp.broadcast_to(inverse, (chosen, LANES))
            h2[at] = (normal * gain_two[...][None] + shift_two[...][None]).astype(LOW)
            resid[at] = jnp.zeros((chosen, width), FULL)

        h2_t[...] = h2[...].T
        for tile in range(TILES):
            @pl.loop(0, halves)
            def _(half, tile=tile):
                wait_tile(half)
                for part in range(2):
                    at = slice(part * per_half // 2, (part + 1) * per_half // 2)
                    to = pl.ds(
                        pl.multiple_of(half * per_half + part * per_half // 2, LANES), per_half // 2
                    )
                    hidden = nn(h2[...], wup[half, :, at])
                    hidden_slope = nt(dyb[...], wdown[half, at])
                    share = 0.5 * (1.0 + lax.erf(hidden * 0.7071067811865476))
                    active[:, to] = (hidden * share).astype(LOW)
                    density = hidden * jnp.exp(-0.5 * hidden * hidden) * 0.3989422804014327
                    low_slope[:, to] = (hidden_slope * (share + density)).astype(LOW)
                to = pl.ds(pl.multiple_of(half * per_half, LANES), per_half)
                after[...] += nn(active[:, to], wdown[half])
                resid[...] += nt(low_slope[:, to], wup[half])
                if tile + 1 < TILES:
                    load_tile(tile + 1, half)

            hook("tile%d.1" % tile)

            @pl.loop(0, 4)
            def _(part, tile=tile):
                at = pl.ds(pl.multiple_of(part * tile_width // 4, LANES), tile_width // 4)
                grads = nn(h2_t[...], low_slope[:, at]).astype(LOW)
                target = up_both.at[tile, (part // 2 + core) % 2]
                target[:, part % 2] = grads.reshape(count, -1, grads.shape[1])
                grads = tn(active[:, at], dyb[...]).astype(LOW)
                owners = count // 4
                grads = grads.reshape(owners, 2, 2, -1, width)
                for side in range(2):
                    target = down_both.at[tile, (side + core) % 2]
                    target[pl.ds(part * owners, owners)] = grads[:, side]

            pieces[tile].advance()
            hook("tile%d.3" % tile)
        sums[...] = jnp.zeros_like(sums)
        hook("after0")

        @steps
        def _(step):
            at = chunk(step, chosen)
            strided_store(wide, step, chosen, jnp.where(valid_rows(step), after[at], 0.0))
            given, normal = resid[at], norm_two[at]
            sums[2] += fold_rows(given * normal)
            sums[3] += fold_rows(given)
            scaled = given * gain_two[...][None]
            part = scaled - row_mean(scaled) - normal * row_mean(scaled * normal)
            value_here = dyb[at].astype(FULL) + spread_two[at][:, :1] * part
            resid[at] = value_here
            h2[at] = value_here.astype(LOW)

        for group in range(width // LANES):
            staged[:, group * LANES : (group + 1) * LANES] = wide[group].astype(LOW)
        pltpu.make_async_copy(staged, mixed_out, store_sem.at[1]).start()
        half = width // 2
        hook("after1")
        for n in range(2):
            at = slice(n * half, (n + 1) * half)
            split_last(2 * n + 1, 1, nn(attn[...].reshape(width, rows), h2[:, at]))
        slope[...] = nt(wo[...], h2[...]).astype(LOW).reshape(HEADS, HEAD_WIDTH, rows)

        @pl.loop(0, HEADS)
        def _(head):
            product = slope[head].astype(FULL) * attn[head].astype(FULL)
            delta[head] = jnp.sum(product, axis=0, keepdims=True)

        hook("after2")

    pl.run_scoped(
        forward_part,
        vm((rows, width), FULL),
        vm((rows, LANES), FULL),
        vm((rows, width), LOW),
        vm((width, rows), LOW),
        vm((rows, tile_width), LOW),
        vm((rows, tile_width), LOW),
        vm((2, width, tile_width // 2), LOW),
        vm((2, tile_width // 2, width), LOW),
    )

    def backward_part(weights, slopes, far_query, far_send, given):
        norm_one = after

        def load_group(group):
            slot, kept, sem = kept_group(group, weights)
            return pltpu.make_async_copy(kept, slot, sem)

        load_group(0).start()
        load_group(1).start()
        norm_load = pltpu.make_async_copy(norm_kept, norm_one, store_sem.at[0])
        norm_load.start()

        @pl.loop(0, HEADS // 4)
        def _(group):
            for member in range(4):
                head = group * 4 + member
                first_slope = slope[head][:, :LANES]
                low = far_weights[head]
                change = tn(far_value[head], first_slope) - delta[head][:, :LANES]
                score_slope = (low.astype(FULL) * far_scale[head] * change).astype(LOW)
                far_query[head] = nn(far_key[head, :HEAD_WIDTH], score_slope)
                scaled = (first_slope.astype(FULL) * far_scale[head]).astype(LOW)
                given[0, head] = nt(query[head, :HEAD_WIDTH, :LANES], score_slope).astype(LOW)
                given[1, head] = nt(scaled, low).astype(LOW)

        hook("far0")
        far_normed[...] = all_far[...].reshape(distant, width).T
        into = nn(wqkv[1], given[0].reshape(width, distant))
        into += nn(wqkv[2], given[1].reshape(width, distant))
        far_send[...] = into.T.astype(LOW).reshape(count, chosen, width)
        for n, peer in enumerate(peers):
            remote(
                far_send.at[peer[0]], far_got.at[n], far_send_sem.at[n], far_recv_sem.at[n], peer
            ).start()
        hook("far")

        def weight_slopes(half):
            at = slice(half * HEADS // 2, (half + 1) * HEADS // 2)
            for part, (n, side) in enumerate(((0, 0), (0, 1), (1, 0))):
                grads = nt(normed[...], slopes[part, at].reshape(width // 2, rows))
                if part:
                    far = given[part - 1, at].reshape(width // 2, distant)
                    grads += nt(far_normed[...], far)
                split_last(2 * half + n, side, grads)
                if part:
                    pieces[TILES + 2 * half + n].advance()
                    hook("last%d" % (2 * half + n))

        for group in range(HEADS // members):
            load_group(group).wait()
            for member in range(members):
                head = group * members + member
                low = weights[group % 2, member]
                change = tn(value[head], slope[head]) - delta[head]
                score_slope = (low.astype(FULL) * scale[head] * change).astype(LOW)
                query_slope = nn(key[head, :HEAD_WIDTH], score_slope)
                key_slope = nt(query[head, :HEAD_WIDTH], score_slope)
                scaled = (slope[head].astype(FULL) * scale[head]).astype(LOW)
                value_slope = nt(scaled, low)
                first = query_slope[:, :LANES] + far_query[head]
                query_slope = jnp.concatenate([first, query_slope[:, LANES:]], axis=1)
                slopes[0, head] = (query_slope * HEAD_WIDTH ** (-0.5)).astype(LOW)
                slopes[1, head] = key_slope.astype(LOW)
                slopes[2, head] = value_slope.astype(LOW)
                if member % 2:
                    hook("near%d" % (head // 2))
            if (group + 2) * members < HEADS:
                load_group(group + 2).start()
            if group % 2:
                weight_slopes(group // 2)

        def flat_slopes(part):
            return slopes[part].reshape(width, rows)

        into = nn(wqkv[0], flat_slopes(0))
        into += nn(wqkv[1], flat_slopes(1))
        into += nn(wqkv[2], flat_slopes(2))
        norm_load.wait()
        pltpu.make_async_copy(staged, mixed_out, store_sem.at[1]).wait()
        spread(wide, into.T)
        hook("into")
        total = far_send[seq].astype(FULL)
        for n in range(count - 1):
            wait = remote(
                far_got.at[n], far_got.at[n], far_send_sem.at[n], far_recv_sem.at[n], peers[0]
            )
            wait.wait_recv()
            wait.wait_send()
            total = total + far_got[n].astype(FULL)
        for group in range(width // LANES):
            wide[group, :chosen] += total[:, group * LANES : (group + 1) * LANES]

        @steps
        def _(step):
            at = chunk(step, chosen)
            here = jnp.concatenate([wide[group, at, :] for group in range(width // LANES)], axis=1)
            normal = norm_one[at]
            sums[0] += fold_rows(here * normal)
            sums[1] += fold_rows(here)
            scaled = here * gain_one[...][None]
            part = scaled - row_mean(scaled) - normal * row_mean(scaled * normal)
            resid[at] += spread_one[at][:, :1] * part

    pl.run_scoped(
        backward_part,
        vm((2, members, rows, rows), LOW),
        vm((3, HEADS, HEAD_WIDTH, rows), LOW),
        vm((HEADS, HEAD_WIDTH, LANES), FULL),
        vm((count, chosen, width), LOW),
        vm((2, HEADS, HEAD_WIDTH, distant), LOW),
    )
    for n in range(4):
        around[seq, pl.ds(n, 1)] = jnp.sum(sums[n], axis=0, keepdims=True)
    for n, peer in enumerate(peers):
        mine = around.at[seq]
        remote(mine, mine, norm_send_sem.at[n], norm_recv_sem.at[n], peer).start()
    hook("norm")

    @steps
    def _(step):
        strided_store(wide, step, chosen, resid[chunk(step, chosen)])

    for group in range(width // LANES):
        staged[:, group * LANES : (group + 1) * LANES] = wide[group].astype(LOW)
    tokens_copy = pltpu.make_async_copy(staged, tokens_out, store_sem.at[2])
    tokens_copy.start()
    for n in range(count - 1):
        mine = around.at[seq]
        wait = remote(mine, mine, norm_send_sem.at[n], norm_recv_sem.at[n], peers[0])
        wait.wait_recv()
        wait.wait_send()
    total = around[0]
    for n in range(1, count):
        total = total + around[n]
    across[place.slide] = total
    for n, peer in enumerate(place.slide_peers):
        mine, at = across.at[place.slide], count - 1 + n
        remote(mine, mine, norm_send_sem.at[at], norm_recv_sem.at[at], peer).start()
    for n in TAIL + tuple(range(PIECES)) * 6:
        pieces[n].advance()
    for n in range(3):
        mine, at = across.at[0], count - 1 + n
        wait = remote(mine, mine, norm_send_sem.at[at], norm_recv_sem.at[at], peers[0])
        wait.wait_recv()
        wait.wait_send()
    norm_out[...] = (across[0] + across[1]) + (across[2] + across[3])
    for piece in pieces:
        for n in range(len(piece.parts)):
            piece.out_copy(n).wait()
    tokens_copy.wait()


def main_pass(count, tokens, cotangent, weights, norms, visible):
    rows, width = tokens.shape
    chosen = rows // DILATION_STEP
    distant = count * chosen
    owned = width // count
    vm, dma = pltpu.VMEM, pltpu.SemaphoreType.DMA
    down_block, up_block = (LANES // 4, width), (owned, 2 * LANES)
    last_block = (owned // 2, width // 2)
    blocks = ((TILES, down_block), (TILES, up_block), (LASTS, last_block))
    low = [
        (width, rows), (width, distant), (HEADS, AUG, rows), (HEADS, AUG, rows),
        (HEADS, HEAD_WIDTH, rows), (HEADS, AUG, distant), (HEADS, HEAD_WIDTH, distant),
        (HEADS, distant, LANES),
    ]
    scratch = [vm(shape, LOW) for shape in low]
    scratch += [
        vm((HEADS, 1, rows), FULL),
        vm((HEADS, 1, LANES), FULL),
        vm((HEADS, HEAD_WIDTH, rows), LOW),
        vm((HEADS, 1, rows), FULL),
        vm((HEADS, HEAD_WIDTH, rows), LOW),
        vm((rows, width), FULL),
        vm((rows, width), FULL),
        vm((rows, width), LOW),
        vm((3, width, width), LOW),
        vm((width, width), LOW),
        vm((width // LANES, rows, LANES), FULL),
        vm((rows, width), LOW),
        vm((count, chosen, width), LOW),
        vm((count - 1, chosen, width), LOW),
        vm((rows, LANES), FULL),
        vm((4, 8, width), FULL),
        vm((count, 8, width), FULL),
        vm((4, 8, width), FULL),
    ]
    scratch += [vm((n, 2, count, 2) + block, LOW) for n, block in blocks]
    scratch += [vm((n, count, 2) + block, LOW) for n, block in blocks]
    scratch += [vm((n, 15) + block, LOW) for n, block in blocks]
    scratch += [vm((n, 4) + block, LOW) for n, block in blocks]
    scratch += [
        dma((6,)), dma((2, 2)), dma((2,)), dma((3,)), dma((PIECES, 2)),
        dma((PIECES, 2, 7)), dma((PIECES, 2, 7)),
        dma((count - 1,)), dma((count - 1,)), dma((count - 1,)), dma((count - 1,)),
        dma((count + 2,)), dma((count + 2,)),
    ]
    sums = [jax.ShapeDtypeStruct((n, 4) + block, LOW) for n, block in blocks]
    results = pl.pallas_call(
        functools.partial(main_kernel, count),
        out_shape=(
            jax.ShapeDtypeStruct((rows, width), LOW),
            jax.ShapeDtypeStruct((rows, width), LOW),
            *sums,
            jax.ShapeDtypeStruct((8, width), FULL),
            jax.ShapeDtypeStruct((HEADS, rows, rows), LOW),
            jax.ShapeDtypeStruct((rows, width), FULL),
        ),
        in_specs=[ANY] * 6 + [VMEM] * 4 + [SMEM],
        out_specs=(ANY, ANY, ANY, ANY, ANY, VMEM, ANY, ANY),
        scratch_shapes=scratch,
        compiler_params=pltpu.CompilerParams(
            collective_id=1, has_side_effects=True, vmem_limit_bytes=64 << 20
        ),
        name="main_pass",
    )(tokens, cotangent, *weights, *norms, visible)
    return results[:6]


def finish_kernel(
    mixed, tokens_grad, down_sums, up_sums, last_sums, norms,
    mixed_out, tokens_out, qkv_out, out_out, up_out, down_out, *refs
):
    norm_outs = refs[:4]
    mixed_in, tokens_in, down_in, up_in, last_in, norms_in = refs[4:10]
    qkv, out, up, down, in_sem, out_sem = refs[10:]
    loads = [
        pltpu.make_async_copy(source, target, in_sem.at[n])
        for n, (source, target) in enumerate(
            (
                (down_sums, down_in),
                (up_sums, up_in),
                (last_sums, last_in),
                (norms, norms_in),
                (mixed, mixed_in),
                (tokens_grad, tokens_in),
            )
        )
    ]
    for copy in loads:
        copy.start()
    stores = []

    def store(source, target):
        copy = pltpu.make_async_copy(source, target, out_sem.at[len(stores)])
        copy.start()
        stores.append(copy)

    tiles, blocks, rows, _ = down_sums.shape
    loads[0].wait()
    for tile in range(tiles):
        for block in range(blocks):
            first = (tile * blocks + block) * rows
            down[first : first + rows] = down_in[tile, block].astype(FULL)
    store(down, down_out)
    loads[1].wait()
    for tile in range(tiles):
        for block in range(blocks):
            for half in range(2):
                first = ((block * 2 + half) * tiles + tile) * LANES
                part = up_in[tile, block][:, half * LANES : (half + 1) * LANES]
                up[:, first : first + LANES] = part.astype(FULL)
    store(up, up_out)
    loads[2].wait()
    rows, columns = last_sums.shape[2:]
    for piece in range(last_sums.shape[0]):
        half, pair = divmod(piece, 2)
        for block in range(blocks):
            side, row = divmod(block, 2)
            at = slice(row * rows, (row + 1) * rows)
            first = half * columns
            target = out
            if pair == 0 or side == 0:
                target, first = qkv, first + 2 * columns * (2 * pair + side)
            target[at, first : first + columns] = last_in[piece, block].astype(FULL)
    store(qkv, qkv_out)
    store(out, out_out)
    loads[3].wait()
    for n, norm_out in enumerate(norm_outs):
        norm_out[...] = norms_in[n]
    for n, (source, target) in enumerate(((mixed_in, mixed_out), (tokens_in, tokens_out))):
        loads[4 + n].wait()
        store(source, target)
    for copy in stores:
        copy.wait()


def finish_pass(count, results):
    rows, width = results[0].shape
    owned = width // count

    def full(*shape):
        return jax.ShapeDtypeStruct(shape, FULL)

    grads = [
        full(owned, 3 * width),
        full(owned, width),
        full(owned, TILES * count * LANES),
        full(TILES * LANES, width),
    ]
    return pl.pallas_call(
        finish_kernel,
        out_shape=(
            jax.ShapeDtypeStruct((rows, width), LOW),
            jax.ShapeDtypeStruct((rows, width), LOW),
            *grads,
            *[full(width)] * 4,
        ),
        in_specs=[ANY] * 6,
        out_specs=(ANY,) * 6 + (VMEM,) * 4,
        scratch_shapes=[pltpu.VMEM(ref.shape, ref.dtype) for ref in (*results, *grads)]
        + [pltpu.SemaphoreType.DMA((6,)), pltpu.SemaphoreType.DMA((6,))],
        compiler_params=pltpu.CompilerParams(vmem_limit_bytes=63 << 20),
        name="finish_pass",
    )(*results)


def fused_device(
    tokens,
    qkv_weight,
    out_weight,
    up_weight,
    down_weight,
    norm1_gain,
    norm1_bias,
    norm2_gain,
    norm2_bias,
    visible,
    cotangent,
):
    count = lax.axis_size("seq")
    results = main_pass(
        count,
        tokens[0],
        cotangent[0],
        (qkv_weight, out_weight, up_weight, down_weight),
        (norm1_gain, norm1_bias, norm2_gain, norm2_bias),
        visible,
    )
    mixed, tokens_grad, *grads = finish_pass(count, results)
    return (mixed[None], tokens_grad[None], *grads)


def solution(mesh):
    placed = (
        P("slide", "seq", None),
        P(),
        P(),
        P(),
        P(),
        P(),
        P(),
        P(),
        P(),
        P("slide"),
        P("slide", "seq", None),
    )
    fused = mesh.shape["seq"] == 8 and mesh.shape["slide"] == 4
    return jax.shard_map(
        fused_device if fused else plain_device,
        mesh=mesh,
        in_specs=placed,
        out_specs=(
            P("slide", "seq", None),
            P("slide", "seq", None),
            P("seq", None),
            P("seq", None),
            P("seq", None),
            P("seq", None),
            P(),
            P(),
            P(),
            P(),
        ),
        check_vma=False,
    )
```

```python
import functools

import jax
import jax.numpy as jnp
from jax import lax
from jax.experimental import pallas as pl
from jax.experimental.pallas import tpu as pltpu
from jax.sharding import PartitionSpec as P

HEADS = 16
HEAD_WIDTH = 48
SEG = 512
QB = 512
DILATION_STEP = 16


epsilon = 1e-05


def layer_norm(values, norm_gain, norm_shift):
    average = jnp.mean(values, axis=-1, keepdims=True)
    centered = values - average
    variance = jnp.mean(centered * centered, axis=-1, keepdims=True)
    return centered * lax.rsqrt(variance + epsilon) * norm_gain + norm_shift


def exact_gelu(values):
    return jax.nn.gelu(values, approximate=False)


def block_scores(query_block, seg_keys, seg_valid, distant_keys, distant_valid):
    nearby_scores = jnp.einsum(
        "iyo,uyo->yiu", query_block, seg_keys, preferred_element_type=jnp.float32
    )
    nearby_scores = jnp.where(seg_valid[None, None, :], nearby_scores, -1000000000.0)
    far_scores = jnp.einsum(
        "iyo,uyo->yiu",
        query_block[::DILATION_STEP],
        distant_keys,
        preferred_element_type=jnp.float32,
    )
    far_scores = jnp.where(distant_valid[None, None, :], far_scores, -1000000000.0)
    return (nearby_scores, far_scores)


def block_forward(
    query_block, seg_keys, seg_values, seg_valid, distant_keys, distant_values, distant_valid
):
    nearby_scores, far_scores = block_scores(
        query_block, seg_keys, seg_valid, distant_keys, distant_valid
    )
    head_number = nearby_scores.shape[0]
    row_number = nearby_scores.shape[1]
    chosen_count = row_number // DILATION_STEP
    maximum_table = jnp.max(nearby_scores, axis=-1).reshape(
        head_number, chosen_count, DILATION_STEP
    )
    combined_top = jnp.maximum(maximum_table[:, :, 0], jnp.max(far_scores, axis=-1))
    row_maximum = maximum_table.at[:, :, 0].set(combined_top).reshape(head_number, row_number)
    nearby_exponent = jnp.exp(nearby_scores - row_maximum[:, :, None])
    far_exp = jnp.exp(far_scores - combined_top[:, :, None])
    exponent_sums = jnp.sum(nearby_exponent, axis=-1).reshape(
        head_number, chosen_count, DILATION_STEP
    )
    combined_total = exponent_sums[:, :, 0] + jnp.sum(far_exp, axis=-1)
    row_sum_total = exponent_sums.at[:, :, 0].set(combined_total).reshape(head_number, row_number)
    local_weights = (nearby_exponent / row_sum_total[:, :, None]).astype(jnp.bfloat16)
    far_weights = (far_exp / combined_total[:, :, None]).astype(jnp.bfloat16)
    attended_rows = jnp.einsum(
        "hqk,khd->qhd", local_weights, seg_values, preferred_element_type=jnp.float32
    )
    distant_attended = jnp.einsum(
        "hqk,khd->qhd", far_weights, distant_values, preferred_element_type=jnp.float32
    )
    attended_rows = (
        attended_rows.reshape(chosen_count, DILATION_STEP, head_number, HEAD_WIDTH)
        .at[:, 0]
        .add(distant_attended)
    )
    return (attended_rows.reshape(row_number, head_number, HEAD_WIDTH), row_maximum, row_sum_total)


def block_backward(
    query_block,
    seg_keys,
    seg_values,
    seg_valid,
    distant_keys,
    distant_values,
    distant_valid,
    gradient_block,
    row_maximum,
    row_sum_total,
):
    nearby_scores, far_scores = block_scores(
        query_block, seg_keys, seg_valid, distant_keys, distant_valid
    )
    head_number = row_maximum.shape[0]
    row_number = row_maximum.shape[1]
    chosen_count = row_number // DILATION_STEP
    combined_top = row_maximum.reshape(head_number, chosen_count, DILATION_STEP)[:, :, 0]
    combined_total = row_sum_total.reshape(head_number, chosen_count, DILATION_STEP)[:, :, 0]
    nearby_probability = (
        jnp.exp(nearby_scores - row_maximum[:, :, None]) / row_sum_total[:, :, None]
    )
    far_prob = jnp.exp(far_scores - combined_top[:, :, None]) / combined_total[:, :, None]
    local_weights = nearby_probability.astype(jnp.bfloat16)
    gradient_sampled = gradient_block[::DILATION_STEP]
    value_grad = jnp.einsum(
        "mns,nmg->smg", local_weights, gradient_block, preferred_element_type=jnp.float32
    )
    nearby_dots = jnp.einsum(
        "iyo,uyo->yiu", gradient_block, seg_values, preferred_element_type=jnp.float32
    )
    far_dots = jnp.einsum(
        "iyo,uyo->yiu", gradient_sampled, distant_values, preferred_element_type=jnp.float32
    )
    delta_table = jnp.sum(nearby_probability * nearby_dots, axis=-1).reshape(
        head_number, chosen_count, DILATION_STEP
    )
    joint_delta = delta_table[:, :, 0] + jnp.sum(far_prob * far_dots, axis=-1)
    row_delta = delta_table.at[:, :, 0].set(joint_delta).reshape(head_number, row_number)
    local_slope = (nearby_probability * (nearby_dots - row_delta[:, :, None])).astype(jnp.bfloat16)
    distant_slope = (far_prob * (far_dots - joint_delta[:, :, None])).astype(jnp.bfloat16)
    query_gradient = jnp.einsum(
        "hqk,khd->qhd", local_slope, seg_keys, preferred_element_type=jnp.float32
    )
    distant_query = jnp.einsum(
        "hqk,khd->qhd", distant_slope, distant_keys, preferred_element_type=jnp.float32
    )
    query_gradient = (
        query_gradient.reshape(chosen_count, DILATION_STEP, head_number, HEAD_WIDTH)
        .at[:, 0]
        .add(distant_query)
    )
    key_grad = jnp.einsum(
        "mns,nmg->smg", local_slope, query_block, preferred_element_type=jnp.float32
    )
    far_weights = far_prob.astype(jnp.bfloat16)
    far_value_grad = jnp.einsum(
        "mns,nmg->smg", far_weights, gradient_sampled, preferred_element_type=jnp.float32
    )
    far_key_grad = jnp.einsum(
        "mns,nmg->smg",
        distant_slope,
        query_block[::DILATION_STEP],
        preferred_element_type=jnp.float32,
    )
    return (
        query_gradient.reshape(row_number, head_number, HEAD_WIDTH),
        key_grad,
        value_grad,
        far_key_grad,
        far_value_grad,
    )


def plain_device(
    tokens,
    qkv_weight,
    out_weight,
    up_weight,
    down_weight,
    norm1_gain,
    norm1_bias,
    norm2_gain,
    norm2_bias,
    visible,
    cotangent,
):
    row_number = tokens.shape[1]
    embedding_width = tokens.shape[2]
    query_scale = HEAD_WIDTH ** (-0.5)
    first_row = lax.axis_index("seq") * row_number
    positions = first_row + jnp.arange(row_number, dtype=jnp.int32)
    row_validity = positions < visible[0]
    inputs = tokens[0].astype(jnp.float32)
    norm_one, pull_one = jax.vjp(layer_norm, inputs, norm1_gain, norm1_bias)
    normed = norm_one.astype(jnp.bfloat16)
    projected = jnp.dot(normed, qkv_weight, preferred_element_type=jnp.float32)
    query_rows = (
        (projected[:, :embedding_width] * query_scale)
        .astype(jnp.bfloat16)
        .reshape(row_number, HEADS, HEAD_WIDTH)
    )
    flat_keys = projected[:, embedding_width : 2 * embedding_width].astype(jnp.bfloat16)
    flat_values = projected[:, 2 * embedding_width :].astype(jnp.bfloat16)
    key_matrix = flat_keys.reshape(row_number, HEADS, HEAD_WIDTH)
    value_matrix = flat_values.reshape(row_number, HEADS, HEAD_WIDTH)
    gathered_keys, gathered_values = (
        lax.all_gather(flat_keys[::DILATION_STEP], "seq", axis=0, tiled=True),
        lax.all_gather(flat_values[::DILATION_STEP], "seq", axis=0, tiled=True),
    )
    distant_count = gathered_keys.shape[0]
    distant_valid = jnp.arange(distant_count, dtype=jnp.int32) * DILATION_STEP < visible[0]
    distant_keys = gathered_keys.reshape(distant_count, HEADS, HEAD_WIDTH)
    distant_values = gathered_values.reshape(distant_count, HEADS, HEAD_WIDTH)
    per_segment = SEG // QB
    attended_rows, row_maximum, row_sum_total = block_forward(
        query_rows,
        key_matrix,
        value_matrix,
        row_validity,
        distant_keys,
        distant_values,
        distant_valid,
    )
    attn_low = attended_rows.reshape(row_number, embedding_width).astype(jnp.bfloat16)
    after_attn = inputs + jnp.dot(attn_low, out_weight, preferred_element_type=jnp.float32)
    norm_two, pull_two = jax.vjp(layer_norm, after_attn, norm2_gain, norm2_bias)
    normed_two = norm_two.astype(jnp.bfloat16)
    up_cols = jnp.dot(normed_two, up_weight, preferred_element_type=jnp.float32)
    activated, pull_gelu = jax.vjp(exact_gelu, up_cols)
    hidden = activated.astype(jnp.bfloat16)
    result = after_attn + jnp.dot(hidden, down_weight, preferred_element_type=jnp.float32)
    mixed_out = jnp.where(row_validity[:, None], result, 0.0).astype(jnp.bfloat16)[None]
    grad_out = jnp.where(row_validity[:, None], cotangent[0], jnp.zeros_like(cotangent[0]))
    down_grad = jnp.einsum("tf,td->fd", hidden, grad_out, preferred_element_type=jnp.float32)
    hidden_grad = jnp.einsum("td,fd->tf", grad_out, down_weight, preferred_element_type=jnp.float32)
    (up_slope,) = pull_gelu(hidden_grad)
    up_low = up_slope.astype(jnp.bfloat16)
    up_grad = jnp.einsum("td,tf->df", normed_two, up_low, preferred_element_type=jnp.float32)
    norm_two_in = jnp.einsum("tf,df->td", up_low, up_weight, preferred_element_type=jnp.float32)
    after_part, gain_two_grad, shift_two_grad = pull_two(norm_two_in)
    resid_grad = grad_out.astype(jnp.float32) + after_part
    resid_low = resid_grad.astype(jnp.bfloat16)
    out_grad = jnp.einsum("td,te->de", attn_low, resid_low, preferred_element_type=jnp.float32)
    attn_grad = jnp.einsum("te,de->td", resid_low, out_weight, preferred_element_type=jnp.float32)
    attn_grad = attn_grad.astype(jnp.bfloat16).reshape(row_number, HEADS, HEAD_WIDTH)
    query_gradient, key_grad, value_grad, far_key_grad, far_value_grad = block_backward(
        query_rows,
        key_matrix,
        value_matrix,
        row_validity,
        distant_keys,
        distant_values,
        distant_valid,
        attn_grad,
        row_maximum,
        row_sum_total,
    )
    key_list = [key_grad]
    value_list = [value_grad]
    owned_keys, owned_values = (
        lax.psum_scatter(
            far_key_grad.reshape(distant_count, embedding_width),
            "seq",
            scatter_dimension=0,
            tiled=True,
        ),
        lax.psum_scatter(
            far_value_grad.reshape(distant_count, embedding_width),
            "seq",
            scatter_dimension=0,
            tiled=True,
        ),
    )
    chosen_count = row_number // DILATION_STEP
    segment_count = row_number // SEG
    nearby_keys = jnp.sum(
        jnp.stack(key_list).reshape(segment_count, per_segment, SEG, embedding_width), axis=1
    )
    nearby_values = jnp.sum(
        jnp.stack(value_list).reshape(segment_count, per_segment, SEG, embedding_width), axis=1
    )
    key_total = (
        nearby_keys.reshape(chosen_count, DILATION_STEP, embedding_width)
        .at[:, 0]
        .add(owned_keys)
        .reshape(row_number, embedding_width)
    )
    value_total = (
        nearby_values.reshape(chosen_count, DILATION_STEP, embedding_width)
        .at[:, 0]
        .add(owned_values)
        .reshape(row_number, embedding_width)
    )
    query_total = query_gradient.reshape(row_number, embedding_width)
    mixed_grad = jnp.concatenate(
        [
            (query_total * query_scale).astype(jnp.bfloat16),
            key_total.astype(jnp.bfloat16),
            value_total.astype(jnp.bfloat16),
        ],
        axis=1,
    )
    qkv_grad = jnp.einsum("td,tf->df", normed, mixed_grad, preferred_element_type=jnp.float32)
    norm_one_in = jnp.einsum(
        "tf,df->td", mixed_grad, qkv_weight, preferred_element_type=jnp.float32
    )
    input_part, gain_one_grad, shift_one_grad = pull_one(norm_one_in)
    tokens_grad = (resid_grad + input_part).astype(jnp.bfloat16)[None]
    weight_grads = (qkv_grad, out_grad, up_grad, down_grad)
    row_parts = (
        lax.psum_scatter(weight_grads[0], "seq", scatter_dimension=0, tiled=True),
        lax.psum_scatter(weight_grads[1], "seq", scatter_dimension=0, tiled=True),
        lax.psum_scatter(weight_grads[2], "seq", scatter_dimension=0, tiled=True),
        lax.psum_scatter(weight_grads[3], "seq", scatter_dimension=0, tiled=True),
    )
    final_grads = (
        lax.psum(row_parts[0].astype(jnp.bfloat16), "slide").astype(jnp.float32),
        lax.psum(row_parts[1].astype(jnp.bfloat16), "slide").astype(jnp.float32),
        lax.psum(row_parts[2].astype(jnp.bfloat16), "slide").astype(jnp.float32),
        lax.psum(row_parts[3].astype(jnp.bfloat16), "slide").astype(jnp.float32),
    )
    norm_grads = lax.psum(
        (gain_one_grad, shift_one_grad, gain_two_grad, shift_two_grad), ("seq", "slide")
    )
    return (
        mixed_out,
        tokens_grad,
        final_grads[0],
        final_grads[1],
        final_grads[2],
        final_grads[3],
        norm_grads[0],
        norm_grads[1],
        norm_grads[2],
        norm_grads[3],
    )


MESH = pl.DeviceIdType.MESH
LOW = jnp.bfloat16
FULL = jnp.float32
AUG = 64
LANES = 128
NEVER = -2000000000.0
ANY = pl.BlockSpec(memory_space=pl.ANY)
VMEM = pl.BlockSpec(memory_space=pltpu.VMEM)
SMEM = pl.BlockSpec(memory_space=pltpu.SMEM)


def nn(left, right):
    return jnp.dot(left, right, preferred_element_type=FULL)


def nt(left, right):
    return lax.dot_general(left, right, (((1,), (1,)), ((), ())), preferred_element_type=FULL)


def tn(left, right):
    return lax.dot_general(left, right, (((0,), (0,)), ((), ())), preferred_element_type=FULL)


def remote(src, dst, send_sem, recv_sem, device):
    return pltpu.make_async_remote_copy(
        src_ref=src,
        dst_ref=dst,
        send_sem=send_sem,
        recv_sem=recv_sem,
        device_id=device,
        device_id_type=MESH,
    )


def greet(devices):
    barrier = pltpu.get_barrier_semaphore()
    for device in devices:
        pl.semaphore_signal(barrier, inc=1, device_id=device, device_id_type=MESH)
    pl.semaphore_wait(barrier, len(devices))


def row_peers(count):
    seq, slide = lax.axis_index("seq"), lax.axis_index("slide")
    return [(lax.rem(seq + step, count), slide) for step in range(1, count)]


def spread(ref, values):
    for group in range(ref.shape[0]):
        ref[group] = values[:, group * LANES : (group + 1) * LANES]


def strided_rows(ref, step, count):
    groups = [
        ref[group, pl.ds(step, count, stride=DILATION_STEP), :] for group in range(ref.shape[0])
    ]
    return jnp.concatenate(groups, axis=1)


def strided_store(ref, step, count, values):
    for group in range(ref.shape[0]):
        ref[group, pl.ds(step, count, stride=DILATION_STEP), :] = values[
            :, group * LANES : (group + 1) * LANES
        ]


def chunk(step, size):
    return pl.ds(pl.multiple_of(step * size, size), size)


def steps(body):
    @pl.loop(0, DILATION_STEP // 4)
    def _(group):
        for member in range(4):
            body(group * 4 + member)


def row_mean(values):
    return jnp.mean(values, axis=-1, keepdims=True)


def fold_rows(values):
    return jnp.sum(values.reshape(-1, 8, values.shape[-1]), axis=0)


def mask_rows(ref, bias):
    first = lax.broadcasted_iota(jnp.int32, (AUG - HEAD_WIDTH, ref.shape[2]), 0) == 0
    ref[:, HEAD_WIDTH:, :] = jnp.broadcast_to(
        jnp.where(first, bias, 0.0).astype(LOW), (HEADS, AUG - HEAD_WIDTH, ref.shape[2])
    )


class Place:
    def __init__(self):
        seq, slide = lax.axis_index("seq"), lax.axis_index("slide")
        self.seq, self.slide = seq, slide
        self.z, self.x = seq // 2, seq % 2
        self.b, self.a = self.z // 2, self.z % 2
        self.y, self.c = slide // 2, slide % 2
        self.sibling = (seq, slide + 1 - 2 * self.c)
        self.across_y = (seq, slide + 2 - 4 * self.y)
        self.diagonal = (seq, 3 - slide)
        self.across_x = (seq + 1 - 2 * self.x, slide)
        self.slide_peers = (self.sibling, self.across_y, self.diagonal)

    def layer(self, step):
        return (self.z + step) % 4


class Part:
    def __init__(self, place, orders, folds, both, core_got, got, final, send_sem, recv_sem):
        self.place, self.orders, self.both = place, orders, both
        self.core_got, self.got, self.final = core_got, got, final
        self.send_sem, self.recv_sem = send_sem, recv_sem
        self.folds = folds

    def blocks(self, core, phase, value):
        choices = {}
        for at, name in enumerate(self.orders[core], 1):
            if at < phase:
                choices[name] = [getattr(self.place, name)]
            elif at == phase:
                choices[name] = [value]
            else:
                choices[name] = list(range(4 if name == "z" else 2))
        if "z" not in choices:
            choices["z"] = [2 * b + a for b in choices["b"] for a in choices["a"]]
        return [(2 * z + x, y) for z in choices["z"] for x in choices["x"] for y in choices["y"]]

    def partners(self, core, phase):
        place, name = self.place, self.orders[core][phase - 1]
        if name == "x":
            return [(1 - place.x, place.across_x)]
        if name == "y":
            return [(1 - place.y, place.across_y)]
        if name == "a":
            return [(1 - place.a, (place.seq + 2 - 4 * place.a, place.slide))]
        if name == "b":
            return [(1 - place.b, (place.seq + 4 - 8 * place.b, place.slide))]
        layers = [place.layer(k) for k in (1, 2, 3)]
        return [(z, (2 * z + place.x, place.slide)) for z in layers]

    def span(self, core, phase):
        first, left = 0, 16
        for at, name in enumerate(self.orders[core], 1):
            left //= 4 if name == "z" else 2
            number = left * (3 if name == "z" else 1)
            if at == phase:
                return first, number
            first += number

    def transfers(self, core, phase):
        kept, got = self.both.at[0], self.got
        slot = self.span(core, phase)[0]
        pairs = "y" in self.orders[core][phase:]
        moves = []
        for value, device in self.partners(core, phase):
            for owner, y in self.blocks(core, phase, value):
                if not pairs:
                    moves.append((kept.at[owner, y], got.at[slot], device))
                elif y == 0:
                    moves.append((kept.at[owner], got.at[pl.ds(slot, 2)], device))
                slot += 1
        return moves

    def start(self, phase, merged):
        place, send, recv = self.place, self.send_sem.at[phase], self.recv_sem.at[phase]
        if phase == 0:
            remote(self.both.at[1], self.core_got, send, recv, place.sibling).start()
        elif phase <= self.folds:
            for core in range(2):
                if phase > len(self.orders[core]):
                    continue

                @pl.when(place.c == core)
                def _(core=core):
                    for source, target, device in self.transfers(core, phase):
                        remote(source, target, send, recv, device).start()
        elif phase == self.folds + 1:
            own = self.final.at[place.c * 2 + place.y]
            for device in place.slide_peers if merged else (place.across_y,):
                remote(own, own, send, recv, device).start()
        else:
            own = self.final.at[pl.ds(place.c * 2, 2)]
            remote(own, own, send, recv, place.sibling).start()

    def wait(self, phase, whole):
        both_ways = remote(
            whole, whole, self.send_sem.at[phase], self.recv_sem.at[phase], self.place.sibling
        )
        both_ways.wait_recv()
        both_ways.wait_send()

    def finish(self, phase, merged):
        place = self.place
        if phase == 0:
            self.wait(phase, self.core_got)

            @pl.loop(0, 8)
            def _(owner):
                for row in range(2):
                    self.both[0, owner, row] += self.core_got[owner, row]
        elif phase <= self.folds:
            for core in range(2):
                if phase > len(self.orders[core]):
                    continue

                @pl.when(place.c == core)
                def _(core=core):
                    first, number = self.span(core, phase)
                    self.wait(phase, self.got.at[pl.ds(first, number)])
                    name = self.orders[core][phase - 1]
                    blocks = self.blocks(core, phase, getattr(place, name))
                    for n, (owner, y) in enumerate(blocks):
                        slots = range(first + n, first + number, len(blocks))
                        self.add(owner, y, slots, core if phase == len(self.orders[core]) else None)
        elif phase == self.folds + 1:
            self.wait(phase, self.final.at[pl.ds(0, 3 if merged else 1)])
        else:
            self.wait(phase, self.final.at[pl.ds(0, 2)])

    def add(self, owner, y, slots, core):
        if len(slots) == 1:
            total = self.both[0, owner, y] + self.got[slots[0]]
        else:
            total = self.both[0, owner, y].astype(FULL)
            for slot in slots:
                total = total + self.got[slot].astype(FULL)
            total = total.astype(LOW)
        if core is None:
            self.both[0, owner, y] = total
        else:
            self.final[core * 2 + self.place.y] = total


class Piece:
    def __init__(self, parts, merged, outs, out_sem):
        self.parts, self.merged, self.outs, self.out_sem = parts, merged, outs, out_sem
        self.last = parts[0].folds + (1 if merged else 2)
        self.phase = -1

    @property
    def done(self):
        return self.phase > self.last

    def advance(self):
        if self.done:
            return
        if self.phase >= 0:
            for part in self.parts:
                part.finish(self.phase, self.merged)
        self.phase += 1
        if not self.done:
            for part in self.parts:
                part.start(self.phase, self.merged)
            return
        for n in range(len(self.parts)):
            self.out_copy(n).start()

    def out_copy(self, n):
        return pltpu.make_async_copy(self.parts[n].final, self.outs[n], self.out_sem.at[n])


LN_TWO = 0.6931471805599453
QUERY_SCALE = HEAD_WIDTH ** (-0.5) / LN_TWO
TILES = 3
LASTS = 4
PIECES = TILES + LASTS
ORDERS = (
    (('yxab', 'zxy', 'xyz', 'zyx'), False),
    (('yxab', 'ayxb', 'xyz', 'yxz'), False),
    (('xyz', 'yaxb', 'yzx', 'abyx'), False),
    (('yabx', 'xaby'), False),
    (('yzx', 'xyz'), False),
    (('yxab', 'xayb'), True),
    (('yxz', 'xyz'), True),
)
HOOKS = {
    "tile1.1": (0,),
    "tile2.1": (1,),
    "after2": (2,),
    "far": (0, 1),
    "near3": (2,),
    "near4": (0, 3, 4),
    "near5": (1,),
    "last2": (3, 2),
    "last3": (5,),
    "into": (0, 6, 4),
    "norm": (1,),
}
TAIL = (5, 3, 2, 0, 6, 5, 4, 0, 1, 6, 0, 5, 3, 2, 4, 1, 3, 1, 6, 2, 5, 4, 3, 2, 4, 3, 6, 5)

def main_kernel(
    count, tokens, cotangent, qkv_weight, out_weight, up_weight, down_weight,
    gain_one, shift_one, gain_two, shift_two, visible,
    mixed_out, tokens_out, down_sums, up_sums, last_sums, norm_out, weights_kept, norm_kept,
    normed, far_normed, query, key, value, far_key, far_value, far_weights, scale, far_scale, attn,
    delta, slope, resid, after, dyb, wqkv, wo, wide, staged, all_far, far_got, spread_one,
    sums, around, across,
    down_both, up_both, last_both, down_core, up_core, last_core,
    down_got, up_got, last_got, down_final, up_final, last_final,
    load_sem, tile_sem, group_sem, store_sem, out_sem, send_sem, recv_sem,
    gather_send_sem, gather_recv_sem, far_send_sem, far_recv_sem, norm_send_sem, norm_recv_sem,
):
    place = Place()
    seq, core = place.seq, place.c
    rows, width = resid.shape
    chosen = rows // DILATION_STEP
    group_lanes = LANES
    tile_width = count * group_lanes
    first_row = seq * rows
    limit = visible[0]
    peers = row_peers(count)
    others = list(place.slide_peers) + peers
    barrier = pltpu.get_barrier_semaphore()
    for other in others:
        pl.semaphore_signal(barrier, inc=1, device_id=other, device_id_type=MESH)

    def valid_rows(step):
        places = lax.broadcasted_iota(jnp.int32, (chosen, 1), 0) * DILATION_STEP + step
        return first_row + places < limit

    def landed(n):
        sources = (
            (tokens, staged),
            (qkv_weight.at[:, pl.ds(width, width)], wqkv.at[1]),
            (qkv_weight.at[:, pl.ds(2 * width, width)], wqkv.at[2]),
            (qkv_weight.at[:, pl.ds(0, width)], wqkv.at[0]),
            (out_weight, wo),
            (cotangent, staged),
        )
        return pltpu.make_async_copy(*sources[n], load_sem.at[n])

    for n in range(5):
        landed(n).start()
    distant = count * chosen
    members = 4

    def kept_group(group, slots):
        kept = weights_kept.at[pl.ds(group * members, members)]
        return slots.at[group % 2], kept, group_sem.at[group % 2]

    pieces = []
    for n in range(TILES):
        parts = [
            Part(
                place,
                ORDERS[n][0][2 * which : 2 * which + 2],
                max(len(order) for order in ORDERS[n][0]),
                both.at[n],
                core_got.at[n],
                got.at[n],
                final.at[n],
                send_sem.at[n, which],
                recv_sem.at[n, which],
            )
            for which, (both, core_got, got, final) in enumerate(
                (
                    (down_both, down_core, down_got, down_final),
                    (up_both, up_core, up_got, up_final),
                )
            )
        ]
        pieces.append(Piece(parts, ORDERS[n][1], (down_sums.at[n], up_sums.at[n]), out_sem.at[n]))
    for n in range(LASTS):
        part = Part(
            place,
            ORDERS[TILES + n][0],
            max(len(order) for order in ORDERS[TILES + n][0]),
            last_both.at[n],
            last_core.at[n],
            last_got.at[n],
            last_final.at[n],
            send_sem.at[TILES + n, 0],
            recv_sem.at[TILES + n, 0],
        )
        pieces.append(Piece([part], ORDERS[TILES + n][1], (last_sums.at[n],), out_sem.at[TILES + n]))

    def hook(name):
        for n in HOOKS.get(name, ()):
            if pieces[n].phase >= 0:
                pieces[n].advance()

    def split_last(n, side, grads):
        target = last_both.at[n, (side + core) % 2]
        target[...] = grads.astype(LOW).reshape(count, 2, -1, grads.shape[1])

    def attend_part(h1, top, total, attended, weights):
        landed(0).wait()
        spread(wide, staged[...].astype(FULL))
        landed(5).start()

        def normalize(step):
            at = chunk(step, chosen)
            values = strided_rows(wide, step, chosen)
            centered = values - row_mean(values)
            inverse = lax.rsqrt(row_mean(centered * centered) + epsilon)
            normal = centered * inverse
            after[at] = values
            resid[at] = normal
            spread_one[at] = jnp.broadcast_to(inverse, (chosen, LANES))
            low = (normal * gain_one[...][None] + shift_one[...][None]).astype(LOW)
            h1[at] = low
            return low

        all_far[seq] = normalize(0)

        @pl.loop(0, 5)
        def _(group):
            for member in range(3):
                normalize(group * 3 + member + 1)

        pltpu.make_async_copy(resid, norm_kept, store_sem.at[0]).start()
        for part, ref in ((1, key), (2, value)):
            landed(part).wait()
            projected = nn(h1[...], wqkv[part]).astype(LOW)
            ref[:, :HEAD_WIDTH, :] = projected.T.reshape(HEADS, HEAD_WIDTH, rows)
            if part == 1:
                pl.semaphore_wait(barrier, len(others))
                for n, peer in enumerate(peers):
                    mine = all_far.at[seq]
                    send, recv = gather_send_sem.at[n], gather_recv_sem.at[n]
                    remote(mine, mine, send, recv, peer).start()
        landed(3).wait()
        projected = (nn(h1[...], wqkv[0]) * QUERY_SCALE).astype(LOW)
        query[:, :HEAD_WIDTH, :] = projected.T.reshape(HEADS, HEAD_WIDTH, rows)
        places = lax.broadcasted_iota(jnp.int32, (1, rows), 1)
        places = first_row + (places % chosen) * DILATION_STEP + places // chosen
        mask_rows(key, jnp.where(places < limit, 0.0, NEVER))
        mask_rows(query, jnp.ones((1, rows), FULL))
        mask_rows(value, jnp.ones((1, rows), FULL))

        @pl.loop(0, HEADS // members)
        def _(group):
            slot, kept, sem = kept_group(group, weights)

            @pl.when(group >= 2)
            def _():
                pltpu.make_async_copy(slot, kept, sem).wait()

            for member in range(members):
                head = group * members + member
                scores = tn(key[head], query[head])
                highest = jnp.max(scores, axis=0, keepdims=True)
                low = jnp.exp2(scores - highest).astype(LOW)
                top[head] = highest
                weights[group % 2, member] = low
                result = nn(value[head], low)
                attended[head] = result[:HEAD_WIDTH]
                total[head] = result[HEAD_WIDTH : HEAD_WIDTH + 1]
            pltpu.make_async_copy(slot, kept, sem).start()

        normed[...] = h1[...].T
        landed(5).wait()
        spread(wide, staged[...].astype(FULL))

        @steps
        def _(step):
            at = chunk(step, chosen)
            dyb[at] = jnp.where(valid_rows(step), strided_rows(wide, step, chosen), 0.0).astype(LOW)

        for n in range(count - 1):
            source = lax.rem(seq + count - 1 - n, count)
            mine, theirs = all_far.at[seq], all_far.at[source]
            wait = remote(mine, theirs, gather_send_sem.at[n], gather_recv_sem.at[n], peers[0])
            wait.wait_recv()
            wait.wait_send()
        flat = all_far[...].reshape(distant, width)
        for part, ref in ((1, far_key), (2, far_value)):
            projected = nn(flat, wqkv[part]).astype(LOW)
            ref[:, :HEAD_WIDTH, :] = projected.T.reshape(HEADS, HEAD_WIDTH, distant)
        places = lax.broadcasted_iota(jnp.int32, (1, distant), 1) * DILATION_STEP
        mask_rows(far_key, jnp.where(places < limit, 0.0, NEVER))
        mask_rows(far_value, jnp.ones((1, distant), FULL))
        lane_mask = jnp.where(lax.broadcasted_iota(jnp.int32, (1, LANES), 1) < chosen, 0.0, NEVER)

        @pl.loop(0, HEADS // 4)
        def _(group):
            for member in range(4):
                head = group * 4 + member
                scores = tn(far_key[head], query[head][:, :LANES]) + lane_mask
                highest = jnp.max(scores, axis=0, keepdims=True)
                low = jnp.exp2(scores - highest).astype(LOW)
                far_weights[head] = low
                near = top[head][:, :LANES]
                joint = jnp.maximum(near, highest)
                near_part, far_part = jnp.exp2(near - joint), jnp.exp2(highest - joint)
                far_result = nn(far_value[head], low)
                far_total = far_result[HEAD_WIDTH : HEAD_WIDTH + 1]
                joint_total = total[head][:, :LANES] * near_part + far_total * far_part
                near_part, far_part = near_part / joint_total, far_part / joint_total
                far_scale[head] = far_part
                local = jnp.concatenate([near_part, 1.0 / total[head][:, LANES:]], axis=1)
                scale[head] = local
                result = attended[head] * local
                with_far = result[:, :LANES] + far_result[:HEAD_WIDTH] * far_part
                result = jnp.concatenate([with_far, result[:, LANES:]], axis=1)
                attn[head] = result.astype(LOW)

        for group in (2, 3):
            slot, kept, sem = kept_group(group, weights)
            pltpu.make_async_copy(slot, kept, sem).wait()
        pltpu.make_async_copy(resid, norm_kept, store_sem.at[0]).wait()

    vm = pltpu.VMEM
    pl.run_scoped(
        attend_part,
        vm((rows, width), LOW),
        vm((HEADS, 1, rows), FULL),
        vm((HEADS, 1, rows), FULL),
        vm((HEADS, HEAD_WIDTH, rows), FULL),
        vm((2, members, rows, rows), LOW),
    )

    def forward_part(norm_two, spread_two, h2, h2_t, active, low_slope, wup, wdown):
        halves = 2
        per_half = tile_width // halves

        def load_tile(tile, half):
            for local in range(count // halves):
                owner = half * (count // halves) + local
                first = owner * TILES * group_lanes + tile * group_lanes
                at = pl.ds(pl.multiple_of(first, LANES), group_lanes)
                to = pl.ds(local * group_lanes, group_lanes)
                pltpu.make_async_copy(
                    up_weight.at[:, at], wup.at[half, :, to], tile_sem.at[half, 0]
                ).start()
                pltpu.make_async_copy(
                    down_weight.at[at], wdown.at[half, to], tile_sem.at[half, 1]
                ).start()

        def wait_tile(half):
            pltpu.make_async_copy(wup.at[half], wup.at[half], tile_sem.at[half, 0]).wait()
            pltpu.make_async_copy(wdown.at[half], wdown.at[half], tile_sem.at[half, 1]).wait()

        load_tile(0, 0)
        load_tile(0, 1)
        landed(4).wait()
        after[...] += nn(attn[...].reshape(width, rows).T, wo[...])

        @steps
        def _(step):
            at = chunk(step, chosen)
            values = after[at]
            centered = values - row_mean(values)
            inverse = lax.rsqrt(row_mean(centered * centered) + epsilon)
            normal = centered * inverse
            norm_two[at] = normal
            spread_two[at] = jnp.broadcast_to(inverse, (chosen, LANES))
            h2[at] = (normal * gain_two[...][None] + shift_two[...][None]).astype(LOW)
            resid[at] = jnp.zeros((chosen, width), FULL)

        h2_t[...] = h2[...].T
        for tile in range(TILES):
            @pl.loop(0, halves)
            def _(half, tile=tile):
                wait_tile(half)
                to = pl.ds(pl.multiple_of(half * per_half, LANES), per_half)
                hidden = nn(h2[...], wup[half])
                hidden_slope = nt(dyb[...], wdown[half])
                share = 0.5 * (1.0 + lax.erf(hidden * 0.7071067811865476))
                active[:, to] = (hidden * share).astype(LOW)
                density = hidden * jnp.exp(-0.5 * hidden * hidden) * 0.3989422804014327
                low_slope[:, to] = (hidden_slope * (share + density)).astype(LOW)
                after[...] += nn(active[:, to], wdown[half])
                resid[...] += nt(low_slope[:, to], wup[half])
                if tile + 1 < TILES:
                    load_tile(tile + 1, half)

            hook("tile%d.1" % tile)

            @pl.loop(0, 4)
            def _(part, tile=tile):
                at = pl.ds(pl.multiple_of(part * tile_width // 4, LANES), tile_width // 4)
                grads = nn(h2_t[...], low_slope[:, at]).astype(LOW)
                target = up_both.at[tile, (part // 2 + core) % 2]
                target[:, part % 2] = grads.reshape(count, -1, grads.shape[1])
                grads = tn(active[:, at], dyb[...]).astype(LOW)
                owners = count // 4
                grads = grads.reshape(owners, 2, 2, -1, width)
                for side in range(2):
                    target = down_both.at[tile, (side + core) % 2]
                    target[pl.ds(part * owners, owners)] = grads[:, side]

            pieces[tile].advance()
            hook("tile%d.3" % tile)
        sums[...] = jnp.zeros_like(sums)
        hook("after0")

        @steps
        def _(step):
            at = chunk(step, chosen)
            strided_store(wide, step, chosen, jnp.where(valid_rows(step), after[at], 0.0))
            given, normal = resid[at], norm_two[at]
            sums[2] += fold_rows(given * normal)
            sums[3] += fold_rows(given)
            scaled = given * gain_two[...][None]
            part = scaled - row_mean(scaled) - normal * row_mean(scaled * normal)
            value_here = dyb[at].astype(FULL) + spread_two[at][:, :1] * part
            resid[at] = value_here
            h2[at] = value_here.astype(LOW)

        for group in range(width // LANES):
            staged[:, group * LANES : (group + 1) * LANES] = wide[group].astype(LOW)
        pltpu.make_async_copy(staged, mixed_out, store_sem.at[1]).start()
        half = width // 2
        hook("after1")
        for n in range(2):
            at = slice(n * half, (n + 1) * half)
            split_last(2 * n + 1, 1, nn(attn[...].reshape(width, rows), h2[:, at]))
        slope[...] = nt(wo[...], h2[...]).astype(LOW).reshape(HEADS, HEAD_WIDTH, rows)

        @pl.loop(0, HEADS)
        def _(head):
            product = slope[head].astype(FULL) * attn[head].astype(FULL)
            delta[head] = jnp.sum(product, axis=0, keepdims=True)

        hook("after2")

    pl.run_scoped(
        forward_part,
        vm((rows, width), FULL),
        vm((rows, LANES), FULL),
        vm((rows, width), LOW),
        vm((width, rows), LOW),
        vm((rows, tile_width), LOW),
        vm((rows, tile_width), LOW),
        vm((2, width, tile_width // 2), LOW),
        vm((2, tile_width // 2, width), LOW),
    )

    def backward_part(weights, slopes, far_query, far_send, given):
        norm_one = after

        def load_group(group):
            slot, kept, sem = kept_group(group, weights)
            return pltpu.make_async_copy(kept, slot, sem)

        load_group(0).start()
        load_group(1).start()
        norm_load = pltpu.make_async_copy(norm_kept, norm_one, store_sem.at[0])
        norm_load.start()

        @pl.loop(0, HEADS // 4)
        def _(group):
            for member in range(4):
                head = group * 4 + member
                first_slope = slope[head][:, :LANES]
                low = far_weights[head]
                change = tn(far_value[head, :HEAD_WIDTH], first_slope) - delta[head][:, :LANES]
                score_slope = (low.astype(FULL) * far_scale[head] * change).astype(LOW)
                far_query[head] = nn(far_key[head, :HEAD_WIDTH], score_slope)
                scaled = (first_slope.astype(FULL) * far_scale[head]).astype(LOW)
                key_slope = nt(query[head, :HEAD_WIDTH, :LANES], score_slope)
                given[0, head] = (key_slope * LN_TWO).astype(LOW)
                given[1, head] = nt(scaled, low).astype(LOW)

        hook("far0")
        far_normed[...] = all_far[...].reshape(distant, width).T
        into = nn(wqkv[1], given[0].reshape(width, distant))
        into += nn(wqkv[2], given[1].reshape(width, distant))
        far_send[...] = into.T.astype(LOW).reshape(count, chosen, width)
        for n, peer in enumerate(peers):
            remote(
                far_send.at[peer[0]], far_got.at[n], far_send_sem.at[n], far_recv_sem.at[n], peer
            ).start()
        hook("far")

        def weight_slopes(half):
            at = slice(half * HEADS // 2, (half + 1) * HEADS // 2)
            for part, (n, side) in enumerate(((0, 0), (0, 1), (1, 0))):
                grads = nt(normed[...], slopes[part, at].reshape(width // 2, rows))
                if part:
                    far = given[part - 1, at].reshape(width // 2, distant)
                    grads += nt(far_normed[...], far)
                split_last(2 * half + n, side, grads)
                if part:
                    pieces[TILES + 2 * half + n].advance()
                    hook("last%d" % (2 * half + n))

        for group in range(HEADS // members):
            load_group(group).wait()
            for member in range(members):
                head = group * members + member
                low = weights[group % 2, member]
                change = tn(value[head, :HEAD_WIDTH], slope[head]) - delta[head]
                score_slope = (low.astype(FULL) * scale[head] * change).astype(LOW)
                query_slope = nn(key[head, :HEAD_WIDTH], score_slope)
                key_slope = nt(query[head, :HEAD_WIDTH], score_slope)
                scaled = (slope[head].astype(FULL) * scale[head]).astype(LOW)
                value_slope = nt(scaled, low)
                first = query_slope[:, :LANES] + far_query[head]
                query_slope = jnp.concatenate([first, query_slope[:, LANES:]], axis=1)
                slopes[0, head] = (query_slope * HEAD_WIDTH ** (-0.5)).astype(LOW)
                slopes[1, head] = (key_slope * LN_TWO).astype(LOW)
                slopes[2, head] = value_slope.astype(LOW)
                if member % 2:
                    hook("near%d" % (head // 2))
            if (group + 2) * members < HEADS:
                load_group(group + 2).start()
            if group % 2:
                weight_slopes(group // 2)

        def flat_slopes(part):
            return slopes[part].reshape(width, rows)

        into = nn(wqkv[0], flat_slopes(0))
        into += nn(wqkv[1], flat_slopes(1))
        into += nn(wqkv[2], flat_slopes(2))
        norm_load.wait()
        pltpu.make_async_copy(staged, mixed_out, store_sem.at[1]).wait()
        spread(wide, into.T)
        hook("into")
        total = far_send[seq].astype(FULL)
        for n in range(count - 1):
            wait = remote(
                far_got.at[n], far_got.at[n], far_send_sem.at[n], far_recv_sem.at[n], peers[0]
            )
            wait.wait_recv()
            wait.wait_send()
            total = total + far_got[n].astype(FULL)
        for group in range(width // LANES):
            wide[group, :chosen] += total[:, group * LANES : (group + 1) * LANES]

        @steps
        def _(step):
            at = chunk(step, chosen)
            here = jnp.concatenate([wide[group, at, :] for group in range(width // LANES)], axis=1)
            normal = norm_one[at]
            sums[0] += fold_rows(here * normal)
            sums[1] += fold_rows(here)
            scaled = here * gain_one[...][None]
            part = scaled - row_mean(scaled) - normal * row_mean(scaled * normal)
            resid[at] += spread_one[at][:, :1] * part

    pl.run_scoped(
        backward_part,
        vm((2, members, rows, rows), LOW),
        vm((3, HEADS, HEAD_WIDTH, rows), LOW),
        vm((HEADS, HEAD_WIDTH, LANES), FULL),
        vm((count, chosen, width), LOW),
        vm((2, HEADS, HEAD_WIDTH, distant), LOW),
    )
    for n in range(4):
        around[seq, pl.ds(n, 1)] = jnp.sum(sums[n], axis=0, keepdims=True)
    for n, peer in enumerate(peers):
        mine = around.at[seq]
        remote(mine, mine, norm_send_sem.at[n], norm_recv_sem.at[n], peer).start()
    hook("norm")

    @steps
    def _(step):
        strided_store(wide, step, chosen, resid[chunk(step, chosen)])

    for group in range(width // LANES):
        staged[:, group * LANES : (group + 1) * LANES] = wide[group].astype(LOW)
    tokens_copy = pltpu.make_async_copy(staged, tokens_out, store_sem.at[2])
    tokens_copy.start()
    for n in range(count - 1):
        mine = around.at[seq]
        wait = remote(mine, mine, norm_send_sem.at[n], norm_recv_sem.at[n], peers[0])
        wait.wait_recv()
        wait.wait_send()
    total = around[0]
    for n in range(1, count):
        total = total + around[n]
    across[place.slide] = total
    for n, peer in enumerate(place.slide_peers):
        mine, at = across.at[place.slide], count - 1 + n
        remote(mine, mine, norm_send_sem.at[at], norm_recv_sem.at[at], peer).start()
    for n in TAIL + tuple(range(PIECES)) * 6:
        pieces[n].advance()
    for n in range(3):
        mine, at = across.at[0], count - 1 + n
        wait = remote(mine, mine, norm_send_sem.at[at], norm_recv_sem.at[at], peers[0])
        wait.wait_recv()
        wait.wait_send()
    norm_out[...] = (across[0] + across[1]) + (across[2] + across[3])
    for piece in pieces:
        for n in range(len(piece.parts)):
            piece.out_copy(n).wait()
    tokens_copy.wait()


def main_pass(count, tokens, cotangent, weights, norms, visible):
    rows, width = tokens.shape
    chosen = rows // DILATION_STEP
    distant = count * chosen
    owned = width // count
    vm, dma = pltpu.VMEM, pltpu.SemaphoreType.DMA
    down_block, up_block = (LANES // 4, width), (owned, 2 * LANES)
    last_block = (owned // 2, width // 2)
    blocks = ((TILES, down_block), (TILES, up_block), (LASTS, last_block))
    low = [
        (width, rows), (width, distant), (HEADS, AUG, rows), (HEADS, AUG, rows),
        (HEADS, AUG, rows), (HEADS, AUG, distant), (HEADS, AUG, distant),
        (HEADS, distant, LANES),
    ]
    scratch = [vm(shape, LOW) for shape in low]
    scratch += [
        vm((HEADS, 1, rows), FULL),
        vm((HEADS, 1, LANES), FULL),
        vm((HEADS, HEAD_WIDTH, rows), LOW),
        vm((HEADS, 1, rows), FULL),
        vm((HEADS, HEAD_WIDTH, rows), LOW),
        vm((rows, width), FULL),
        vm((rows, width), FULL),
        vm((rows, width), LOW),
        vm((3, width, width), LOW),
        vm((width, width), LOW),
        vm((width // LANES, rows, LANES), FULL),
        vm((rows, width), LOW),
        vm((count, chosen, width), LOW),
        vm((count - 1, chosen, width), LOW),
        vm((rows, LANES), FULL),
        vm((4, 8, width), FULL),
        vm((count, 8, width), FULL),
        vm((4, 8, width), FULL),
    ]
    scratch += [vm((n, 2, count, 2) + block, LOW) for n, block in blocks]
    scratch += [vm((n, count, 2) + block, LOW) for n, block in blocks]
    scratch += [vm((n, 15) + block, LOW) for n, block in blocks]
    scratch += [vm((n, 4) + block, LOW) for n, block in blocks]
    scratch += [
        dma((6,)), dma((2, 2)), dma((2,)), dma((3,)), dma((PIECES, 2)),
        dma((PIECES, 2, 7)), dma((PIECES, 2, 7)),
        dma((count - 1,)), dma((count - 1,)), dma((count - 1,)), dma((count - 1,)),
        dma((count + 2,)), dma((count + 2,)),
    ]
    sums = [jax.ShapeDtypeStruct((n, 4) + block, LOW) for n, block in blocks]
    results = pl.pallas_call(
        functools.partial(main_kernel, count),
        out_shape=(
            jax.ShapeDtypeStruct((rows, width), LOW),
            jax.ShapeDtypeStruct((rows, width), LOW),
            *sums,
            jax.ShapeDtypeStruct((8, width), FULL),
            jax.ShapeDtypeStruct((HEADS, rows, rows), LOW),
            jax.ShapeDtypeStruct((rows, width), FULL),
        ),
        in_specs=[ANY] * 6 + [VMEM] * 4 + [SMEM],
        out_specs=(ANY, ANY, ANY, ANY, ANY, VMEM, ANY, ANY),
        scratch_shapes=scratch,
        compiler_params=pltpu.CompilerParams(
            collective_id=1, has_side_effects=True, vmem_limit_bytes=64 << 20
        ),
        name="main_pass",
    )(tokens, cotangent, *weights, *norms, visible)
    return results[:6]


def finish_kernel(
    mixed, tokens_grad, down_sums, up_sums, last_sums, norms,
    mixed_out, tokens_out, qkv_out, out_out, up_out, down_out, *refs
):
    norm_outs = refs[:4]
    mixed_in, tokens_in, down_in, up_in, last_in, norms_in = refs[4:10]
    qkv, out, up, down, in_sem, out_sem = refs[10:]
    loads = [
        pltpu.make_async_copy(source, target, in_sem.at[n])
        for n, (source, target) in enumerate(
            (
                (down_sums, down_in),
                (up_sums, up_in),
                (last_sums, last_in),
                (norms, norms_in),
                (mixed, mixed_in),
                (tokens_grad, tokens_in),
            )
        )
    ]
    for copy in loads:
        copy.start()
    stores = []

    def store(source, target):
        copy = pltpu.make_async_copy(source, target, out_sem.at[len(stores)])
        copy.start()
        stores.append(copy)

    tiles, blocks, rows, _ = down_sums.shape
    loads[0].wait()
    for tile in range(tiles):
        for block in range(blocks):
            first = (tile * blocks + block) * rows
            down[first : first + rows] = down_in[tile, block].astype(FULL)
    store(down, down_out)
    loads[1].wait()
    for tile in range(tiles):
        for block in range(blocks):
            for half in range(2):
                first = ((block * 2 + half) * tiles + tile) * LANES
                part = up_in[tile, block][:, half * LANES : (half + 1) * LANES]
                up[:, first : first + LANES] = part.astype(FULL)
    store(up, up_out)
    loads[2].wait()
    rows, columns = last_sums.shape[2:]
    for piece in range(last_sums.shape[0]):
        half, pair = divmod(piece, 2)
        for block in range(blocks):
            side, row = divmod(block, 2)
            at = slice(row * rows, (row + 1) * rows)
            first = half * columns
            target = out
            if pair == 0 or side == 0:
                target, first = qkv, first + 2 * columns * (2 * pair + side)
            target[at, first : first + columns] = last_in[piece, block].astype(FULL)
    store(qkv, qkv_out)
    store(out, out_out)
    loads[3].wait()
    for n, norm_out in enumerate(norm_outs):
        norm_out[...] = norms_in[n]
    for n, (source, target) in enumerate(((mixed_in, mixed_out), (tokens_in, tokens_out))):
        loads[4 + n].wait()
        store(source, target)
    for copy in stores:
        copy.wait()


def finish_pass(count, results):
    rows, width = results[0].shape
    owned = width // count

    def full(*shape):
        return jax.ShapeDtypeStruct(shape, FULL)

    grads = [
        full(owned, 3 * width),
        full(owned, width),
        full(owned, TILES * count * LANES),
        full(TILES * LANES, width),
    ]
    return pl.pallas_call(
        finish_kernel,
        out_shape=(
            jax.ShapeDtypeStruct((rows, width), LOW),
            jax.ShapeDtypeStruct((rows, width), LOW),
            *grads,
            *[full(width)] * 4,
        ),
        in_specs=[ANY] * 6,
        out_specs=(ANY,) * 6 + (VMEM,) * 4,
        scratch_shapes=[pltpu.VMEM(ref.shape, ref.dtype) for ref in (*results, *grads)]
        + [pltpu.SemaphoreType.DMA((6,)), pltpu.SemaphoreType.DMA((6,))],
        compiler_params=pltpu.CompilerParams(vmem_limit_bytes=63 << 20),
        name="finish_pass",
    )(*results)


def fused_device(
    tokens,
    qkv_weight,
    out_weight,
    up_weight,
    down_weight,
    norm1_gain,
    norm1_bias,
    norm2_gain,
    norm2_bias,
    visible,
    cotangent,
):
    count = lax.axis_size("seq")
    results = main_pass(
        count,
        tokens[0],
        cotangent[0],
        (qkv_weight, out_weight, up_weight, down_weight),
        (norm1_gain, norm1_bias, norm2_gain, norm2_bias),
        visible,
    )
    mixed, tokens_grad, *grads = finish_pass(count, results)
    return (mixed[None], tokens_grad[None], *grads)


def solution(mesh):
    placed = (
        P("slide", "seq", None),
        P(),
        P(),
        P(),
        P(),
        P(),
        P(),
        P(),
        P(),
        P("slide"),
        P("slide", "seq", None),
    )
    fused = mesh.shape["seq"] == 8 and mesh.shape["slide"] == 4
    return jax.shard_map(
        fused_device if fused else plain_device,
        mesh=mesh,
        in_specs=placed,
        out_specs=(
            P("slide", "seq", None),
            P("slide", "seq", None),
            P("seq", None),
            P("seq", None),
            P("seq", None),
            P("seq", None),
            P(),
            P(),
            P(),
            P(),
        ),
        check_vma=False,
    )
```

```python
import functools

import jax
import jax.numpy as jnp
from jax import lax
from jax.experimental import pallas as pl
from jax.experimental.pallas import tpu as pltpu
from jax.sharding import PartitionSpec as P

HEADS = 16
HEAD_WIDTH = 48
SEG = 512
QB = 512
DILATION_STEP = 16


epsilon = 1e-05


def layer_norm(values, norm_gain, norm_shift):
    average = jnp.mean(values, axis=-1, keepdims=True)
    centered = values - average
    variance = jnp.mean(centered * centered, axis=-1, keepdims=True)
    return centered * lax.rsqrt(variance + epsilon) * norm_gain + norm_shift


def exact_gelu(values):
    return jax.nn.gelu(values, approximate=False)


def block_scores(query_block, seg_keys, seg_valid, distant_keys, distant_valid):
    nearby_scores = jnp.einsum(
        "iyo,uyo->yiu", query_block, seg_keys, preferred_element_type=jnp.float32
    )
    nearby_scores = jnp.where(seg_valid[None, None, :], nearby_scores, -1000000000.0)
    far_scores = jnp.einsum(
        "iyo,uyo->yiu",
        query_block[::DILATION_STEP],
        distant_keys,
        preferred_element_type=jnp.float32,
    )
    far_scores = jnp.where(distant_valid[None, None, :], far_scores, -1000000000.0)
    return (nearby_scores, far_scores)


def block_forward(
    query_block, seg_keys, seg_values, seg_valid, distant_keys, distant_values, distant_valid
):
    nearby_scores, far_scores = block_scores(
        query_block, seg_keys, seg_valid, distant_keys, distant_valid
    )
    head_number = nearby_scores.shape[0]
    row_number = nearby_scores.shape[1]
    chosen_count = row_number // DILATION_STEP
    maximum_table = jnp.max(nearby_scores, axis=-1).reshape(
        head_number, chosen_count, DILATION_STEP
    )
    combined_top = jnp.maximum(maximum_table[:, :, 0], jnp.max(far_scores, axis=-1))
    row_maximum = maximum_table.at[:, :, 0].set(combined_top).reshape(head_number, row_number)
    nearby_exponent = jnp.exp(nearby_scores - row_maximum[:, :, None])
    far_exp = jnp.exp(far_scores - combined_top[:, :, None])
    exponent_sums = jnp.sum(nearby_exponent, axis=-1).reshape(
        head_number, chosen_count, DILATION_STEP
    )
    combined_total = exponent_sums[:, :, 0] + jnp.sum(far_exp, axis=-1)
    row_sum_total = exponent_sums.at[:, :, 0].set(combined_total).reshape(head_number, row_number)
    local_weights = (nearby_exponent / row_sum_total[:, :, None]).astype(jnp.bfloat16)
    far_weights = (far_exp / combined_total[:, :, None]).astype(jnp.bfloat16)
    attended_rows = jnp.einsum(
        "hqk,khd->qhd", local_weights, seg_values, preferred_element_type=jnp.float32
    )
    distant_attended = jnp.einsum(
        "hqk,khd->qhd", far_weights, distant_values, preferred_element_type=jnp.float32
    )
    attended_rows = (
        attended_rows.reshape(chosen_count, DILATION_STEP, head_number, HEAD_WIDTH)
        .at[:, 0]
        .add(distant_attended)
    )
    return (attended_rows.reshape(row_number, head_number, HEAD_WIDTH), row_maximum, row_sum_total)


def block_backward(
    query_block,
    seg_keys,
    seg_values,
    seg_valid,
    distant_keys,
    distant_values,
    distant_valid,
    gradient_block,
    row_maximum,
    row_sum_total,
):
    nearby_scores, far_scores = block_scores(
        query_block, seg_keys, seg_valid, distant_keys, distant_valid
    )
    head_number = row_maximum.shape[0]
    row_number = row_maximum.shape[1]
    chosen_count = row_number // DILATION_STEP
    combined_top = row_maximum.reshape(head_number, chosen_count, DILATION_STEP)[:, :, 0]
    combined_total = row_sum_total.reshape(head_number, chosen_count, DILATION_STEP)[:, :, 0]
    nearby_probability = (
        jnp.exp(nearby_scores - row_maximum[:, :, None]) / row_sum_total[:, :, None]
    )
    far_prob = jnp.exp(far_scores - combined_top[:, :, None]) / combined_total[:, :, None]
    local_weights = nearby_probability.astype(jnp.bfloat16)
    gradient_sampled = gradient_block[::DILATION_STEP]
    value_grad = jnp.einsum(
        "mns,nmg->smg", local_weights, gradient_block, preferred_element_type=jnp.float32
    )
    nearby_dots = jnp.einsum(
        "iyo,uyo->yiu", gradient_block, seg_values, preferred_element_type=jnp.float32
    )
    far_dots = jnp.einsum(
        "iyo,uyo->yiu", gradient_sampled, distant_values, preferred_element_type=jnp.float32
    )
    delta_table = jnp.sum(nearby_probability * nearby_dots, axis=-1).reshape(
        head_number, chosen_count, DILATION_STEP
    )
    joint_delta = delta_table[:, :, 0] + jnp.sum(far_prob * far_dots, axis=-1)
    row_delta = delta_table.at[:, :, 0].set(joint_delta).reshape(head_number, row_number)
    local_slope = (nearby_probability * (nearby_dots - row_delta[:, :, None])).astype(jnp.bfloat16)
    distant_slope = (far_prob * (far_dots - joint_delta[:, :, None])).astype(jnp.bfloat16)
    query_gradient = jnp.einsum(
        "hqk,khd->qhd", local_slope, seg_keys, preferred_element_type=jnp.float32
    )
    distant_query = jnp.einsum(
        "hqk,khd->qhd", distant_slope, distant_keys, preferred_element_type=jnp.float32
    )
    query_gradient = (
        query_gradient.reshape(chosen_count, DILATION_STEP, head_number, HEAD_WIDTH)
        .at[:, 0]
        .add(distant_query)
    )
    key_grad = jnp.einsum(
        "mns,nmg->smg", local_slope, query_block, preferred_element_type=jnp.float32
    )
    far_weights = far_prob.astype(jnp.bfloat16)
    far_value_grad = jnp.einsum(
        "mns,nmg->smg", far_weights, gradient_sampled, preferred_element_type=jnp.float32
    )
    far_key_grad = jnp.einsum(
        "mns,nmg->smg",
        distant_slope,
        query_block[::DILATION_STEP],
        preferred_element_type=jnp.float32,
    )
    return (
        query_gradient.reshape(row_number, head_number, HEAD_WIDTH),
        key_grad,
        value_grad,
        far_key_grad,
        far_value_grad,
    )


def plain_device(
    tokens,
    qkv_weight,
    out_weight,
    up_weight,
    down_weight,
    norm1_gain,
    norm1_bias,
    norm2_gain,
    norm2_bias,
    visible,
    cotangent,
):
    row_number = tokens.shape[1]
    embedding_width = tokens.shape[2]
    query_scale = HEAD_WIDTH ** (-0.5)
    first_row = lax.axis_index("seq") * row_number
    positions = first_row + jnp.arange(row_number, dtype=jnp.int32)
    row_validity = positions < visible[0]
    inputs = tokens[0].astype(jnp.float32)
    norm_one, pull_one = jax.vjp(layer_norm, inputs, norm1_gain, norm1_bias)
    normed = norm_one.astype(jnp.bfloat16)
    projected = jnp.dot(normed, qkv_weight, preferred_element_type=jnp.float32)
    query_rows = (
        (projected[:, :embedding_width] * query_scale)
        .astype(jnp.bfloat16)
        .reshape(row_number, HEADS, HEAD_WIDTH)
    )
    flat_keys = projected[:, embedding_width : 2 * embedding_width].astype(jnp.bfloat16)
    flat_values = projected[:, 2 * embedding_width :].astype(jnp.bfloat16)
    key_matrix = flat_keys.reshape(row_number, HEADS, HEAD_WIDTH)
    value_matrix = flat_values.reshape(row_number, HEADS, HEAD_WIDTH)
    gathered_keys, gathered_values = (
        lax.all_gather(flat_keys[::DILATION_STEP], "seq", axis=0, tiled=True),
        lax.all_gather(flat_values[::DILATION_STEP], "seq", axis=0, tiled=True),
    )
    distant_count = gathered_keys.shape[0]
    distant_valid = jnp.arange(distant_count, dtype=jnp.int32) * DILATION_STEP < visible[0]
    distant_keys = gathered_keys.reshape(distant_count, HEADS, HEAD_WIDTH)
    distant_values = gathered_values.reshape(distant_count, HEADS, HEAD_WIDTH)
    per_segment = SEG // QB
    attended_rows, row_maximum, row_sum_total = block_forward(
        query_rows,
        key_matrix,
        value_matrix,
        row_validity,
        distant_keys,
        distant_values,
        distant_valid,
    )
    attn_low = attended_rows.reshape(row_number, embedding_width).astype(jnp.bfloat16)
    after_attn = inputs + jnp.dot(attn_low, out_weight, preferred_element_type=jnp.float32)
    norm_two, pull_two = jax.vjp(layer_norm, after_attn, norm2_gain, norm2_bias)
    normed_two = norm_two.astype(jnp.bfloat16)
    up_cols = jnp.dot(normed_two, up_weight, preferred_element_type=jnp.float32)
    activated, pull_gelu = jax.vjp(exact_gelu, up_cols)
    hidden = activated.astype(jnp.bfloat16)
    result = after_attn + jnp.dot(hidden, down_weight, preferred_element_type=jnp.float32)
    mixed_out = jnp.where(row_validity[:, None], result, 0.0).astype(jnp.bfloat16)[None]
    grad_out = jnp.where(row_validity[:, None], cotangent[0], jnp.zeros_like(cotangent[0]))
    down_grad = jnp.einsum("tf,td->fd", hidden, grad_out, preferred_element_type=jnp.float32)
    hidden_grad = jnp.einsum("td,fd->tf", grad_out, down_weight, preferred_element_type=jnp.float32)
    (up_slope,) = pull_gelu(hidden_grad)
    up_low = up_slope.astype(jnp.bfloat16)
    up_grad = jnp.einsum("td,tf->df", normed_two, up_low, preferred_element_type=jnp.float32)
    norm_two_in = jnp.einsum("tf,df->td", up_low, up_weight, preferred_element_type=jnp.float32)
    after_part, gain_two_grad, shift_two_grad = pull_two(norm_two_in)
    resid_grad = grad_out.astype(jnp.float32) + after_part
    resid_low = resid_grad.astype(jnp.bfloat16)
    out_grad = jnp.einsum("td,te->de", attn_low, resid_low, preferred_element_type=jnp.float32)
    attn_grad = jnp.einsum("te,de->td", resid_low, out_weight, preferred_element_type=jnp.float32)
    attn_grad = attn_grad.astype(jnp.bfloat16).reshape(row_number, HEADS, HEAD_WIDTH)
    query_gradient, key_grad, value_grad, far_key_grad, far_value_grad = block_backward(
        query_rows,
        key_matrix,
        value_matrix,
        row_validity,
        distant_keys,
        distant_values,
        distant_valid,
        attn_grad,
        row_maximum,
        row_sum_total,
    )
    key_list = [key_grad]
    value_list = [value_grad]
    owned_keys, owned_values = (
        lax.psum_scatter(
            far_key_grad.reshape(distant_count, embedding_width),
            "seq",
            scatter_dimension=0,
            tiled=True,
        ),
        lax.psum_scatter(
            far_value_grad.reshape(distant_count, embedding_width),
            "seq",
            scatter_dimension=0,
            tiled=True,
        ),
    )
    chosen_count = row_number // DILATION_STEP
    segment_count = row_number // SEG
    nearby_keys = jnp.sum(
        jnp.stack(key_list).reshape(segment_count, per_segment, SEG, embedding_width), axis=1
    )
    nearby_values = jnp.sum(
        jnp.stack(value_list).reshape(segment_count, per_segment, SEG, embedding_width), axis=1
    )
    key_total = (
        nearby_keys.reshape(chosen_count, DILATION_STEP, embedding_width)
        .at[:, 0]
        .add(owned_keys)
        .reshape(row_number, embedding_width)
    )
    value_total = (
        nearby_values.reshape(chosen_count, DILATION_STEP, embedding_width)
        .at[:, 0]
        .add(owned_values)
        .reshape(row_number, embedding_width)
    )
    query_total = query_gradient.reshape(row_number, embedding_width)
    mixed_grad = jnp.concatenate(
        [
            (query_total * query_scale).astype(jnp.bfloat16),
            key_total.astype(jnp.bfloat16),
            value_total.astype(jnp.bfloat16),
        ],
        axis=1,
    )
    qkv_grad = jnp.einsum("td,tf->df", normed, mixed_grad, preferred_element_type=jnp.float32)
    norm_one_in = jnp.einsum(
        "tf,df->td", mixed_grad, qkv_weight, preferred_element_type=jnp.float32
    )
    input_part, gain_one_grad, shift_one_grad = pull_one(norm_one_in)
    tokens_grad = (resid_grad + input_part).astype(jnp.bfloat16)[None]
    weight_grads = (qkv_grad, out_grad, up_grad, down_grad)
    row_parts = (
        lax.psum_scatter(weight_grads[0], "seq", scatter_dimension=0, tiled=True),
        lax.psum_scatter(weight_grads[1], "seq", scatter_dimension=0, tiled=True),
        lax.psum_scatter(weight_grads[2], "seq", scatter_dimension=0, tiled=True),
        lax.psum_scatter(weight_grads[3], "seq", scatter_dimension=0, tiled=True),
    )
    final_grads = (
        lax.psum(row_parts[0].astype(jnp.bfloat16), "slide").astype(jnp.float32),
        lax.psum(row_parts[1].astype(jnp.bfloat16), "slide").astype(jnp.float32),
        lax.psum(row_parts[2].astype(jnp.bfloat16), "slide").astype(jnp.float32),
        lax.psum(row_parts[3].astype(jnp.bfloat16), "slide").astype(jnp.float32),
    )
    norm_grads = lax.psum(
        (gain_one_grad, shift_one_grad, gain_two_grad, shift_two_grad), ("seq", "slide")
    )
    return (
        mixed_out,
        tokens_grad,
        final_grads[0],
        final_grads[1],
        final_grads[2],
        final_grads[3],
        norm_grads[0],
        norm_grads[1],
        norm_grads[2],
        norm_grads[3],
    )


MESH = pl.DeviceIdType.MESH
LOW = jnp.bfloat16
FULL = jnp.float32
AUG = 64
LANES = 128
NEVER = -2000000000.0
ANY = pl.BlockSpec(memory_space=pl.ANY)
VMEM = pl.BlockSpec(memory_space=pltpu.VMEM)
SMEM = pl.BlockSpec(memory_space=pltpu.SMEM)


def nn(left, right):
    return jnp.dot(left, right, preferred_element_type=FULL)


def nt(left, right):
    return lax.dot_general(left, right, (((1,), (1,)), ((), ())), preferred_element_type=FULL)


def tn(left, right):
    return lax.dot_general(left, right, (((0,), (0,)), ((), ())), preferred_element_type=FULL)


def remote(src, dst, send_sem, recv_sem, device):
    return pltpu.make_async_remote_copy(
        src_ref=src,
        dst_ref=dst,
        send_sem=send_sem,
        recv_sem=recv_sem,
        device_id=device,
        device_id_type=MESH,
    )


def greet(devices):
    barrier = pltpu.get_barrier_semaphore()
    for device in devices:
        pl.semaphore_signal(barrier, inc=1, device_id=device, device_id_type=MESH)
    pl.semaphore_wait(barrier, len(devices))


def row_peers(count):
    seq, slide = lax.axis_index("seq"), lax.axis_index("slide")
    return [(lax.rem(seq + step, count), slide) for step in range(1, count)]


def spread(ref, values):
    for group in range(ref.shape[0]):
        ref[group] = values[:, group * LANES : (group + 1) * LANES]


def strided_rows(ref, step, count):
    groups = [
        ref[group, pl.ds(step, count, stride=DILATION_STEP), :] for group in range(ref.shape[0])
    ]
    return jnp.concatenate(groups, axis=1)


def strided_store(ref, step, count, values):
    for group in range(ref.shape[0]):
        ref[group, pl.ds(step, count, stride=DILATION_STEP), :] = values[
            :, group * LANES : (group + 1) * LANES
        ]


def chunk(step, size):
    return pl.ds(pl.multiple_of(step * size, size), size)


def steps(body):
    @pl.loop(0, DILATION_STEP // 4)
    def _(group):
        for member in range(4):
            body(group * 4 + member)


def row_mean(values):
    return jnp.mean(values, axis=-1, keepdims=True)


def fold_rows(values):
    return jnp.sum(values.reshape(-1, 8, values.shape[-1]), axis=0)


def mask_rows(ref, bias):
    first = lax.broadcasted_iota(jnp.int32, (AUG - HEAD_WIDTH, ref.shape[2]), 0) == 0
    ref[:, HEAD_WIDTH:, :] = jnp.broadcast_to(
        jnp.where(first, bias, 0.0).astype(LOW), (HEADS, AUG - HEAD_WIDTH, ref.shape[2])
    )


class Place:
    def __init__(self):
        seq, slide = lax.axis_index("seq"), lax.axis_index("slide")
        self.seq, self.slide = seq, slide
        self.z, self.x = seq // 2, seq % 2
        self.b, self.a = self.z // 2, self.z % 2
        self.y, self.c = slide // 2, slide % 2
        self.sibling = (seq, slide + 1 - 2 * self.c)
        self.across_y = (seq, slide + 2 - 4 * self.y)
        self.diagonal = (seq, 3 - slide)
        self.across_x = (seq + 1 - 2 * self.x, slide)
        self.slide_peers = (self.sibling, self.across_y, self.diagonal)

    def layer(self, step):
        return (self.z + step) % 4


class Part:
    def __init__(self, place, orders, folds, both, core_got, got, final, send_sem, recv_sem):
        self.place, self.orders, self.both = place, orders, both
        self.core_got, self.got, self.final = core_got, got, final
        self.send_sem, self.recv_sem = send_sem, recv_sem
        self.folds = folds

    def blocks(self, core, phase, value):
        choices = {}
        for at, name in enumerate(self.orders[core], 1):
            if at < phase:
                choices[name] = [getattr(self.place, name)]
            elif at == phase:
                choices[name] = [value]
            else:
                choices[name] = list(range(4 if name == "z" else 2))
        if "z" not in choices:
            choices["z"] = [2 * b + a for b in choices["b"] for a in choices["a"]]
        return [(2 * z + x, y) for z in choices["z"] for x in choices["x"] for y in choices["y"]]

    def partners(self, core, phase):
        place, name = self.place, self.orders[core][phase - 1]
        if name == "x":
            return [(1 - place.x, place.across_x)]
        if name == "y":
            return [(1 - place.y, place.across_y)]
        if name == "a":
            return [(1 - place.a, (place.seq + 2 - 4 * place.a, place.slide))]
        if name == "b":
            return [(1 - place.b, (place.seq + 4 - 8 * place.b, place.slide))]
        layers = [place.layer(k) for k in (1, 2, 3)]
        return [(z, (2 * z + place.x, place.slide)) for z in layers]

    def span(self, core, phase):
        first, left = 0, 16
        for at, name in enumerate(self.orders[core], 1):
            left //= 4 if name == "z" else 2
            number = left * (3 if name == "z" else 1)
            if at == phase:
                return first, number
            first += number

    def transfers(self, core, phase):
        kept, got = self.both.at[0], self.got
        slot = self.span(core, phase)[0]
        pairs = "y" in self.orders[core][phase:]
        moves = []
        for value, device in self.partners(core, phase):
            for owner, y in self.blocks(core, phase, value):
                if not pairs:
                    moves.append((kept.at[owner, y], got.at[slot], device))
                elif y == 0:
                    moves.append((kept.at[owner], got.at[pl.ds(slot, 2)], device))
                slot += 1
        return moves

    def start(self, phase, merged):
        place, send, recv = self.place, self.send_sem.at[phase], self.recv_sem.at[phase]
        if phase == 0:
            remote(self.both.at[1], self.core_got, send, recv, place.sibling).start()
        elif phase <= self.folds:
            for core in range(2):
                if phase > len(self.orders[core]):
                    continue

                @pl.when(place.c == core)
                def _(core=core):
                    for source, target, device in self.transfers(core, phase):
                        remote(source, target, send, recv, device).start()
        elif phase == self.folds + 1:
            own = self.final.at[place.c * 2 + place.y]
            for device in place.slide_peers if merged else (place.across_y,):
                remote(own, own, send, recv, device).start()
        else:
            own = self.final.at[pl.ds(place.c * 2, 2)]
            remote(own, own, send, recv, place.sibling).start()

    def wait(self, phase, whole):
        both_ways = remote(
            whole, whole, self.send_sem.at[phase], self.recv_sem.at[phase], self.place.sibling
        )
        both_ways.wait_recv()
        both_ways.wait_send()

    def finish(self, phase, merged):
        place = self.place
        if phase == 0:
            self.wait(phase, self.core_got)

            @pl.loop(0, 8)
            def _(owner):
                for row in range(2):
                    self.both[0, owner, row] += self.core_got[owner, row]
        elif phase <= self.folds:
            for core in range(2):
                if phase > len(self.orders[core]):
                    continue

                @pl.when(place.c == core)
                def _(core=core):
                    first, number = self.span(core, phase)
                    self.wait(phase, self.got.at[pl.ds(first, number)])
                    name = self.orders[core][phase - 1]
                    blocks = self.blocks(core, phase, getattr(place, name))
                    for n, (owner, y) in enumerate(blocks):
                        slots = range(first + n, first + number, len(blocks))
                        self.add(owner, y, slots, core if phase == len(self.orders[core]) else None)
        elif phase == self.folds + 1:
            self.wait(phase, self.final.at[pl.ds(0, 3 if merged else 1)])
        else:
            self.wait(phase, self.final.at[pl.ds(0, 2)])

    def add(self, owner, y, slots, core):
        if len(slots) == 1:
            total = self.both[0, owner, y] + self.got[slots[0]]
        else:
            total = self.both[0, owner, y].astype(FULL)
            for slot in slots:
                total = total + self.got[slot].astype(FULL)
            total = total.astype(LOW)
        if core is None:
            self.both[0, owner, y] = total
        else:
            self.final[core * 2 + self.place.y] = total


class Piece:
    def __init__(self, parts, merged, outs, out_sem):
        self.parts, self.merged, self.outs, self.out_sem = parts, merged, outs, out_sem
        self.last = parts[0].folds + (1 if merged else 2)
        self.phase = -1

    @property
    def done(self):
        return self.phase > self.last

    def advance(self):
        if self.done:
            return
        if self.phase >= 0:
            for part in self.parts:
                part.finish(self.phase, self.merged)
        self.phase += 1
        if not self.done:
            for part in self.parts:
                part.start(self.phase, self.merged)
            return
        for n in range(len(self.parts)):
            self.out_copy(n).start()

    def out_copy(self, n):
        return pltpu.make_async_copy(self.parts[n].final, self.outs[n], self.out_sem.at[n])


EARLY = 5
LN_TWO = 0.6931471805599453
QUERY_SCALE = HEAD_WIDTH ** (-0.5) / LN_TWO
TILES = 3
LASTS = 4
PIECES = TILES + LASTS
ORDERS = (
    (('yxab', 'zxy', 'xyz', 'zyx'), False),
    (('yxab', 'ayxb', 'xyz', 'yxz'), False),
    (('xyz', 'yaxb', 'yzx', 'abyx'), False),
    (('yabx', 'xaby'), False),
    (('yzx', 'xyz'), False),
    (('yxab', 'xayb'), True),
    (('yxz', 'xyz'), True),
)
HOOKS = {
    "tile1.1": (0,),
    "tile2.1": (1,),
    "after2": (2,),
    "far": (0, 1),
    "near3": (2,),
    "near4": (0, 3, 4),
    "near5": (1,),
    "last2": (3, 2),
    "last3": (5,),
    "into": (0, 6, 4),
    "norm": (1,),
}
TAIL = (5, 3, 2, 0, 6, 5, 0, 4, 1, 6, 0, 5, 3, 2, 4, 1, 3, 1, 6, 2, 5, 3, 2, 4, 3, 6, 4, 5)

def main_kernel(
    count, tokens, cotangent, qkv_weight, out_weight, up_weight, down_weight,
    gain_one, shift_one, gain_two, shift_two, visible,
    mixed_out, tokens_out, down_sums, up_sums, last_sums, norm_out, weights_kept, norm_kept,
    normed, far_normed, query, key, value, far_key, far_value, far_weights, scale, far_scale, attn,
    delta, slope, resid, after, dyb, wqkv, wo, wide, staged, all_far, far_got, spread_one,
    sums, around, across,
    down_both, up_both, last_both, down_core, up_core, last_core,
    down_got, up_got, last_got, down_final, up_final, last_final,
    load_sem, tile_sem, group_sem, store_sem, out_sem, send_sem, recv_sem,
    gather_send_sem, gather_recv_sem, far_send_sem, far_recv_sem, norm_send_sem, norm_recv_sem,
):
    place = Place()
    seq, core = place.seq, place.c
    rows, width = resid.shape
    chosen = rows // DILATION_STEP
    group_lanes = LANES
    tile_width = count * group_lanes
    first_row = seq * rows
    limit = visible[0]
    peers = row_peers(count)
    others = list(place.slide_peers) + peers
    barrier = pltpu.get_barrier_semaphore()
    for other in others:
        pl.semaphore_signal(barrier, inc=1, device_id=other, device_id_type=MESH)

    def valid_rows(step):
        places = lax.broadcasted_iota(jnp.int32, (chosen, 1), 0) * DILATION_STEP + step
        return first_row + places < limit

    def landed(n):
        sources = (
            (tokens, staged),
            (qkv_weight.at[:, pl.ds(width, width)], wqkv.at[1]),
            (qkv_weight.at[:, pl.ds(2 * width, width)], wqkv.at[2]),
            (qkv_weight.at[:, pl.ds(0, width)], wqkv.at[0]),
            (out_weight, wo),
            (cotangent, staged),
        )
        return pltpu.make_async_copy(*sources[n], load_sem.at[n])

    for n in range(5):
        landed(n).start()
    distant = count * chosen
    members = 4

    def kept_group(group, slots):
        kept = weights_kept.at[pl.ds(group * members, members)]
        return slots.at[group % 2], kept, group_sem.at[group % 2]

    pieces = []
    for n in range(TILES):
        parts = [
            Part(
                place,
                ORDERS[n][0][2 * which : 2 * which + 2],
                max(len(order) for order in ORDERS[n][0]),
                both.at[n],
                core_got.at[n],
                got.at[n],
                final.at[n],
                send_sem.at[n, which],
                recv_sem.at[n, which],
            )
            for which, (both, core_got, got, final) in enumerate(
                (
                    (down_both, down_core, down_got, down_final),
                    (up_both, up_core, up_got, up_final),
                )
            )
        ]
        pieces.append(Piece(parts, ORDERS[n][1], (down_sums.at[n], up_sums.at[n]), out_sem.at[n]))
    for n in range(LASTS):
        part = Part(
            place,
            ORDERS[TILES + n][0],
            max(len(order) for order in ORDERS[TILES + n][0]),
            last_both.at[n],
            last_core.at[n],
            last_got.at[n],
            last_final.at[n],
            send_sem.at[TILES + n, 0],
            recv_sem.at[TILES + n, 0],
        )
        pieces.append(Piece([part], ORDERS[TILES + n][1], (last_sums.at[n],), out_sem.at[TILES + n]))

    def hook(name):
        for n in HOOKS.get(name, ()):
            if pieces[n].phase >= 0:
                pieces[n].advance()

    def split_last(n, side, grads):
        target = last_both.at[n, (side + core) % 2]
        target[...] = grads.astype(LOW).reshape(count, 2, -1, grads.shape[1])

    def attend_part(h1, top, total, attended, weights):
        landed(0).wait()
        spread(wide, staged[...].astype(FULL))
        landed(5).start()

        def normalize(step):
            at = chunk(step, chosen)
            values = strided_rows(wide, step, chosen)
            centered = values - row_mean(values)
            inverse = lax.rsqrt(row_mean(centered * centered) + epsilon)
            normal = centered * inverse
            after[at] = values
            resid[at] = normal
            spread_one[at] = jnp.broadcast_to(inverse, (chosen, LANES))
            low = (normal * gain_one[...][None] + shift_one[...][None]).astype(LOW)
            h1[at] = low
            return low

        all_far[seq] = normalize(0)

        @pl.loop(0, 5)
        def _(group):
            for member in range(3):
                normalize(group * 3 + member + 1)

        pltpu.make_async_copy(resid, norm_kept, store_sem.at[0]).start()
        for part, ref in ((1, key), (2, value)):
            landed(part).wait()
            projected = nn(h1[...], wqkv[part]).astype(LOW)
            ref[:, :HEAD_WIDTH, :] = projected.T.reshape(HEADS, HEAD_WIDTH, rows)
            if part == 1:
                pl.semaphore_wait(barrier, len(others))
                for n, peer in enumerate(peers):
                    mine = all_far.at[seq]
                    send, recv = gather_send_sem.at[n], gather_recv_sem.at[n]
                    remote(mine, mine, send, recv, peer).start()
        landed(3).wait()
        projected = (nn(h1[...], wqkv[0]) * QUERY_SCALE).astype(LOW)
        query[:, :HEAD_WIDTH, :] = projected.T.reshape(HEADS, HEAD_WIDTH, rows)
        places = lax.broadcasted_iota(jnp.int32, (1, rows), 1)
        places = first_row + (places % chosen) * DILATION_STEP + places // chosen
        mask_rows(key, jnp.where(places < limit, 0.0, NEVER))
        mask_rows(query, jnp.ones((1, rows), FULL))
        mask_rows(value, jnp.ones((1, rows), FULL))

        @pl.loop(0, HEADS // members)
        def _(group):
            slot, kept, sem = kept_group(group, weights)

            @pl.when(group >= 2)
            def _():
                pltpu.make_async_copy(slot, kept, sem).wait()

            for member in range(members):
                head = group * members + member
                scores = tn(key[head], query[head])
                highest = jnp.max(scores, axis=0, keepdims=True)
                low = jnp.exp2(scores - highest).astype(LOW)
                top[head] = highest
                weights[group % 2, member] = low
                result = nn(value[head], low)
                attended[head] = result[:HEAD_WIDTH]
                total[head] = result[HEAD_WIDTH : HEAD_WIDTH + 1]
            pltpu.make_async_copy(slot, kept, sem).start()

        normed[...] = h1[...].T
        landed(5).wait()
        spread(wide, staged[...].astype(FULL))

        @steps
        def _(step):
            at = chunk(step, chosen)
            dyb[at] = jnp.where(valid_rows(step), strided_rows(wide, step, chosen), 0.0).astype(LOW)

        for n in range(count - 1):
            source = lax.rem(seq + count - 1 - n, count)
            mine, theirs = all_far.at[seq], all_far.at[source]
            wait = remote(mine, theirs, gather_send_sem.at[n], gather_recv_sem.at[n], peers[0])
            wait.wait_recv()
            wait.wait_send()
        flat = all_far[...].reshape(distant, width)
        for part, ref in ((1, far_key), (2, far_value)):
            projected = nn(flat, wqkv[part]).astype(LOW)
            ref[:, :HEAD_WIDTH, :] = projected.T.reshape(HEADS, HEAD_WIDTH, distant)
        places = lax.broadcasted_iota(jnp.int32, (1, distant), 1) * DILATION_STEP
        mask_rows(far_key, jnp.where(places < limit, 0.0, NEVER))
        mask_rows(far_value, jnp.ones((1, distant), FULL))
        lane_mask = jnp.where(lax.broadcasted_iota(jnp.int32, (1, LANES), 1) < chosen, 0.0, NEVER)

        @pl.loop(0, HEADS // 4)
        def _(group):
            for member in range(4):
                head = group * 4 + member
                scores = tn(far_key[head], query[head][:, :LANES]) + lane_mask
                highest = jnp.max(scores, axis=0, keepdims=True)
                low = jnp.exp2(scores - highest).astype(LOW)
                far_weights[head] = low
                near = top[head][:, :LANES]
                joint = jnp.maximum(near, highest)
                near_part, far_part = jnp.exp2(near - joint), jnp.exp2(highest - joint)
                far_result = nn(far_value[head], low)
                far_total = far_result[HEAD_WIDTH : HEAD_WIDTH + 1]
                joint_total = total[head][:, :LANES] * near_part + far_total * far_part
                near_part, far_part = near_part / joint_total, far_part / joint_total
                far_scale[head] = far_part
                local = jnp.concatenate([near_part, 1.0 / total[head][:, LANES:]], axis=1)
                scale[head] = local
                result = attended[head] * local
                with_far = result[:, :LANES] + far_result[:HEAD_WIDTH] * far_part
                result = jnp.concatenate([with_far, result[:, LANES:]], axis=1)
                attn[head] = result.astype(LOW)

        for group in (2, 3):
            slot, kept, sem = kept_group(group, weights)
            pltpu.make_async_copy(slot, kept, sem).wait()
        pltpu.make_async_copy(resid, norm_kept, store_sem.at[0]).wait()

    vm = pltpu.VMEM
    pl.run_scoped(
        attend_part,
        vm((rows, width), LOW),
        vm((HEADS, 1, rows), FULL),
        vm((HEADS, 1, rows), FULL),
        vm((HEADS, HEAD_WIDTH, rows), FULL),
        vm((2, members, rows, rows), LOW),
    )

    def forward_part(norm_two, spread_two, h2, h2_t, active, low_slope, wup, wdown):
        halves = 2
        per_half = tile_width // halves

        def load_tile(tile, half):
            for local in range(count // halves):
                owner = half * (count // halves) + local
                first = owner * TILES * group_lanes + tile * group_lanes
                at = pl.ds(pl.multiple_of(first, LANES), group_lanes)
                to = pl.ds(local * group_lanes, group_lanes)
                pltpu.make_async_copy(
                    up_weight.at[:, at], wup.at[half, :, to], tile_sem.at[half, 0]
                ).start()
                pltpu.make_async_copy(
                    down_weight.at[at], wdown.at[half, to], tile_sem.at[half, 1]
                ).start()

        def wait_tile(half):
            pltpu.make_async_copy(wup.at[half], wup.at[half], tile_sem.at[half, 0]).wait()
            pltpu.make_async_copy(wdown.at[half], wdown.at[half], tile_sem.at[half, 1]).wait()

        load_tile(0, 0)
        load_tile(0, 1)
        landed(4).wait()
        after[...] += nn(attn[...].reshape(width, rows).T, wo[...])

        @steps
        def _(step):
            at = chunk(step, chosen)
            values = after[at]
            centered = values - row_mean(values)
            inverse = lax.rsqrt(row_mean(centered * centered) + epsilon)
            normal = centered * inverse
            norm_two[at] = normal
            spread_two[at] = jnp.broadcast_to(inverse, (chosen, LANES))
            h2[at] = (normal * gain_two[...][None] + shift_two[...][None]).astype(LOW)
            resid[at] = jnp.zeros((chosen, width), FULL)

        h2_t[...] = h2[...].T
        for tile in range(TILES):
            @pl.loop(0, halves)
            def _(half, tile=tile):
                wait_tile(half)
                to = pl.ds(pl.multiple_of(half * per_half, LANES), per_half)
                hidden = nn(h2[...], wup[half])
                hidden_slope = nt(dyb[...], wdown[half])
                share = 0.5 * (1.0 + lax.erf(hidden * 0.7071067811865476))
                active[:, to] = (hidden * share).astype(LOW)
                density = hidden * jnp.exp(-0.5 * hidden * hidden) * 0.3989422804014327
                low_slope[:, to] = (hidden_slope * (share + density)).astype(LOW)
                after[...] += nn(active[:, to], wdown[half])
                resid[...] += nt(low_slope[:, to], wup[half])
                if tile + 1 < TILES:
                    load_tile(tile + 1, half)

            hook("tile%d.1" % tile)

            @pl.loop(0, 4)
            def _(part, tile=tile):
                at = pl.ds(pl.multiple_of(part * tile_width // 4, LANES), tile_width // 4)
                grads = nn(h2_t[...], low_slope[:, at]).astype(LOW)
                target = up_both.at[tile, (part // 2 + core) % 2]
                target[:, part % 2] = grads.reshape(count, -1, grads.shape[1])
                grads = tn(active[:, at], dyb[...]).astype(LOW)
                owners = count // 4
                grads = grads.reshape(owners, 2, 2, -1, width)
                for side in range(2):
                    target = down_both.at[tile, (side + core) % 2]
                    target[pl.ds(part * owners, owners)] = grads[:, side]

            pieces[tile].advance()
            hook("tile%d.3" % tile)
        sums[...] = jnp.zeros_like(sums)
        hook("after0")

        @steps
        def _(step):
            at = chunk(step, chosen)
            strided_store(wide, step, chosen, jnp.where(valid_rows(step), after[at], 0.0))
            given, normal = resid[at], norm_two[at]
            sums[2] += fold_rows(given * normal)
            sums[3] += fold_rows(given)
            scaled = given * gain_two[...][None]
            part = scaled - row_mean(scaled) - normal * row_mean(scaled * normal)
            value_here = dyb[at].astype(FULL) + spread_two[at][:, :1] * part
            resid[at] = value_here
            h2[at] = value_here.astype(LOW)

        for group in range(width // LANES):
            staged[:, group * LANES : (group + 1) * LANES] = wide[group].astype(LOW)
        pltpu.make_async_copy(staged, mixed_out, store_sem.at[1]).start()
        half = width // 2
        hook("after1")
        for n in range(2):
            at = slice(n * half, (n + 1) * half)
            split_last(2 * n + 1, 1, nn(attn[...].reshape(width, rows), h2[:, at]))
        slope[...] = nt(wo[...], h2[...]).astype(LOW).reshape(HEADS, HEAD_WIDTH, rows)

        @pl.loop(0, HEADS)
        def _(head):
            product = slope[head].astype(FULL) * attn[head].astype(FULL)
            delta[head] = jnp.sum(product, axis=0, keepdims=True)

        hook("after2")

    pl.run_scoped(
        forward_part,
        vm((rows, width), FULL),
        vm((rows, LANES), FULL),
        vm((rows, width), LOW),
        vm((width, rows), LOW),
        vm((rows, tile_width), LOW),
        vm((rows, tile_width), LOW),
        vm((2, width, tile_width // 2), LOW),
        vm((2, tile_width // 2, width), LOW),
    )

    def backward_part(weights, slopes, far_query, far_send, given):
        norm_one = after

        def load_group(group):
            slot, kept, sem = kept_group(group, weights)
            return pltpu.make_async_copy(kept, slot, sem)

        load_group(0).start()
        load_group(1).start()
        norm_load = pltpu.make_async_copy(norm_kept, norm_one, store_sem.at[0])
        norm_load.start()

        @pl.loop(0, HEADS // 4)
        def _(group):
            for member in range(4):
                head = group * 4 + member
                first_slope = slope[head][:, :LANES]
                low = far_weights[head]
                change = tn(far_value[head, :HEAD_WIDTH], first_slope) - delta[head][:, :LANES]
                score_slope = (low.astype(FULL) * far_scale[head] * change).astype(LOW)
                far_query[head] = nn(far_key[head, :HEAD_WIDTH], score_slope)
                scaled = (first_slope.astype(FULL) * far_scale[head]).astype(LOW)
                key_slope = nt(query[head, :HEAD_WIDTH, :LANES], score_slope)
                given[0, head] = (key_slope * LN_TWO).astype(LOW)
                given[1, head] = nt(scaled, low).astype(LOW)

        hook("far0")
        far_normed[...] = all_far[...].reshape(distant, width).T
        into = nn(wqkv[1], given[0].reshape(width, distant))
        into += nn(wqkv[2], given[1].reshape(width, distant))
        far_send[...] = into.T.astype(LOW).reshape(count, chosen, width)
        for n, peer in enumerate(peers):
            remote(
                far_send.at[peer[0]], far_got.at[n], far_send_sem.at[n], far_recv_sem.at[n], peer
            ).start()
        hook("far")

        def weight_slopes(half):
            at = slice(half * HEADS // 2, (half + 1) * HEADS // 2)
            for part, (n, side) in enumerate(((0, 0), (0, 1), (1, 0))):
                grads = nt(normed[...], slopes[part, at].reshape(width // 2, rows))
                if part:
                    far = given[part - 1, at].reshape(width // 2, distant)
                    grads += nt(far_normed[...], far)
                split_last(2 * half + n, side, grads)
                if part:
                    pieces[TILES + 2 * half + n].advance()
                    hook("last%d" % (2 * half + n))

        for group in range(HEADS // members):
            load_group(group).wait()
            for member in range(members):
                head = group * members + member
                low = weights[group % 2, member]
                change = tn(value[head, :HEAD_WIDTH], slope[head]) - delta[head]
                score_slope = (low.astype(FULL) * scale[head] * change).astype(LOW)
                query_slope = nn(key[head, :HEAD_WIDTH], score_slope)
                key_slope = nt(query[head, :HEAD_WIDTH], score_slope)
                scaled = (slope[head].astype(FULL) * scale[head]).astype(LOW)
                value_slope = nt(scaled, low)
                first = query_slope[:, :LANES] + far_query[head]
                query_slope = jnp.concatenate([first, query_slope[:, LANES:]], axis=1)
                slopes[0, head] = (query_slope * HEAD_WIDTH ** (-0.5)).astype(LOW)
                slopes[1, head] = (key_slope * LN_TWO).astype(LOW)
                slopes[2, head] = value_slope.astype(LOW)
                if member % 2:
                    hook("near%d" % (head // 2))
            if (group + 2) * members < HEADS:
                load_group(group + 2).start()
            if group % 2:
                weight_slopes(group // 2)

        def flat_slopes(part):
            return slopes[part].reshape(width, rows)

        into = nn(wqkv[0], flat_slopes(0))
        into += nn(wqkv[1], flat_slopes(1))
        into += nn(wqkv[2], flat_slopes(2))
        norm_load.wait()
        pltpu.make_async_copy(staged, mixed_out, store_sem.at[1]).wait()
        spread(wide, into.T)
        hook("into")
        hook("norm")
        for n in TAIL[:EARLY]:
            pieces[n].advance()
        total = far_send[seq].astype(FULL)
        for n in range(count - 1):
            wait = remote(
                far_got.at[n], far_got.at[n], far_send_sem.at[n], far_recv_sem.at[n], peers[0]
            )
            wait.wait_recv()
            wait.wait_send()
            total = total + far_got[n].astype(FULL)
        for group in range(width // LANES):
            wide[group, :chosen] += total[:, group * LANES : (group + 1) * LANES]

        @steps
        def _(step):
            at = chunk(step, chosen)
            here = jnp.concatenate([wide[group, at, :] for group in range(width // LANES)], axis=1)
            normal = norm_one[at]
            sums[0] += fold_rows(here * normal)
            sums[1] += fold_rows(here)
            scaled = here * gain_one[...][None]
            part = scaled - row_mean(scaled) - normal * row_mean(scaled * normal)
            resid[at] += spread_one[at][:, :1] * part

    pl.run_scoped(
        backward_part,
        vm((2, members, rows, rows), LOW),
        vm((3, HEADS, HEAD_WIDTH, rows), LOW),
        vm((HEADS, HEAD_WIDTH, LANES), FULL),
        vm((count, chosen, width), LOW),
        vm((2, HEADS, HEAD_WIDTH, distant), LOW),
    )
    for n in range(4):
        around[seq, pl.ds(n, 1)] = jnp.sum(sums[n], axis=0, keepdims=True)
    for n, peer in enumerate(peers):
        mine = around.at[seq]
        remote(mine, mine, norm_send_sem.at[n], norm_recv_sem.at[n], peer).start()
    @steps
    def _(step):
        strided_store(wide, step, chosen, resid[chunk(step, chosen)])

    for group in range(width // LANES):
        staged[:, group * LANES : (group + 1) * LANES] = wide[group].astype(LOW)
    tokens_copy = pltpu.make_async_copy(staged, tokens_out, store_sem.at[2])
    tokens_copy.start()
    for n in range(count - 1):
        mine = around.at[seq]
        wait = remote(mine, mine, norm_send_sem.at[n], norm_recv_sem.at[n], peers[0])
        wait.wait_recv()
        wait.wait_send()
    total = around[0]
    for n in range(1, count):
        total = total + around[n]
    across[place.slide] = total
    for n, peer in enumerate(place.slide_peers):
        mine, at = across.at[place.slide], count - 1 + n
        remote(mine, mine, norm_send_sem.at[at], norm_recv_sem.at[at], peer).start()
    for n in TAIL[EARLY:] + tuple(range(PIECES)) * 6:
        pieces[n].advance()
    for n in range(3):
        mine, at = across.at[0], count - 1 + n
        wait = remote(mine, mine, norm_send_sem.at[at], norm_recv_sem.at[at], peers[0])
        wait.wait_recv()
        wait.wait_send()
    norm_out[...] = (across[0] + across[1]) + (across[2] + across[3])
    for piece in pieces:
        for n in range(len(piece.parts)):
            piece.out_copy(n).wait()
    tokens_copy.wait()


def main_pass(count, tokens, cotangent, weights, norms, visible):
    rows, width = tokens.shape
    chosen = rows // DILATION_STEP
    distant = count * chosen
    owned = width // count
    vm, dma = pltpu.VMEM, pltpu.SemaphoreType.DMA
    down_block, up_block = (LANES // 4, width), (owned, 2 * LANES)
    last_block = (owned // 2, width // 2)
    blocks = ((TILES, down_block), (TILES, up_block), (LASTS, last_block))
    low = [
        (width, rows), (width, distant), (HEADS, AUG, rows), (HEADS, AUG, rows),
        (HEADS, AUG, rows), (HEADS, AUG, distant), (HEADS, AUG, distant),
        (HEADS, distant, LANES),
    ]
    scratch = [vm(shape, LOW) for shape in low]
    scratch += [
        vm((HEADS, 1, rows), FULL),
        vm((HEADS, 1, LANES), FULL),
        vm((HEADS, HEAD_WIDTH, rows), LOW),
        vm((HEADS, 1, rows), FULL),
        vm((HEADS, HEAD_WIDTH, rows), LOW),
        vm((rows, width), FULL),
        vm((rows, width), FULL),
        vm((rows, width), LOW),
        vm((3, width, width), LOW),
        vm((width, width), LOW),
        vm((width // LANES, rows, LANES), FULL),
        vm((rows, width), LOW),
        vm((count, chosen, width), LOW),
        vm((count - 1, chosen, width), LOW),
        vm((rows, LANES), FULL),
        vm((4, 8, width), FULL),
        vm((count, 8, width), FULL),
        vm((4, 8, width), FULL),
    ]
    scratch += [vm((n, 2, count, 2) + block, LOW) for n, block in blocks]
    scratch += [vm((n, count, 2) + block, LOW) for n, block in blocks]
    scratch += [vm((n, 15) + block, LOW) for n, block in blocks]
    scratch += [vm((n, 4) + block, LOW) for n, block in blocks]
    scratch += [
        dma((6,)), dma((2, 2)), dma((2,)), dma((3,)), dma((PIECES, 2)),
        dma((PIECES, 2, 7)), dma((PIECES, 2, 7)),
        dma((count - 1,)), dma((count - 1,)), dma((count - 1,)), dma((count - 1,)),
        dma((count + 2,)), dma((count + 2,)),
    ]
    sums = [jax.ShapeDtypeStruct((n, 4) + block, LOW) for n, block in blocks]
    results = pl.pallas_call(
        functools.partial(main_kernel, count),
        out_shape=(
            jax.ShapeDtypeStruct((rows, width), LOW),
            jax.ShapeDtypeStruct((rows, width), LOW),
            *sums,
            jax.ShapeDtypeStruct((8, width), FULL),
            jax.ShapeDtypeStruct((HEADS, rows, rows), LOW),
            jax.ShapeDtypeStruct((rows, width), FULL),
        ),
        in_specs=[ANY] * 6 + [VMEM] * 4 + [SMEM],
        out_specs=(ANY, ANY, ANY, ANY, ANY, VMEM, ANY, ANY),
        scratch_shapes=scratch,
        compiler_params=pltpu.CompilerParams(
            collective_id=1, has_side_effects=True, vmem_limit_bytes=64 << 20
        ),
        name="main_pass",
    )(tokens, cotangent, *weights, *norms, visible)
    return results[:6]


def finish_kernel(
    mixed, tokens_grad, down_sums, up_sums, last_sums, norms,
    mixed_out, tokens_out, qkv_out, out_out, up_out, down_out, *refs
):
    norm_outs = refs[:4]
    mixed_in, tokens_in, down_in, up_in, last_in, norms_in = refs[4:10]
    qkv, out, up, down, in_sem, out_sem = refs[10:]
    loads = [
        pltpu.make_async_copy(source, target, in_sem.at[n])
        for n, (source, target) in enumerate(
            (
                (down_sums, down_in),
                (up_sums, up_in),
                (last_sums, last_in),
                (norms, norms_in),
                (mixed, mixed_in),
                (tokens_grad, tokens_in),
            )
        )
    ]
    for copy in loads:
        copy.start()
    stores = []

    def store(source, target):
        copy = pltpu.make_async_copy(source, target, out_sem.at[len(stores)])
        copy.start()
        stores.append(copy)

    tiles, blocks, rows, _ = down_sums.shape
    loads[0].wait()
    for tile in range(tiles):
        for block in range(blocks):
            first = (tile * blocks + block) * rows
            down[first : first + rows] = down_in[tile, block].astype(FULL)
    store(down, down_out)
    loads[1].wait()
    for tile in range(tiles):
        for block in range(blocks):
            for half in range(2):
                first = ((block * 2 + half) * tiles + tile) * LANES
                part = up_in[tile, block][:, half * LANES : (half + 1) * LANES]
                up[:, first : first + LANES] = part.astype(FULL)
    store(up, up_out)
    loads[2].wait()
    rows, columns = last_sums.shape[2:]
    for piece in range(last_sums.shape[0]):
        half, pair = divmod(piece, 2)
        for block in range(blocks):
            side, row = divmod(block, 2)
            at = slice(row * rows, (row + 1) * rows)
            first = half * columns
            target = out
            if pair == 0 or side == 0:
                target, first = qkv, first + 2 * columns * (2 * pair + side)
            target[at, first : first + columns] = last_in[piece, block].astype(FULL)
    store(qkv, qkv_out)
    store(out, out_out)
    loads[3].wait()
    for n, norm_out in enumerate(norm_outs):
        norm_out[...] = norms_in[n]
    for n, (source, target) in enumerate(((mixed_in, mixed_out), (tokens_in, tokens_out))):
        loads[4 + n].wait()
        store(source, target)
    for copy in stores:
        copy.wait()


def finish_pass(count, results):
    rows, width = results[0].shape
    owned = width // count

    def full(*shape):
        return jax.ShapeDtypeStruct(shape, FULL)

    grads = [
        full(owned, 3 * width),
        full(owned, width),
        full(owned, TILES * count * LANES),
        full(TILES * LANES, width),
    ]
    return pl.pallas_call(
        finish_kernel,
        out_shape=(
            jax.ShapeDtypeStruct((rows, width), LOW),
            jax.ShapeDtypeStruct((rows, width), LOW),
            *grads,
            *[full(width)] * 4,
        ),
        in_specs=[ANY] * 6,
        out_specs=(ANY,) * 6 + (VMEM,) * 4,
        scratch_shapes=[pltpu.VMEM(ref.shape, ref.dtype) for ref in (*results, *grads)]
        + [pltpu.SemaphoreType.DMA((6,)), pltpu.SemaphoreType.DMA((6,))],
        compiler_params=pltpu.CompilerParams(vmem_limit_bytes=63 << 20),
        name="finish_pass",
    )(*results)


def fused_device(
    tokens,
    qkv_weight,
    out_weight,
    up_weight,
    down_weight,
    norm1_gain,
    norm1_bias,
    norm2_gain,
    norm2_bias,
    visible,
    cotangent,
):
    count = lax.axis_size("seq")
    results = main_pass(
        count,
        tokens[0],
        cotangent[0],
        (qkv_weight, out_weight, up_weight, down_weight),
        (norm1_gain, norm1_bias, norm2_gain, norm2_bias),
        visible,
    )
    mixed, tokens_grad, *grads = finish_pass(count, results)
    return (mixed[None], tokens_grad[None], *grads)


def solution(mesh):
    placed = (
        P("slide", "seq", None),
        P(),
        P(),
        P(),
        P(),
        P(),
        P(),
        P(),
        P(),
        P("slide"),
        P("slide", "seq", None),
    )
    fused = mesh.shape["seq"] == 8 and mesh.shape["slide"] == 4
    return jax.shard_map(
        fused_device if fused else plain_device,
        mesh=mesh,
        in_specs=placed,
        out_specs=(
            P("slide", "seq", None),
            P("slide", "seq", None),
            P("seq", None),
            P("seq", None),
            P("seq", None),
            P("seq", None),
            P(),
            P(),
            P(),
            P(),
        ),
        check_vma=False,
    )
```
